32 devices in a mesh: tok: 16 (over z, y, x), head: 2 (over core).
Axes of the slice: x: 2, y: 2, z: 4, core: 2. Of those that a mesh axis runs over, the one named last changes fastest.
Arguments:
- tokens: bfloat16 [32768, 768], P(('tok', 'head')), may hold values from -6 to 6
- cotangent: bfloat16 [32768, 768], P(('tok', 'head')), may hold values from -6 to 6
- block_source: int32 [32, 4, 2], replicated, may hold values from 0 to 1, as said below
- mask_index: int32 [32, 256], replicated, may hold values from 0 to 1023, as said below
- mask_count: int32 [32], replicated, may hold values from 51 to 256
- w_query: bfloat16 [768, 768], P(None, 'head'), may hold values from -0.21875 to 0.21875
- w_key: bfloat16 [768, 768], P(None, 'head'), may hold values from -0.21875 to 0.21875
- w_value: bfloat16 [768, 768], P(None, 'head'), may hold values from -0.21875 to 0.21875
- w_output: bfloat16 [768, 768], P('head'), may hold values from -3 to 3
- mid_gain: float32 [768], replicated, may hold values from 0.25 to 1.75
- mid_shift: float32 [768], replicated, may hold values from -3 to 3
- w_inner: bfloat16 [768, 3072], P(None, 'head'), may hold values from -0.21875 to 0.21875
- bias_inner: float32 [3072], P('head'), may hold values from -3 to 3
- w_outer: bfloat16 [3072, 768], P('head'), may hold values from -0.109375 to 0.109375
- bias_outer: float32 [768], replicated, may hold values from -3 to 3
- end_gain: float32 [768], replicated, may hold values from 0.25 to 1.75
- end_shift: float32 [768], replicated, may hold values from -3 to 3
Outputs:
- out: bfloat16 [32768, 768], P(('tok', 'head'))
- grad_tokens: float32 [32768, 768], P(('tok', 'head'))
- grad_w_query: float32 [768, 768], P(None, 'head')
- grad_w_key: float32 [768, 768], P(None, 'head')
- grad_w_value: float32 [768, 768], P(None, 'head')
- grad_w_output: float32 [768, 768], P('head')
- grad_mid_gain: float32 [768], replicated
- grad_mid_shift: float32 [768], replicated
- grad_w_inner: float32 [768, 3072], P(None, 'head')
- grad_bias_inner: float32 [3072], P('head')
- grad_w_outer: float32 [3072, 768], P('head')
- grad_bias_outer: float32 [768], replicated
- grad_end_gain: float32 [768], replicated
- grad_end_shift: float32 [768], replicated
The draws below stay inside these ranges and needn't reach their ends.
Inputs may be any that keep to these rules, and one draw needn't show every extreme that they name: Each pair block_source[s, g] is (0, 1) or (1, 0); in every sequence at least one group has (1, 0). `mask_index`: the entries of a row are distinct positions of its sequence; only the first mask_count entries of a row are read.
All inputs are finite; a program needn't handle non-finite values.
Results may differ from the reference program's by a relative error of at most 0.015.
Values may be sent and summed in bfloat16 or wider, within the bound.
No kernel may reach another device: no remote copies, remote signals or barrier semaphores. Data moves between devices by JAX's collectives and lax.ppermute only.
A program may use at most 192 MiB of HBM per device.

```python
import jax
import jax.numpy as jnp
from jax import lax

D = 768
HEADS = 12
HDIM = 64
FF = 3072
GROUPS = 4
BLOCK = 512
PAIR_SEQS = 4
SEQ_LEN = 1024
MASK_MAX = 256
SEQS = 32
TOKENS = 32768
N_TOK = 16


def draw_block_source(key, part):
    key = jax.random.fold_in(key, 11)
    flip_key, pick_key = jax.random.split(key)
    flipped = jax.random.randint(flip_key, (SEQS, GROUPS), 0, 2)
    forced = jax.random.randint(pick_key, (SEQS, 1), 0, GROUPS)
    flipped = jnp.maximum(flipped, (jnp.arange(GROUPS)[None, :] == forced).astype(jnp.int32))
    return jnp.stack([flipped, 1 - flipped], axis=-1).astype(jnp.int32)


def draw_mask_index(key, part):
    key = jax.random.fold_in(key, 12)
    seq_keys = jax.random.split(key, SEQS)
    chosen = jax.vmap(lambda single: jax.random.permutation(single, SEQ_LEN)[:MASK_MAX])(seq_keys)
    return chosen.astype(jnp.int32)


def draw_mask_count(key, part):
    key = jax.random.fold_in(key, 13)
    count_key, order_key = jax.random.split(key)
    low_end = max(1, SEQ_LEN // 20)
    counts = jax.random.randint(count_key, (SEQS,), low_end, MASK_MAX + 1)
    ranking = jax.random.permutation(order_key, SEQS)
    counts = jnp.where(ranking == 0, MASK_MAX, counts)
    counts = jnp.where(ranking == 1, low_end, counts)
    return counts.astype(jnp.int32)


def levels(own_key, shape, pieces, low, top_value):
    def one(axis_at, shards_of):
        heights = jax.random.uniform(jax.random.fold_in(jax.random.fold_in(own_key, 6), axis_at), (shards_of,), jnp.float32, low / len(pieces), top_value / len(pieces))
        return jnp.repeat(jnp.exp(heights), shape[axis_at] // shards_of).reshape((-1,) + (1,) * (len(shape) - axis_at - 1))

    loudness = one(*pieces[0])
    for cut in pieces[1:]:
        loudness = loudness * one(*cut)
    return loudness


def scatter_about(rng, extent, scale, limit, cuts=(), dtype=jnp.bfloat16):
    values = jax.random.normal(rng, extent, jnp.float32) * scale
    if len(cuts) > 0:
        values = levels(rng, extent, cuts, -0.22, 0.18) * values
    return jnp.clip(values, min=-limit, max=limit).astype(dtype)


def setup_inputs(seed: int = 0) -> dict:
    keys = jax.random.split(jax.random.key(seed), 18)
    tokens = scatter_about(keys[0], (TOKENS, D), 1.0, 6.0, ((0, 32),))
    cotangent = scatter_about(keys[1], (TOKENS, D), 1.0, 6.0, ((0, 32),))
    block_source = draw_block_source(jax.random.fold_in(keys[17], 71), 0)
    mask_index = draw_mask_index(jax.random.fold_in(keys[17], 71), 0)
    mask_count = draw_mask_count(jax.random.fold_in(keys[17], 71), 0)
    w_query = scatter_about(keys[5], (D, D), D ** -0.5, 0.21875, ((1, 2),))
    w_key = scatter_about(keys[6], (D, D), D ** -0.5, 0.21875, ((1, 2),))
    w_value = scatter_about(keys[7], (D, D), D ** -0.5, 0.21875, ((1, 2),))
    w_output = scatter_about(keys[8], (D, D), (3 * D // BLOCK) ** -0.5, 3.0, ((0, 2),))
    mid_gain = jnp.clip(1.0 + 0.15 * jax.random.normal(keys[9], (D,), jnp.float32), 0.25, 1.75)
    mid_shift = scatter_about(keys[10], (D,), 0.5, 3.0, (), jnp.float32)
    w_inner = scatter_about(keys[11], (D, FF), D ** -0.5, 0.21875, ((1, 2),))
    bias_inner = scatter_about(keys[12], (FF,), 0.5, 3.0, ((0, 2),), jnp.float32)
    w_outer = scatter_about(keys[13], (FF, D), FF ** -0.5, 0.109375, ((0, 2),))
    bias_outer = scatter_about(keys[14], (D,), 0.5, 3.0, (), jnp.float32)
    end_gain = jnp.clip(1.0 + 0.15 * jax.random.normal(keys[15], (D,), jnp.float32), 0.25, 1.75)
    end_shift = scatter_about(keys[16], (D,), 0.5, 3.0, (), jnp.float32)
    return {"tokens": tokens, "cotangent": cotangent, "block_source": block_source, "mask_index": mask_index, "mask_count": mask_count, "w_query": w_query, "w_key": w_key, "w_value": w_value, "w_output": w_output, "mid_gain": mid_gain, "mid_shift": mid_shift, "w_inner": w_inner, "bias_inner": bias_inner, "w_outer": w_outer, "bias_outer": bias_outer, "end_gain": end_gain, "end_shift": end_shift}


HIGH = lax.Precision.HIGHEST
NORM_EPS = 1e-05

@jax.custom_vjp
def low(v):
    return lax.optimization_barrier(v.astype(jnp.bfloat16)).astype(jnp.float32)

@jax.custom_vjp
def low_back(v):
    return v

def low_keep(v):
    return (low(v), None)

def low_pass(kept, grad):
    return (grad,)

def back_keep(v):
    return (v, None)

def back_low(kept, grad):
    return (low(grad),)
low.defvjp(low_keep, low_pass)
low_back.defvjp(back_keep, back_low)

def layer_norm(summed, gain, shift):
    center = summed - lax.optimization_barrier(jnp.mean(summed, axis=-1, keepdims=True))
    spread = lax.optimization_barrier(jnp.mean(center * center, axis=-1, keepdims=True))
    return center * lax.rsqrt(spread + NORM_EPS) * gain + shift

def attend(queries, key_block, value_block):
    scores = low_back(jnp.dot(queries, key_block.T, precision=HIGH)) * HDIM ** (-0.5)
    probs = jax.nn.softmax(scores, axis=-1)
    return low(low_back(jnp.dot(low(probs), value_block, precision=HIGH)))

def heads_of(full, count):
    return full.reshape(count, 2, BLOCK, HEADS, HDIM).transpose(0, 3, 1, 2, 4)

def flatten_blocks(array):
    return array.reshape(-1, BLOCK, HDIM)

def forward(inputs, source, w_query, w_key, w_value, w_output, mid_gain, mid_shift, w_inner, bias_inner, w_outer, bias_outer, end_gain, end_shift):
    count = inputs.shape[0]

    def project(weight):
        return heads_of(low(low_back(jnp.dot(inputs, weight, precision=HIGH))), count)
    queries = project(w_query)
    key_heads = project(w_key)
    value_heads = project(w_value)
    head_source = jnp.repeat(source, HEADS // GROUPS, axis=1)
    picker = (head_source[..., None] == jnp.arange(2)).astype(jnp.float32)
    key_heads = jnp.einsum('shqk,shkbd->shqbd', picker, key_heads, precision=HIGH)
    value_heads = jnp.einsum('shqk,shkbd->shqbd', picker, value_heads, precision=HIGH)
    checked = jax.checkpoint(attend)
    context = lax.map(lambda triple: checked(*triple), (flatten_blocks(queries), flatten_blocks(key_heads), flatten_blocks(value_heads)))
    context = context.reshape(count, HEADS, 2, BLOCK, HDIM).transpose(0, 2, 3, 1, 4).reshape(count, 2 * BLOCK, D)
    branch = low_back(jnp.dot(context, w_output, precision=HIGH))
    normed = layer_norm(inputs + branch, mid_gain, mid_shift)
    inner = low_back(jnp.dot(low(normed), w_inner, precision=HIGH)) + bias_inner
    active = low(jax.nn.gelu(inner, approximate=False))
    outer = low_back(jnp.dot(active, w_outer, precision=HIGH))
    return layer_norm(normed + outer + bias_outer, end_gain, end_shift)

def loss_weight(positions, counts):
    live = jnp.arange(positions.shape[1])[None, :] < counts[:, None]
    places = jnp.arange(SEQ_LEN)
    hits = jnp.any((positions[:, :, None] == places[None, None, :]) & live[:, :, None], axis=1)
    return 1.0 + 3.0 * hits.astype(jnp.float32)

def to_sequences(array):
    return array.astype(jnp.float32).reshape(N_TOK // 2, 2, PAIR_SEQS, BLOCK, D).transpose(0, 2, 1, 3, 4).reshape(SEQS, SEQ_LEN, D)

def to_rows(array):
    return array.reshape(N_TOK // 2, PAIR_SEQS, 2, BLOCK, D).transpose(0, 2, 1, 3, 4).reshape(TOKENS, D)

def reference(tokens, cotangent, block_source, mask_index, mask_count, w_query, w_key, w_value, w_output, mid_gain, mid_shift, w_inner, bias_inner, w_outer, bias_outer, end_gain, end_shift):
    params = tuple((item.astype(jnp.float32) for item in (w_query, w_key, w_value, w_output, mid_gain, mid_shift, w_inner, bias_inner, w_outer, bias_outer, end_gain, end_shift)))
    steps_total = SEQS // 4
    inputs = to_sequences(tokens).reshape(steps_total, 4, SEQ_LEN, D)
    cotangents = to_sequences(cotangent).reshape(steps_total, 4, SEQ_LEN, D)
    sources = block_source.reshape(steps_total, 4, GROUPS, 2)
    positions = mask_index.reshape(steps_total, 4, MASK_MAX)
    counts = mask_count.reshape(steps_total, 4)

    def step(totals, batch):
        part_in, part_cot, part_source, part_pos, part_count = batch

        def local(first, *rest):
            return forward(first, part_source, *rest)
        result, pull = jax.vjp(local, part_in, *params)
        grads = pull(part_cot * loss_weight(part_pos, part_count)[..., None])
        totals = tuple((total + grad for total, grad in zip(totals, grads[1:])))
        return (totals, (result, grads[0]))
    start = tuple((jnp.zeros_like(item) for item in params))
    totals, (results, grad_inputs) = lax.scan(step, start, (inputs, cotangents, sources, positions, counts))
    out = to_rows(results.reshape(SEQS, SEQ_LEN, D)).astype(jnp.bfloat16)
    grad_tokens = to_rows(grad_inputs.reshape(SEQS, SEQ_LEN, D))
    return (out, grad_tokens, totals[0], totals[1], totals[2], totals[3], totals[4], totals[5], totals[6], totals[7], totals[8], totals[9], totals[10], totals[11])
```

```python
import functools

import jax
import jax.numpy as jnp
from jax import lax
from jax.experimental import pallas as pl
from jax.experimental.pallas import tpu as pltpu
from jax.sharding import PartitionSpec as P

HEADS = 12
HDIM = 64
GROUPS = 4
BLOCK = 512
PAIR_SEQS = 4
LANES = 128

NORM_EPS = 1e-05
LOG2E = 1.4426950408889634
BF16 = jnp.bfloat16
F32 = jnp.float32


def swap_bit(x, axis, bit):
    return lax.ppermute(x, axis, [(i, i ^ 1 << bit) for i in range(lax.axis_size(axis))])


def dot(a, b, dims=((1,), (0,))):
    return lax.dot_general(a, b, (dims, ((), ())), preferred_element_type=F32)


NT = ((1,), (1,))
TN = ((0,), (0,))


def head_lanes(first):
    lane = lax.broadcasted_iota(jnp.int32, (1, LANES), 1)
    return (lane < HDIM) if first else (lane >= HDIM)


def attend_kernel(swap_ref, qkv_ref, ctx_ref, lse_ref):
    swap = swap_ref[...] > 0
    keys = [qkv_ref[i * BLOCK : (i + 1) * BLOCK, LANES : 2 * LANES] for i in (0, 1)]
    values = [qkv_ref[i * BLOCK : (i + 1) * BLOCK, 2 * LANES :] for i in (0, 1)]
    scale = LOG2E * HDIM**-0.5
    ones = jnp.ones((16, BLOCK), BF16)
    for i in (0, 1):
        rows = slice(i * BLOCK, (i + 1) * BLOCK)
        q = qkv_ref[rows, :LANES]
        k = jnp.where(swap, keys[1 - i], keys[i])
        v_t = jnp.where(swap, values[1 - i], values[i]).T
        parts = []
        for n in (0, 1):
            q_n = jnp.where(head_lanes(n == 0), q, jnp.zeros_like(q))
            s = dot(k, q_n, NT)
            top = jnp.max(s, axis=0, keepdims=True)
            p = jnp.exp2((s - top) * scale).astype(BF16)
            v_n = jnp.concatenate([v_t[n * HDIM : (n + 1) * HDIM], ones], axis=0)
            acc = dot(v_n, p)
            total = acc[HDIM : HDIM + 1]
            parts.append(acc[:HDIM] / total)
            lse_ref[0, n : n + 1, rows] = top * scale + jnp.log2(total)
        ctx_ref[rows, :] = jnp.concatenate(parts, axis=0).T.astype(BF16)


def attend_back_kernel(swap_ref, qkv_ref, ctx_ref, dctx_ref, lse_ref, dqkv_ref):
    swap = swap_ref[...] > 0
    keys = [qkv_ref[i * BLOCK : (i + 1) * BLOCK, LANES : 2 * LANES] for i in (0, 1)]
    values = [qkv_ref[i * BLOCK : (i + 1) * BLOCK, 2 * LANES :] for i in (0, 1)]
    scale = LOG2E * HDIM**-0.5
    found = []
    for i in (0, 1):
        rows = slice(i * BLOCK, (i + 1) * BLOCK)
        q = qkv_ref[rows, :LANES]
        k = jnp.where(swap, keys[1 - i], keys[i])
        v = jnp.where(swap, values[1 - i], values[i])
        k_t = k.T
        dctx = dctx_ref[rows, :]
        prod_t = (dctx.astype(F32) * ctx_ref[rows, :].astype(F32)).T
        dq_t = []
        dk = dv = None
        for n in (0, 1):
            own = head_lanes(n == 0)
            cut = slice(n * HDIM, (n + 1) * HDIM)
            q_n = jnp.where(own, q, jnp.zeros_like(q))
            d_n = jnp.where(own, dctx, jnp.zeros_like(dctx))
            p = jnp.exp2(dot(k, q_n, NT) * scale - lse_ref[0, n : n + 1, rows])
            inner = jnp.sum(prod_t[cut], axis=0, keepdims=True)
            ds = (p * (dot(v, d_n, NT) - inner)).astype(BF16)
            dv_n = dot(p.astype(BF16), d_n)
            dk_n = dot(ds, q_n)
            dv = dv_n if dv is None else dv + dv_n
            dk = dk_n if dk is None else dk + dk_n
            dq_t.append(dot(k_t[cut], ds))
        dq = jnp.concatenate(dq_t, axis=0).T
        dqkv_ref[rows, :LANES] = (dq * HDIM**-0.5).astype(BF16)
        found.append(((dk * HDIM**-0.5).astype(BF16), dv.astype(BF16)))
    for i in (0, 1):
        rows = slice(i * BLOCK, (i + 1) * BLOCK)
        for at in (0, 1):
            dqkv_ref[rows, (at + 1) * LANES : (at + 2) * LANES] = jnp.where(
                swap, found[1 - i][at], found[i][at]
            )


def attention(swap_lanes, qkv):
    rows = qkv.shape[0]
    pairs = qkv.shape[1] // (3 * LANES)
    units = 4 * pairs
    return pl.pallas_call(
        attend_kernel,
        grid=(pairs,),
        in_specs=[
            pl.BlockSpec((1, LANES), lambda p: (0, p)),
            pl.BlockSpec((rows, 3 * LANES), lambda p: (0, p)),
        ],
        out_specs=[
            pl.BlockSpec((rows, LANES), lambda p: (0, p)),
            pl.BlockSpec((1, 2, rows), lambda p: (p, 0, 0)),
        ],
        out_shape=[
            jax.ShapeDtypeStruct((rows, pairs * LANES), BF16),
            jax.ShapeDtypeStruct((pairs, 2, rows), F32),
        ],
        compiler_params=pltpu.CompilerParams(vmem_limit_bytes=48 * 1024 * 1024),
        cost_estimate=pl.CostEstimate(
            flops=units * 4 * BLOCK * BLOCK * 256,
            bytes_accessed=rows * pairs * LANES * 8,
            transcendentals=units * BLOCK * BLOCK,
        ),
        name="attention_forward",
    )(swap_lanes, qkv)


def attention_back(swap_lanes, qkv, ctx, dctx, lse):
    rows = qkv.shape[0]
    pairs = qkv.shape[1] // (3 * LANES)
    units = 4 * pairs
    return pl.pallas_call(
        attend_back_kernel,
        grid=(pairs,),
        in_specs=[
            pl.BlockSpec((1, LANES), lambda p: (0, p)),
            pl.BlockSpec((rows, 3 * LANES), lambda p: (0, p)),
            pl.BlockSpec((rows, LANES), lambda p: (0, p)),
            pl.BlockSpec((rows, LANES), lambda p: (0, p)),
            pl.BlockSpec((1, 2, rows), lambda p: (p, 0, 0)),
        ],
        out_specs=pl.BlockSpec((rows, 3 * LANES), lambda p: (0, p)),
        out_shape=jax.ShapeDtypeStruct(qkv.shape, BF16),
        compiler_params=pltpu.CompilerParams(vmem_limit_bytes=48 * 1024 * 1024),
        cost_estimate=pl.CostEstimate(
            flops=units * 10 * BLOCK * BLOCK * 256,
            bytes_accessed=rows * pairs * LANES * 16,
            transcendentals=units * BLOCK * BLOCK,
        ),
        name="attention_backward",
    )(swap_lanes, qkv, ctx, dctx, lse)


def normalize(summed):
    center = summed - jnp.mean(summed, axis=-1, keepdims=True)
    rate = lax.rsqrt(jnp.mean(center * center, axis=-1, keepdims=True) + NORM_EPS)
    return center * rate, rate


def norm_back(grad, normed, rate, gain):
    scaled = grad * gain
    return rate * (
        scaled
        - jnp.mean(scaled, axis=-1, keepdims=True)
        - normed * jnp.mean(scaled * normed, axis=-1, keepdims=True)
    )


def gelu_parts(u):
    size = jnp.abs(u)
    bell = jnp.exp2(u * u * (-0.5 * LOG2E))
    t = 1.0 / (1.0 + (0.3275911 * 0.5**0.5) * size)
    poly = t * (
        0.5 * 0.254829592
        + t
        * (
            0.5 * -0.284496736
            + t * (0.5 * 1.421413741 + t * (0.5 * -1.453152027 + t * (0.5 * 1.061405429)))
        )
    )
    tail = poly * bell
    phi = jnp.where(u > 0, 1.0 - tail, tail)
    return u * phi, phi + u * (bell * 0.3989422804014327)


def halves(x, place):
    rows = x.shape[0] // 2
    return (
        lax.dynamic_slice_in_dim(x, place * rows, rows, 0),
        lax.dynamic_slice_in_dim(x, (1 - place) * rows, rows, 0),
    )


def joined(mine, other, place):
    return jnp.where(
        place == 0,
        jnp.concatenate([mine, other], axis=0),
        jnp.concatenate([other, mine], axis=0),
    )


def add_low(a, b):
    return (a.astype(F32) + b.astype(F32)).astype(BF16)


def tok_sum(first, second):
    size = lax.axis_size("tok")
    place = lax.axis_index("tok")
    bits = size.bit_length() - 1

    def at(bit):
        return place >> bit & 1

    def scatter(x, bit):
        mine, other = halves(x, at(bit))
        return add_low(mine, swap_bit(other, "tok", bit))

    def gather(x, bit):
        return joined(x, swap_bit(x, "tok", bit), at(bit))

    a, b = first, second
    a, b = scatter(a, 0), scatter(b, 1)
    a, b = scatter(a, 1), scatter(b, 0)
    rows = a.shape[0]
    for bit in range(2, bits):
        mine_a, other_a = halves(a, at(bit))
        mine_b, other_b = halves(b, at(bit))
        got = swap_bit(jnp.concatenate([other_a, other_b], axis=0), "tok", bit)
        cut = mine_a.shape[0]
        a, b = add_low(mine_a, got[:cut]), add_low(mine_b, got[cut:])
    for bit in reversed(range(2, bits)):
        cut = a.shape[0]
        got = swap_bit(jnp.concatenate([a, b], axis=0), "tok", bit)
        a, b = joined(a, got[:cut], at(bit)), joined(b, got[cut:], at(bit))
    a, b = gather(a, 1), gather(b, 0)
    a, b = gather(a, 0), gather(b, 1)
    return a, b


def body(
    tokens,
    cotangent,
    block_source,
    mask_index,
    mask_count,
    w_query,
    w_key,
    w_value,
    w_output,
    mid_gain,
    mid_shift,
    w_inner,
    bias_inner,
    w_outer,
    bias_outer,
    end_gain,
    end_shift,
):
    tok_place = lax.axis_index("tok")
    head_place = lax.axis_index("head")
    half = tok_place % 2
    width = tokens.shape[1]

    def mate(x):
        return swap_bit(x, "head", 0)

    kept, given = halves(tokens, half)
    x = jnp.concatenate([kept, swap_bit(given, "tok", 0)], axis=0)
    cot_kept, cot_given = halves(cotangent, half)
    cot = jnp.concatenate([cot_kept, swap_bit(cot_given, "tok", 0)], axis=0)

    local_pairs = w_query.shape[1] // LANES
    w_own = jnp.concatenate(
        [
            w[:, p * LANES : (p + 1) * LANES]
            for p in range(local_pairs)
            for w in (w_query, w_key, w_value)
        ],
        axis=1,
    )
    w_qkv = jnp.concatenate([w_own, mate(w_own)], axis=1)
    w_out = jnp.concatenate([w_output, mate(w_output)], axis=0)
    w_in = jnp.concatenate([w_inner, mate(w_inner)], axis=1)
    b_in = jnp.concatenate([bias_inner, mate(bias_inner)], axis=0)
    w_down = jnp.concatenate([w_outer, mate(w_outer)], axis=0)
    hidden = w_inner.shape[1]

    sequence = tok_place // 2 * PAIR_SEQS + 2 * head_place + half
    source = lax.dynamic_slice_in_dim(block_source, sequence, 1, 0)[0, :, 0]
    per_half = GROUPS // 2
    flags = jnp.concatenate(
        [
            lax.dynamic_slice_in_dim(source, head_place * per_half, per_half, 0),
            lax.dynamic_slice_in_dim(source, (1 - head_place) * per_half, per_half, 0),
        ]
    )
    swap_lanes = jnp.repeat(flags, HEADS // GROUPS * HDIM)[None, :]
    positions = lax.dynamic_slice_in_dim(mask_index, sequence, 1, 0)[0]
    count = lax.dynamic_slice_in_dim(mask_count, sequence, 1, 0)[0]
    within = jnp.arange(BLOCK)
    places = jnp.concatenate([half * BLOCK + within, (1 - half) * BLOCK + within])
    live = jnp.arange(positions.shape[0]) < count
    hits = jnp.any((positions[None, :] == places[:, None]) & live[None, :], axis=1)
    weight = 1.0 + 3.0 * hits.astype(F32)

    qkv = dot(x, w_qkv).astype(BF16)
    ctx, lse = attention(swap_lanes, qkv)
    mid_n, mid_rate = normalize(x.astype(F32) + dot(ctx, w_out))
    h1 = mid_n * mid_gain + mid_shift
    h1_low = h1.astype(BF16)
    active, slope = gelu_parts(dot(h1_low, w_in) + b_in)
    active = active.astype(BF16)
    slope = slope.astype(BF16)
    end_n, end_rate = normalize(h1 + dot(active, w_down) + bias_outer)
    out = (end_n * end_gain + end_shift).astype(BF16)
    out = joined(out[:BLOCK], swap_bit(out[BLOCK:], "tok", 0), half)

    d_y = cot.astype(F32) * weight[:, None]
    grad_end_shift = jnp.sum(d_y, axis=0)
    grad_end_gain = jnp.sum(d_y * end_n, axis=0)
    d_s2 = norm_back(d_y, end_n, end_rate, end_gain)
    grad_bias_outer = jnp.sum(d_s2, axis=0)
    d_f = d_s2.astype(BF16)

    def down_grad(rows):
        return dot(active[:, rows], d_f, TN)

    got = mate(down_grad(slice(hidden, 2 * hidden)).astype(BF16))
    g_down = (down_grad(slice(0, hidden)) + got.astype(F32)).astype(BF16)

    d_u = dot(d_f, w_down, NT) * slope.astype(F32)
    grad_b_in = jnp.sum(d_u, axis=0)
    d_u = d_u.astype(BF16)

    def inner_grad(cols):
        return dot(h1_low, d_u[:, cols], TN)

    got = mate(inner_grad(slice(hidden, 2 * hidden)).astype(BF16))
    g_in = (inner_grad(slice(0, hidden)) + got.astype(F32)).astype(BF16)

    d_h1 = d_s2 + dot(d_u, w_in, NT)
    grad_mid_shift = jnp.sum(d_h1, axis=0)
    grad_mid_gain = jnp.sum(d_h1 * mid_n, axis=0)
    d_s1 = norm_back(d_h1, mid_n, mid_rate, mid_gain)
    d_a = d_s1.astype(BF16)
    own_out = w_output.shape[0]
    got = mate(dot(ctx[:, own_out:], d_a, TN).astype(BF16))
    g_out = (dot(ctx[:, :own_out], d_a, TN) + got.astype(F32)).astype(BF16)
    d_ctx = dot(d_a, w_out, NT).astype(BF16)

    d_qkv = attention_back(swap_lanes, qkv, ctx, d_ctx, lse)
    own_qkv = w_own.shape[1]
    got = mate(dot(x, d_qkv[:, own_qkv:], TN).astype(BF16))
    g_qkv = (dot(x, d_qkv[:, :own_qkv], TN) + got.astype(F32)).astype(BF16)
    d_x = d_s1 + dot(d_qkv, w_qkv, NT)
    grad_tokens = joined(
        d_x[:BLOCK], swap_bit(d_x[BLOCK:].astype(BF16), "tok", 0).astype(F32), half
    )

    mixed = jnp.stack(
        [grad_end_shift, grad_end_gain, grad_bias_outer, grad_mid_shift, grad_mid_gain]
    )
    small = jnp.concatenate(
        [mixed, grad_b_in.reshape(-1, width), jnp.zeros((3, width), F32)], axis=0
    )
    own_rows = grad_b_in.shape[0] // 2 // width
    theirs = mate(small)
    small = jnp.concatenate(
        [
            small[:5] + theirs[:5],
            small[5 : 5 + own_rows] + theirs[5 + own_rows : 5 + 2 * own_rows],
            jnp.zeros((1, width), F32),
        ],
        axis=0,
    )
    for bit in range(lax.axis_size("tok").bit_length() - 1):
        small = small + swap_bit(small, "tok", bit)

    cut = hidden // 2
    g_down = jnp.concatenate(tok_sum(g_down[:cut], g_down[cut:]), axis=0).astype(F32)
    cut = width // 2
    g_in = jnp.concatenate(tok_sum(g_in[:cut], g_in[cut:]), axis=0).astype(F32)
    g_qkv = jnp.concatenate(tok_sum(g_qkv[:cut], g_qkv[cut:]), axis=0).astype(F32)
    cut = own_out // 2
    g_out = jnp.concatenate(tok_sum(g_out[:cut], g_out[cut:]), axis=0).astype(F32)

    def unpack(at):
        return jnp.concatenate(
            [
                g_qkv[:, (3 * p + at) * LANES : (3 * p + at + 1) * LANES]
                for p in range(local_pairs)
            ],
            axis=1,
        )

    return (
        out,
        grad_tokens,
        unpack(0),
        unpack(1),
        unpack(2),
        g_out,
        small[4],
        small[3],
        g_in,
        small[5 : 5 + own_rows].reshape(-1),
        g_down,
        small[2],
        small[1],
        small[0],
    )


def solution(mesh):
    rows = P(("tok", "head"), None)
    return jax.shard_map(
        body,
        mesh=mesh,
        in_specs=(
            rows,
            rows,
            P(),
            P(),
            P(),
            P(None, "head"),
            P(None, "head"),
            P(None, "head"),
            P("head", None),
            P(),
            P(),
            P(None, "head"),
            P("head"),
            P("head", None),
            P(),
            P(),
            P(),
        ),
        out_specs=(
            rows,
            rows,
            P(None, "head"),
            P(None, "head"),
            P(None, "head"),
            P("head", None),
            P(),
            P(),
            P(None, "head"),
            P("head"),
            P("head", None),
            P(),
            P(),
            P(),
        ),
        check_vma=False,
    )
```

```python
import functools

import jax
import jax.numpy as jnp
from jax import lax
from jax.experimental import pallas as pl
from jax.experimental.pallas import tpu as pltpu
from jax.sharding import PartitionSpec as P

HEADS = 12
HDIM = 64
GROUPS = 4
BLOCK = 512
PAIR_SEQS = 4
LANES = 128

NORM_EPS = 1e-05
LOG2E = 1.4426950408889634
BF16 = jnp.bfloat16
F32 = jnp.float32


def swap_bit(x, axis, bit):
    return lax.ppermute(x, axis, [(i, i ^ 1 << bit) for i in range(lax.axis_size(axis))])


def dot(a, b, dims=((1,), (0,))):
    return lax.dot_general(a, b, (dims, ((), ())), preferred_element_type=F32)


NT = ((1,), (1,))
TN = ((0,), (0,))


def head_lanes(first):
    lane = lax.broadcasted_iota(jnp.int32, (1, LANES), 1)
    return (lane < HDIM) if first else (lane >= HDIM)


def vmem(limit=56):
    return pltpu.CompilerParams(vmem_limit_bytes=limit * 1024 * 1024)


def whole(shape):
    return pl.BlockSpec(shape, lambda *_: (0,) * len(shape), pipeline_mode=pl.Buffered(1))


def pick(own, w_own_ref, w_mate_ref):
    return jnp.where(own, w_own_ref[...], w_mate_ref[...])


def normalize(summed):
    center = summed - jnp.mean(summed, axis=-1, keepdims=True)
    rate = lax.rsqrt(jnp.mean(center * center, axis=-1, keepdims=True) + NORM_EPS)
    return center * rate, rate


def norm_back(grad, normed, rate, gain):
    scaled = grad * gain
    return rate * (
        scaled
        - jnp.mean(scaled, axis=-1, keepdims=True)
        - normed * jnp.mean(scaled * normed, axis=-1, keepdims=True)
    )


def gelu_parts(u):
    size = jnp.abs(u)
    bell = jnp.exp2(u * u * (-0.5 * LOG2E))
    t = 1.0 / (1.0 + (0.3275911 * 0.5**0.5) * size)
    poly = t * (
        0.5 * 0.254829592
        + t
        * (
            0.5 * -0.284496736
            + t * (0.5 * 1.421413741 + t * (0.5 * -1.453152027 + t * (0.5 * 1.061405429)))
        )
    )
    tail = poly * bell
    phi = jnp.where(u > 0, 1.0 - tail, tail)
    return u * phi, phi + u * (bell * 0.3989422804014327)


SLOTS = (slice(0, BLOCK), slice(BLOCK, 2 * BLOCK))


def attend_kernel(
    pairs, swap_ref, x_ref, wq_ref, wk_ref, wv_ref, mq_ref, mk_ref, mv_ref, wo_ref, mo_ref,
    qkv_ref, lse_ref, ctx_t_ref, x_t_ref, mid_n_ref, rate_ref, ctx_all,
):
    step = pl.program_id(0)
    own = step < pairs // 2
    swap = swap_ref[...] > 0
    scale = LOG2E * HDIM**-0.5
    ones = jnp.ones((16, BLOCK), BF16)
    w = jnp.concatenate(
        [pick(own, wq_ref, mq_ref), pick(own, wk_ref, mk_ref), pick(own, wv_ref, mv_ref)], axis=1
    )
    for rows in SLOTS:
        qkv_ref[rows, :] = dot(x_ref[rows, :], w).astype(BF16)
    keys = [qkv_ref[rows, LANES : 2 * LANES] for rows in SLOTS]
    values = [qkv_ref[rows, 2 * LANES :] for rows in SLOTS]
    units = []
    for i, rows in enumerate(SLOTS):
        q = qkv_ref[rows, :LANES]
        k = jnp.where(swap, keys[1 - i], keys[i])
        v_t = jnp.where(swap, values[1 - i], values[i]).T
        for n in (0, 1):
            q_n = jnp.where(head_lanes(n == 0), q, jnp.zeros_like(q))
            units.append((rows, n, v_t, dot(k, q_n, NT)))
    parts = []
    for rows, n, v_t, s in units:
        top = jnp.max(s, axis=0, keepdims=True)
        p = jnp.exp2((s - top) * scale).astype(BF16)
        v_n = jnp.concatenate([v_t[n * HDIM : (n + 1) * HDIM], ones], axis=0)
        acc = dot(v_n, p)
        total = acc[HDIM : HDIM + 1]
        parts.append(acc[:HDIM] / total)
        lse_ref[0, n : n + 1, rows] = top * scale + jnp.log2(total)
        if n == 1:
            ctx_t = jnp.concatenate(parts, axis=0)
            parts = []
            ctx_t_ref[:, rows] = ctx_t.astype(BF16)
            ctx_all[step, rows, :] = ctx_t.T.astype(BF16)

    x_t_ref[...] = x_ref[:, pl.ds(pl.multiple_of(step * LANES, LANES), LANES)].T

    @pl.when(step == pairs - 1)
    def _():
        for rows in SLOTS:
            total = x_ref[rows, :].astype(F32)
            every = jnp.concatenate([ctx_all[p, rows, :] for p in range(pairs)], axis=1)
            cut = wo_ref.shape[0]
            total = total + dot(every[:, :cut], wo_ref[...]) + dot(every[:, cut:], mo_ref[...])
            normed, rate = normalize(total)
            mid_n_ref[rows, :] = normed
            rate_ref[rows, :] = rate


def attention(swap_lanes, x, own_w, mate_w, own_out, mate_out):
    rows, width = x.shape
    pairs = width // LANES
    per = own_w[0].shape[1] // LANES
    own_spec = pl.BlockSpec((width, LANES), lambda p: (0, jnp.minimum(p, per - 1)))
    mate_spec = pl.BlockSpec((width, LANES), lambda p: (0, jnp.maximum(p - per, 0)))
    return pl.pallas_call(
        functools.partial(attend_kernel, pairs),
        grid=(pairs,),
        in_specs=[pl.BlockSpec((1, LANES), lambda p: (0, p)), whole((rows, width))]
        + [own_spec] * 3
        + [mate_spec] * 3
        + [whole(own_out.shape)] * 2,
        out_specs=[
            pl.BlockSpec((rows, 3 * LANES), lambda p: (0, p)),
            pl.BlockSpec((1, 2, rows), lambda p: (p, 0, 0)),
            pl.BlockSpec((LANES, rows), lambda p: (p, 0)),
            pl.BlockSpec((LANES, rows), lambda p: (p, 0)),
            whole((rows, width)),
            whole((rows, 1)),
        ],
        out_shape=[
            jax.ShapeDtypeStruct((rows, 3 * width), BF16),
            jax.ShapeDtypeStruct((pairs, 2, rows), F32),
            jax.ShapeDtypeStruct((width, rows), BF16),
            jax.ShapeDtypeStruct((width, rows), BF16),
            jax.ShapeDtypeStruct((rows, width), F32),
            jax.ShapeDtypeStruct((rows, 1), F32),
        ],
        scratch_shapes=[pltpu.VMEM((pairs, rows, LANES), BF16)],
        compiler_params=vmem(),
        cost_estimate=pl.CostEstimate(
            flops=2 * rows * width * width * 4 + 4 * pairs * 4 * BLOCK * BLOCK * 256,
            bytes_accessed=rows * width * 18 + width * width * 8,
            transcendentals=4 * pairs * BLOCK * BLOCK,
        ),
        name="attention_forward",
    )(swap_lanes, x, *own_w, *mate_w, own_out, mate_out)


def ffn_kernel(
    tiles, mid_n_ref, par_ref, wi_ref, mi_ref, bi_ref, mbi_ref, wd_ref, md_ref, cot_ref, wt_ref,
    act_t_ref, slope_ref, h1_t_ref, out_ref, ds2_ref, df_ref, vec_ref, h1_low, acc,
):
    step = pl.program_id(0)
    own = step < tiles // 2

    @pl.when(step == 0)
    def _():
        for rows in SLOTS:
            h1 = mid_n_ref[rows, :] * par_ref[0:1, :] + par_ref[1:2, :]
            low = h1.astype(BF16)
            h1_low[rows, :] = low
            h1_t_ref[:, rows] = low.T
            acc[rows, :] = h1 + par_ref[2:3, :]

    w_in = pick(own, wi_ref, mi_ref)
    w_down = pick(own, wd_ref, md_ref)
    bias = pick(own, bi_ref, mbi_ref)
    size = 256
    cuts = [slice(at, at + size) for at in range(0, 2 * BLOCK, size)]
    ready = [dot(h1_low[cuts[0], :], w_in)]
    for at, rows in enumerate(cuts):
        if at + 1 < len(cuts):
            ready.append(dot(h1_low[cuts[at + 1], :], w_in))
        value, slope = gelu_parts(ready[at] + bias)
        low = value.astype(BF16)
        slope_ref[rows, :] = slope.astype(BF16)
        act_t_ref[:, rows] = low.T
        acc[rows, :] += dot(low, w_down)

    @pl.when(step == tiles - 1)
    def _():
        gain = par_ref[3:4, :]
        sums = [0.0, 0.0, 0.0]
        for at in range(0, 2 * BLOCK, size):
            rows = slice(at, at + size)
            normed, rate = normalize(acc[rows, :])
            out_ref[rows, :] = (normed * gain + par_ref[4:5, :]).astype(BF16)
            d_y = cot_ref[rows, :].astype(F32) * wt_ref[rows, :]
            d_s2 = norm_back(d_y, normed, rate, gain)
            ds2_ref[rows, :] = d_s2
            df_ref[rows, :] = d_s2.astype(BF16)
            for n, term in enumerate((d_y, d_y * normed, d_s2)):
                sums[n] = sums[n] + jnp.sum(term, axis=0, keepdims=True)
        vec_ref[...] = jnp.concatenate(sums + [jnp.zeros((5, gain.shape[1]), F32)], axis=0)


TILE = 768
COLS = 384


def ffn(mid_n, params, own_in, mate_in, own_bias, mate_bias, own_down, mate_down, cot, weight):
    rows, width = mid_n.shape
    per = own_in.shape[1] // TILE
    tiles = 2 * per

    def own_at(j):
        return jnp.minimum(j, per - 1)

    def mate_at(j):
        return jnp.maximum(j - per, 0)

    hidden = 2 * own_in.shape[1]
    return pl.pallas_call(
        functools.partial(ffn_kernel, tiles),
        grid=(tiles,),
        in_specs=[
            whole((rows, width)),
            whole(params.shape),
            pl.BlockSpec((width, TILE), lambda j: (0, own_at(j))),
            pl.BlockSpec((width, TILE), lambda j: (0, mate_at(j))),
            pl.BlockSpec((1, TILE), lambda j: (0, own_at(j))),
            pl.BlockSpec((1, TILE), lambda j: (0, mate_at(j))),
            pl.BlockSpec((TILE, width), lambda j: (own_at(j), 0)),
            pl.BlockSpec((TILE, width), lambda j: (mate_at(j), 0)),
            whole((rows, width)),
            whole((rows, 1)),
        ],
        out_specs=[
            pl.BlockSpec((TILE, rows), lambda j: (j, 0)),
            pl.BlockSpec((rows, TILE), lambda j: (0, j)),
            whole((width, rows)),
            whole((rows, width)),
            whole((rows, width)),
            whole((rows, width)),
            whole((8, width)),
        ],
        out_shape=[
            jax.ShapeDtypeStruct((hidden, rows), BF16),
            jax.ShapeDtypeStruct((rows, hidden), BF16),
            jax.ShapeDtypeStruct((width, rows), BF16),
            jax.ShapeDtypeStruct((rows, width), BF16),
            jax.ShapeDtypeStruct((rows, width), F32),
            jax.ShapeDtypeStruct((rows, width), BF16),
            jax.ShapeDtypeStruct((8, width), F32),
        ],
        scratch_shapes=[pltpu.VMEM((rows, width), BF16), pltpu.VMEM((rows, width), F32)],
        compiler_params=vmem(),
        cost_estimate=pl.CostEstimate(
            flops=4 * rows * width * hidden,
            bytes_accessed=rows * hidden * 4 + rows * width * 16 + width * hidden * 4,
            transcendentals=rows * hidden * 2,
        ),
        name="feed_forward",
    )(mid_n, params, own_in, mate_in, own_bias, mate_bias, own_down, mate_down, cot, weight)


def product_kernel(a_ref, b_ref, c_ref):
    c_ref[...] = dot(a_ref[...], b_ref[...]).astype(BF16)


def product(a, first, rows, b, block):
    return pl.pallas_call(
        product_kernel,
        grid=(rows // block,),
        in_specs=[pl.BlockSpec((block, a.shape[1]), lambda j: (j + first // block, 0)), whole(b.shape)],
        out_specs=pl.BlockSpec((block, b.shape[1]), lambda j: (j, 0)),
        out_shape=jax.ShapeDtypeStruct((rows, b.shape[1]), BF16),
        compiler_params=vmem(12),
        cost_estimate=pl.CostEstimate(
            flops=2 * rows * a.shape[1] * b.shape[1],
            bytes_accessed=2 * (rows * (a.shape[1] + b.shape[1]) + b.shape[0] * b.shape[1]),
            transcendentals=0,
        ),
        name="weight_gradient",
    )(a, b)


def ffn_back_kernel(
    tiles, df_ref, slope_ref, wi_ref, mi_ref, wd_ref, md_ref, h1_t_ref, ds2_ref, mid_n_ref,
    rate_ref, ctx_t_ref, par_ref, gin_ref, gout_ref, db_ref, ds1_ref, da_ref, vec_ref, du, acc,
):
    step = pl.program_id(0)
    own = step < tiles // 2
    w_in = pick(own, wi_ref, mi_ref)
    w_down = pick(own, wd_ref, md_ref)

    @pl.when(step == 0)
    def _():
        acc[...] = ds2_ref[...]

    size = 256
    total = 0.0
    cuts = [slice(at, at + size) for at in range(0, 2 * BLOCK, size)]
    ready = [dot(df_ref[cuts[0], :], w_down, NT)]
    for at, rows in enumerate(cuts):
        if at + 1 < len(cuts):
            ready.append(dot(df_ref[cuts[at + 1], :], w_down, NT))
        d_u = ready[at] * slope_ref[rows, :].astype(F32)
        total = total + jnp.sum(d_u, axis=0, keepdims=True)
        low = d_u.astype(BF16)
        du[rows, :] = low
        acc[rows, :] += dot(low, w_in, NT)
    db_ref[...] = total
    gin_ref[0] = dot(h1_t_ref[...], du[...]).astype(BF16)

    @pl.when(step == tiles - 1)
    def _():
        sums = [0.0, 0.0]
        gain = par_ref[0:1, :]
        for at in range(0, 2 * BLOCK, size):
            rows = slice(at, at + size)
            d_h1 = acc[rows, :]
            normed = mid_n_ref[rows, :]
            d_s1 = norm_back(d_h1, normed, rate_ref[rows, :], gain)
            ds1_ref[rows, :] = d_s1
            da_ref[rows, :] = d_s1.astype(BF16)
            for n, term in enumerate((d_h1, d_h1 * normed)):
                sums[n] = sums[n] + jnp.sum(term, axis=0, keepdims=True)
        vec_ref[...] = jnp.concatenate(sums + [jnp.zeros((6, gain.shape[1]), F32)], axis=0)
        gout_ref[...] = dot(ctx_t_ref[...], da_ref[...]).astype(BF16)


def ffn_back(
    d_f, slope, own_in, mate_in, own_down, mate_down, h1_t, d_s2, mid_n, rate, ctx_t, params
):
    rows, width = d_f.shape
    per = own_in.shape[1] // TILE
    tiles = 2 * per
    hidden = 2 * own_in.shape[1]

    def own_at(j):
        return jnp.minimum(j, per - 1)

    def mate_at(j):
        return jnp.maximum(j - per, 0)

    return pl.pallas_call(
        functools.partial(ffn_back_kernel, tiles),
        grid=(tiles,),
        in_specs=[
            whole((rows, width)),
            pl.BlockSpec((rows, TILE), lambda j: (0, j)),
            pl.BlockSpec((width, TILE), lambda j: (0, own_at(j))),
            pl.BlockSpec((width, TILE), lambda j: (0, mate_at(j))),
            pl.BlockSpec((TILE, width), lambda j: (own_at(j), 0)),
            pl.BlockSpec((TILE, width), lambda j: (mate_at(j), 0)),
            whole((width, rows)),
            whole((rows, width)),
            whole((rows, width)),
            whole((rows, 1)),
            whole((width, rows)),
            whole(params.shape),
        ],
        out_specs=[
            pl.BlockSpec((1, width, TILE), lambda j: (j, 0, 0)),
            whole((width, width)),
            pl.BlockSpec((1, TILE), lambda j: (0, j)),
            whole((rows, width)),
            whole((rows, width)),
            whole((8, width)),
        ],
        out_shape=[
            jax.ShapeDtypeStruct((tiles, width, TILE), BF16),
            jax.ShapeDtypeStruct((width, width), BF16),
            jax.ShapeDtypeStruct((1, hidden), F32),
            jax.ShapeDtypeStruct((rows, width), F32),
            jax.ShapeDtypeStruct((rows, width), BF16),
            jax.ShapeDtypeStruct((8, width), F32),
        ],
        scratch_shapes=[pltpu.VMEM((rows, TILE), BF16), pltpu.VMEM((rows, width), F32)],
        compiler_params=vmem(),
        cost_estimate=pl.CostEstimate(
            flops=6 * rows * width * hidden,
            bytes_accessed=rows * hidden * 2 + rows * width * 18 + width * hidden * 6,
            transcendentals=0,
        ),
        name="feed_forward_back",
    )(d_f, slope, own_in, mate_in, own_down, mate_down, h1_t, d_s2, mid_n, rate, ctx_t, params)


def attend_back_kernel(
    steps, swap_ref, qkv_ref, ctx_t_ref, lse_ref, wq_ref, wk_ref, wv_ref, wo_ref, da_ref, x_t_ref,
    start_ref, gw_ref, dx_ref, dqkv,
):
    step = pl.program_id(0)
    swap = swap_ref[...] > 0
    scale = LOG2E * HDIM**-0.5

    @pl.when(step == 0)
    def _():
        dx_ref[...] = start_ref[...]

    keys = [qkv_ref[rows, LANES : 2 * LANES] for rows in SLOTS]
    values = [qkv_ref[rows, 2 * LANES :] for rows in SLOTS]
    blocks, units = [], []
    for i, rows in enumerate(SLOTS):
        q = qkv_ref[rows, :LANES]
        k = jnp.where(swap, keys[1 - i], keys[i])
        v = jnp.where(swap, values[1 - i], values[i])
        dctx = dot(da_ref[rows, :], wo_ref[...], NT).astype(BF16)
        prod_t = dctx.T.astype(F32) * ctx_t_ref[:, rows].astype(F32)
        blocks.append((rows, q, k, v, k.T, dctx, prod_t))
    for i, (rows, q, k, v, k_t, dctx, prod_t) in enumerate(blocks):
        for n in (0, 1):
            own = head_lanes(n == 0)
            q_n = jnp.where(own, q, jnp.zeros_like(q))
            d_n = jnp.where(own, dctx, jnp.zeros_like(dctx))
            units.append((i, n, q_n, d_n))

    def products(unit):
        i, n, q_n, d_n = unit
        return dot(blocks[i][2], q_n, NT), dot(blocks[i][3], d_n, NT)

    ahead = 1
    ready = [products(unit) for unit in units[:ahead]]
    found = []
    for at, (i, n, q_n, d_n) in enumerate(units):
        if at + ahead < len(units):
            ready.append(products(units[at + ahead]))
        rows, q, k, v, k_t, dctx, prod_t = blocks[i]
        cut = slice(n * HDIM, (n + 1) * HDIM)
        s, d_p = ready[at]
        p = jnp.exp2(s * scale - lse_ref[0, n : n + 1, rows])
        inner = jnp.sum(prod_t[cut], axis=0, keepdims=True)
        ds = (p * (d_p - inner)).astype(BF16)
        dv_n = dot(p.astype(BF16), d_n)
        dk_n = dot(ds, q_n)
        if n == 0:
            dv, dk, dq_t = dv_n, dk_n, [dot(k_t[cut], ds)]
        else:
            dv, dk = dv + dv_n, dk + dk_n
            dq_t.append(dot(k_t[cut], ds))
            dq = jnp.concatenate(dq_t, axis=0).T
            dqkv[rows, :LANES] = (dq * HDIM**-0.5).astype(BF16)
            found.append(((dk * HDIM**-0.5).astype(BF16), dv.astype(BF16)))
    for i, rows in enumerate(SLOTS):
        for at in (0, 1):
            dqkv[rows, (at + 1) * LANES : (at + 2) * LANES] = jnp.where(
                swap, found[1 - i][at], found[i][at]
            )
    gw_ref[0] = dot(x_t_ref[...], dqkv[...]).astype(BF16)
    w = jnp.concatenate([wq_ref[...], wk_ref[...], wv_ref[...]], axis=1)
    for rows in SLOTS:
        dx_ref[rows, :] += dot(dqkv[rows, :], w, NT)


def attention_back(first, swap_lanes, qkv, ctx_t, lse, weights, w_out, d_a, x_t, start):
    rows, width = d_a.shape
    pairs = w_out.shape[0] // LANES
    w_spec = pl.BlockSpec((width, LANES), lambda p: (0, p))
    return pl.pallas_call(
        functools.partial(attend_back_kernel, pairs),
        grid=(pairs,),
        in_specs=[
            pl.BlockSpec((1, LANES), lambda p: (0, p + first)),
            pl.BlockSpec((rows, 3 * LANES), lambda p: (0, p + first)),
            pl.BlockSpec((LANES, rows), lambda p: (p + first, 0)),
            pl.BlockSpec((1, 2, rows), lambda p: (p + first, 0, 0)),
            w_spec,
            w_spec,
            w_spec,
            pl.BlockSpec((LANES, width), lambda p: (p, 0)),
            whole((rows, width)),
            whole((width, rows)),
            whole((rows, width)),
        ],
        out_specs=[
            pl.BlockSpec((1, width, 3 * LANES), lambda p: (p, 0, 0)),
            whole((rows, width)),
        ],
        out_shape=[
            jax.ShapeDtypeStruct((pairs, width, 3 * LANES), BF16),
            jax.ShapeDtypeStruct((rows, width), F32),
        ],
        scratch_shapes=[pltpu.VMEM((rows, 3 * LANES), BF16)],
        compiler_params=vmem(),
        cost_estimate=pl.CostEstimate(
            flops=14 * rows * width * pairs * LANES + 4 * pairs * 10 * BLOCK * BLOCK * 256,
            bytes_accessed=rows * width * 14,
            transcendentals=4 * pairs * BLOCK * BLOCK,
        ),
        name="attention_backward",
    )(swap_lanes, qkv, ctx_t, lse, *weights, w_out, d_a, x_t, start)


def halves(x, place):
    rows = x.shape[0] // 2
    return (
        lax.dynamic_slice_in_dim(x, place * rows, rows, 0),
        lax.dynamic_slice_in_dim(x, (1 - place) * rows, rows, 0),
    )


def joined(mine, other, place, axis=0):
    return jnp.where(
        place == 0,
        jnp.concatenate([mine, other], axis=axis),
        jnp.concatenate([other, mine], axis=axis),
    )


def add_low(a, b):
    return (a.astype(F32) + b.astype(F32)).astype(BF16)


def after(x, *others):
    return lax.optimization_barrier((x, others))[0]


class TokSum:
    def __init__(self, *arrays):
        size = lax.axis_size("tok")
        self.place = lax.axis_index("tok")
        bits = size.bit_length() - 1
        self.parts = [[], []]
        for x in arrays:
            rows, width = x.shape
            rows //= size
            half = -(-rows // 16) * 8 if rows % 16 else rows // 2
            split = x.reshape((2,) * bits + (rows, width))
            self.parts[0].append(split[..., :half, :])
            self.parts[1].append(split[..., half:, :])
        self.left = [list(reversed(range(bits))) for _ in (0, 1)]
        there = [(0, 1), (1, 0)] + [(bit, bit) for bit in range(2, bits)]
        self.steps = [(True, pair) for pair in there] + [(False, pair) for pair in reversed(there)]

    def send(self):
        adding, bits = self.now = self.steps.pop(0)
        self.kept, sent = self.parts, self.parts
        if adding:
            self.kept, sent = [], []
            for stream, left, bit in zip(self.parts, self.left, bits):
                axis = left.index(bit)
                left.remove(bit)
                mine = self.place >> bit & 1
                self.kept.append(
                    [lax.dynamic_index_in_dim(x, mine, axis, keepdims=False) for x in stream]
                )
                sent.append(
                    [lax.dynamic_index_in_dim(x, 1 - mine, axis, keepdims=False) for x in stream]
                )
        sent = [jnp.concatenate(stream, axis=-2) for stream in sent]
        if bits[0] == bits[1]:
            self.sent = [jnp.concatenate(sent, axis=-2)]
            self.got = [swap_bit(self.sent[0], "tok", bits[0])]
        else:
            self.sent = sent
            self.got = [swap_bit(part, "tok", bit) for part, bit in zip(sent, bits)]
        return self.sent

    def take(self, got):
        adding, bits = self.now
        streams, first = [], 0
        for n, stream in enumerate(self.kept):
            if bits[0] != bits[1]:
                first = 0
            whole = got[0] if bits[0] == bits[1] else got[n]
            streams.append([])
            for x in stream:
                streams[-1].append(whole[..., first : first + x.shape[-2], :])
                first += x.shape[-2]
        if adding:
            self.parts = [
                [add_low(a, b) for a, b in zip(kept, new)] for kept, new in zip(self.kept, streams)
            ]
            return
        parts = []
        for stream, new, left, bit in zip(self.kept, streams, self.left, bits):
            axis = sum(other > bit for other in left)
            left.insert(axis, bit)
            place = self.place >> bit & 1
            parts.append(
                [
                    joined(jnp.expand_dims(a, axis), jnp.expand_dims(b, axis), place, axis)
                    for a, b in zip(stream, new)
                ]
            )
        self.parts = parts

    def results(self):
        return [
            jnp.concatenate([a, b], axis=-2).reshape((-1,) + (a.shape[-2] + b.shape[-2], a.shape[-1]))
            for a, b in zip(*self.parts)
        ]


def send(*sums):
    return [one.send() for one in sums]


def settle(sums, *others):
    got, others = lax.optimization_barrier(([one.got for one in sums], others))
    for one, new in zip(sums, got):
        one.take(new)
    return others if len(others) != 1 else others[0]


def body(
    tokens,
    cotangent,
    block_source,
    mask_index,
    mask_count,
    w_query,
    w_key,
    w_value,
    w_output,
    mid_gain,
    mid_shift,
    w_inner,
    bias_inner,
    w_outer,
    bias_outer,
    end_gain,
    end_shift,
):
    tok_place = lax.axis_index("tok")
    head_place = lax.axis_index("head")
    half = tok_place % 2
    width = tokens.shape[1]

    def mate(x):
        return swap_bit(x, "head", 0)

    kept, given = halves(tokens, half)
    x_got = swap_bit(given, "tok", 0)
    own_w = (w_query, w_key, w_value)
    mate_w = tuple(mate(w) for w in own_w)
    mate_out = mate(w_output)
    mate_in = mate(w_inner)
    mate_down = mate(w_outer)
    own_bias = bias_inner[None, :]
    mate_bias = mate(own_bias)

    sequence = tok_place // 2 * PAIR_SEQS + 2 * head_place + half
    source = lax.dynamic_slice_in_dim(block_source, sequence, 1, 0)[0, :, 0]
    per_half = GROUPS // 2
    flags = jnp.concatenate(
        [
            lax.dynamic_slice_in_dim(source, head_place * per_half, per_half, 0),
            lax.dynamic_slice_in_dim(source, (1 - head_place) * per_half, per_half, 0),
        ]
    )
    swap_lanes = jnp.repeat(flags, HEADS // GROUPS * HDIM)[None, :]
    positions = lax.dynamic_slice_in_dim(mask_index, sequence, 1, 0)[0]
    count = lax.dynamic_slice_in_dim(mask_count, sequence, 1, 0)[0]
    within = jnp.arange(BLOCK)
    places = jnp.concatenate([half * BLOCK + within, (1 - half) * BLOCK + within])
    live = jnp.arange(positions.shape[0]) < count
    hits = jnp.any((positions[None, :] == places[:, None]) & live[None, :], axis=1)
    weight = (1.0 + 3.0 * hits.astype(F32))[:, None]
    params = jnp.stack(
        [mid_gain, mid_shift, bias_outer, end_gain, end_shift] + [jnp.zeros_like(mid_gain)] * 3
    )

    x = jnp.concatenate([kept, after(x_got, swap_lanes, weight, params)], axis=0)
    qkv, lse, ctx_t, x_t, mid_n, mid_rate = attention(
        swap_lanes, x, own_w, mate_w, w_output, mate_out
    )
    cot_kept, cot_given = halves(after(cotangent, x_got), half)
    cot = jnp.concatenate([cot_kept, swap_bit(cot_given, "tok", 0)], axis=0)
    act_t, slope, h1_t, out, d_s2, d_f, end_vec = ffn(
        mid_n, params, w_inner, mate_in, own_bias, mate_bias, w_outer, mate_down, cot, weight
    )
    out_got = swap_bit(out[BLOCK:], "tok", 0)
    out = joined(out[:BLOCK], out_got, half)

    hidden = w_inner.shape[1]
    cut = w_output.shape[0]
    pairs = cut // LANES

    def side_by_side(g):
        return jnp.concatenate([g[:, n : n + COLS] for n in range(0, width, COLS)], axis=0)

    got = mate(product(act_t, hidden, hidden, d_f, BLOCK))
    down = TokSum(add_low(product(act_t, 0, hidden, d_f, BLOCK), got))
    sent = send(down)
    g_in, g_out, g_bias, d_s1, d_a, mid_vec = ffn_back(
        after(d_f, sent), slope, w_inner, mate_in, w_outer, mate_down, h1_t, d_s2, mid_n, mid_rate,
        ctx_t, params,
    )
    g_in, g_out, g_bias, d_s1, d_a, mid_vec = settle(
        [down], g_in, g_out, g_bias, d_s1, d_a, mid_vec
    )
    sent = send(down)
    tiles = g_in.shape[0] // 2
    rows = tiles * width
    got_in, got_out = mate(g_in[tiles:]), mate(g_out[cut:])
    mine = (
        add_low(g_in[:tiles], got_in).reshape(-1, width),
        add_low(g_out[:cut], got_out),
    )
    mine = settle([down], *mine)
    inner = TokSum(*mine)
    sent = send(down, inner)
    gw_mate, d_x = attention_back(
        pairs, swap_lanes, qkv, ctx_t, lse, mate_w, mate_out, after(d_a, sent), x_t, d_s1
    )
    gw_mate, d_x = settle([down, inner], gw_mate, d_x)
    gw_got = mate(gw_mate)
    sent = send(down, inner)

    bias_rows = g_bias.reshape(-1, width)
    own_rows = bias_rows.shape[0] // 2
    small = jnp.concatenate([end_vec[:3], mid_vec[:2], bias_rows], axis=0)
    theirs = mate(small)
    small = jnp.concatenate(
        [
            small[:5] + theirs[:5],
            small[5 : 5 + own_rows] + theirs[5 + own_rows :],
            jnp.zeros((1, width), F32),
        ],
        axis=0,
    )
    high = small.astype(BF16)
    low = (small - high.astype(F32)).astype(BF16)

    gw_own, d_x = attention_back(
        0, swap_lanes, qkv, ctx_t, lse, own_w, w_output, after(d_a, sent, gw_mate), x_t, d_x
    )
    gw_own, d_x, gw_got, high, low = settle([down, inner], gw_own, d_x, gw_got, high, low)
    last = TokSum(add_low(gw_own, gw_got).reshape(-1, 3 * LANES))
    sums = [last, inner, down]
    done = 0
    while sums:
        send(*sums)
        if done == 1:
            dx_got = swap_bit(d_x[BLOCK:].astype(BF16), "tok", 0)
        if done == 2:
            dx_got = settle(sums, dx_got)
        else:
            settle(sums)
        done += 1
        sums = [one for one in sums if one.steps]
        if 2 * done == len(last.steps) + done:
            for stream, rest in zip(last.parts, (high, low)):
                stream.append(side_by_side(rest))
    grad_tokens = joined(d_x[:BLOCK], dx_got.astype(F32), half)

    g_down = down.results()[0].reshape(hidden, width).astype(F32)
    g_in, g_out = inner.results()
    g_in = g_in.reshape(tiles, width, -1)
    g_in = jnp.concatenate([g_in[n] for n in range(tiles)], axis=1).astype(F32)
    g_out = g_out.reshape(cut, width).astype(F32)
    last, small = last.results()
    small_rows = high.shape[0]
    small = jnp.sum(small.astype(F32), axis=0)
    sums = small[: 2 * small_rows] + small[2 * small_rows :]
    small = jnp.concatenate([sums[:small_rows], sums[small_rows:]], axis=1)
    last = last.reshape(pairs, width, 3, LANES)

    def unpack(at):
        return jnp.concatenate([last[p, :, at] for p in range(pairs)], axis=1).astype(F32)

    return (
        out,
        grad_tokens,
        unpack(0),
        unpack(1),
        unpack(2),
        g_out,
        small[4],
        small[3],
        g_in,
        small[5 : 5 + own_rows].reshape(-1),
        g_down,
        small[2],
        small[1],
        small[0],
    )


def solution(mesh):
    rows = P(("tok", "head"), None)
    return jax.shard_map(
        body,
        mesh=mesh,
        in_specs=(
            rows,
            rows,
            P(),
            P(),
            P(),
            P(None, "head"),
            P(None, "head"),
            P(None, "head"),
            P("head", None),
            P(),
            P(),
            P(None, "head"),
            P("head"),
            P("head", None),
            P(),
            P(),
            P(),
        ),
        out_specs=(
            rows,
            rows,
            P(None, "head"),
            P(None, "head"),
            P(None, "head"),
            P("head", None),
            P(),
            P(),
            P(None, "head"),
            P("head"),
            P("head", None),
            P(),
            P(),
            P(),
        ),
        check_vma=False,
    )
```

```python
import functools
import math

import jax
import jax.numpy as jnp
from jax import lax
from jax.experimental import pallas as pl
from jax.experimental.pallas import tpu as pltpu
from jax.sharding import PartitionSpec as P

HEADS = 12
HDIM = 64
GROUPS = 4
BLOCK = 512
PAIR_SEQS = 4
LANES = 128

NORM_EPS = 1e-05
LOG2E = 1.4426950408889634
BF16 = jnp.bfloat16
F32 = jnp.float32


def swap_bit(x, axis, bit):
    return lax.ppermute(x, axis, [(i, i ^ 1 << bit) for i in range(lax.axis_size(axis))])


def dot(a, b, dims=((1,), (0,))):
    return lax.dot_general(a, b, (dims, ((), ())), preferred_element_type=F32)


NT = ((1,), (1,))
TN = ((0,), (0,))


def head_lanes(first):
    lane = lax.broadcasted_iota(jnp.int32, (1, LANES), 1)
    return (lane < HDIM) if first else (lane >= HDIM)


def vmem(limit=56):
    return pltpu.CompilerParams(vmem_limit_bytes=limit * 1024 * 1024)


def whole(shape):
    return pl.BlockSpec(shape, lambda *_: (0,) * len(shape), pipeline_mode=pl.Buffered(1))


def hbm(*arrays):
    return [pltpu.with_memory_space_constraint(x, pltpu.HBM) for x in arrays]


def pick(own, w_own_ref, w_mate_ref):
    return jnp.where(own, w_own_ref[...], w_mate_ref[...])


def normalize(summed):
    center = summed - jnp.mean(summed, axis=-1, keepdims=True)
    rate = lax.rsqrt(jnp.mean(center * center, axis=-1, keepdims=True) + NORM_EPS)
    return center * rate, rate


def norm_back(grad, normed, rate, gain):
    scaled = grad * gain
    return rate * (
        scaled
        - jnp.mean(scaled, axis=-1, keepdims=True)
        - normed * jnp.mean(scaled * normed, axis=-1, keepdims=True)
    )


def gelu_parts(u):
    size = jnp.abs(u)
    bell = jnp.exp2(u * u * (-0.5 * LOG2E))
    t = 1.0 / (1.0 + (0.3275911 * 0.5**0.5) * size)
    poly = t * (
        0.5 * 0.254829592
        + t
        * (
            0.5 * -0.284496736
            + t * (0.5 * 1.421413741 + t * (0.5 * -1.453152027 + t * (0.5 * 1.061405429)))
        )
    )
    tail = poly * bell
    phi = jnp.where(u > 0, 1.0 - tail, tail)
    return u * phi, phi + u * (bell * 0.3989422804014327)


SLOTS = (slice(0, BLOCK), slice(BLOCK, 2 * BLOCK))


def attend_kernel(
    pairs, swap_ref, xa_ref, xb_ref, wq_ref, wk_ref, wv_ref, mq_ref, mk_ref, mv_ref, wo_ref, mo_ref,
    qkv_ref, lse_ref, ctx_t_ref, x_t_ref, mid_n_ref, rate_ref, ctx_all,
):
    step = pl.program_id(0)
    own = step < pairs // 2
    swap = swap_ref[...] > 0
    scale = LOG2E * HDIM**-0.5
    ones = jnp.ones((16, BLOCK), BF16)
    w = jnp.concatenate(
        [pick(own, wq_ref, mq_ref), pick(own, wk_ref, mk_ref), pick(own, wv_ref, mv_ref)], axis=1
    )
    for rows, x_ref in zip(SLOTS, (xa_ref, xb_ref)):
        qkv_ref[rows, :] = dot(x_ref[...], w).astype(BF16)
    keys = [qkv_ref[rows, LANES : 2 * LANES] for rows in SLOTS]
    values = [qkv_ref[rows, 2 * LANES :] for rows in SLOTS]
    units = []
    for i, rows in enumerate(SLOTS):
        q = qkv_ref[rows, :LANES]
        k = jnp.where(swap, keys[1 - i], keys[i])
        v_t = jnp.where(swap, values[1 - i], values[i]).T
        for n in (0, 1):
            q_n = jnp.where(head_lanes(n == 0), q, jnp.zeros_like(q))
            units.append((rows, n, v_t, dot(k, q_n, NT)))
    parts = []
    for rows, n, v_t, s in units:
        top = jnp.max(s, axis=0, keepdims=True)
        p = jnp.exp2((s - top) * scale).astype(BF16)
        v_n = jnp.concatenate([v_t[n * HDIM : (n + 1) * HDIM], ones], axis=0)
        acc = dot(v_n, p)
        total = acc[HDIM : HDIM + 1]
        parts.append(acc[:HDIM] / total)
        lse_ref[0, n : n + 1, rows] = top * scale + jnp.log2(total)
        if n == 1:
            ctx_t = jnp.concatenate(parts, axis=0)
            parts = []
            ctx_t_ref[:, rows] = ctx_t.astype(BF16)
            ctx_all[step, rows, :] = ctx_t.T.astype(BF16)

    cols = pl.ds(pl.multiple_of(step * LANES, LANES), LANES)
    for rows, x_ref in zip(SLOTS, (xa_ref, xb_ref)):
        x_t_ref[:, rows] = x_ref[:, cols].T

    @pl.when(step == pairs - 1)
    def _():
        for rows, x_ref in zip(SLOTS, (xa_ref, xb_ref)):
            total = x_ref[...].astype(F32)
            every = jnp.concatenate([ctx_all[p, rows, :] for p in range(pairs)], axis=1)
            cut = wo_ref.shape[0]
            total = total + dot(every[:, :cut], wo_ref[...]) + dot(every[:, cut:], mo_ref[...])
            normed, rate = normalize(total)
            mid_n_ref[rows, :] = normed
            rate_ref[rows, :] = rate


def attention(swap_lanes, blocks, own_w, mate_w, own_out, mate_out):
    width = blocks[0].shape[1]
    rows = 2 * BLOCK
    pairs = width // LANES
    per = own_w[0].shape[1] // LANES
    own_spec = pl.BlockSpec((width, LANES), lambda p: (0, jnp.minimum(p, per - 1)))
    mate_spec = pl.BlockSpec((width, LANES), lambda p: (0, jnp.maximum(p - per, 0)))
    return pl.pallas_call(
        functools.partial(attend_kernel, pairs),
        grid=(pairs,),
        in_specs=[pl.BlockSpec((1, LANES), lambda p: (0, p))]
        + [whole((BLOCK, width))] * 2
        + [own_spec] * 3
        + [mate_spec] * 3
        + [whole(own_out.shape)] * 2,
        out_specs=[
            pl.BlockSpec((rows, 3 * LANES), lambda p: (0, p)),
            pl.BlockSpec((1, 2, rows), lambda p: (p, 0, 0)),
            pl.BlockSpec((LANES, rows), lambda p: (p, 0)),
            pl.BlockSpec((LANES, rows), lambda p: (p, 0)),
            whole((rows, width)),
            whole((rows, 1)),
        ],
        out_shape=[
            pltpu.HBM((rows, 3 * width), BF16),
            jax.ShapeDtypeStruct((pairs, 2, rows), F32),
            pltpu.HBM((width, rows), BF16),
            pltpu.HBM((width, rows), BF16),
            pltpu.HBM((rows, width), F32),
            pltpu.HBM((rows, 1), F32),
        ],
        scratch_shapes=[pltpu.VMEM((pairs, rows, LANES), BF16)],
        compiler_params=vmem(28),
        cost_estimate=pl.CostEstimate(
            flops=2 * rows * width * width * 4 + 4 * pairs * 4 * BLOCK * BLOCK * 256,
            bytes_accessed=rows * width * 18 + width * width * 8,
            transcendentals=4 * pairs * BLOCK * BLOCK,
        ),
        name="attention_forward",
    )(swap_lanes, *blocks, *hbm(*own_w, *mate_w, own_out, mate_out))


def ffn_kernel(
    tiles, mid_n_ref, par_ref, wi_ref, mi_ref, bi_ref, mbi_ref, wd_ref, md_ref, ca_ref, cb_ref, wt_ref,
    act_t_ref, slope_ref, h1_t_ref, out_ref, ds2_ref, df_ref, vec_ref, h1_low, acc,
):
    step = pl.program_id(0)
    own = step < tiles // 2

    @pl.when(step == 0)
    def _():
        for rows in SLOTS:
            h1 = mid_n_ref[rows, :] * par_ref[0:1, :] + par_ref[1:2, :]
            low = h1.astype(BF16)
            h1_low[rows, :] = low
            h1_t_ref[:, rows] = low.T
            acc[rows, :] = h1 + par_ref[2:3, :]

    w_in = pick(own, wi_ref, mi_ref)
    w_down = pick(own, wd_ref, md_ref)
    bias = pick(own, bi_ref, mbi_ref)
    size = 256
    cuts = [slice(at, at + size) for at in range(0, 2 * BLOCK, size)]
    ready = [dot(h1_low[cuts[0], :], w_in)]
    for at, rows in enumerate(cuts):
        if at + 1 < len(cuts):
            ready.append(dot(h1_low[cuts[at + 1], :], w_in))
        value, slope = gelu_parts(ready[at] + bias)
        low = value.astype(BF16)
        slope_ref[rows, :] = slope.astype(BF16)
        act_t_ref[:, rows] = low.T
        acc[rows, :] += dot(low, w_down)

    @pl.when(step == tiles - 1)
    def _():
        gain = par_ref[3:4, :]
        sums = [0.0, 0.0, 0.0]
        for at in range(0, 2 * BLOCK, size):
            rows = slice(at, at + size)
            normed, rate = normalize(acc[rows, :])
            out_ref[rows, :] = (normed * gain + par_ref[4:5, :]).astype(BF16)
            cot_ref, first = (ca_ref, at) if at < BLOCK else (cb_ref, at - BLOCK)
            d_y = cot_ref[first : first + size, :].astype(F32) * wt_ref[rows, :]
            d_s2 = norm_back(d_y, normed, rate, gain)
            ds2_ref[rows, :] = d_s2
            df_ref[rows, :] = d_s2.astype(BF16)
            for n, term in enumerate((d_y, d_y * normed, d_s2)):
                sums[n] = sums[n] + jnp.sum(term, axis=0, keepdims=True)
        vec_ref[...] = jnp.concatenate(sums + [jnp.zeros((5, gain.shape[1]), F32)], axis=0)


TILE = 768
COLS = 384


def ffn(mid_n, params, own_in, mate_in, own_bias, mate_bias, own_down, mate_down, cot, weight):
    rows, width = mid_n.shape
    per = own_in.shape[1] // TILE
    tiles = 2 * per

    def own_at(j):
        return jnp.minimum(j, per - 1)

    def mate_at(j):
        return jnp.maximum(j - per, 0)

    hidden = 2 * own_in.shape[1]
    return pl.pallas_call(
        functools.partial(ffn_kernel, tiles),
        grid=(tiles,),
        in_specs=[
            whole((rows, width)),
            whole(params.shape),
            pl.BlockSpec((width, TILE), lambda j: (0, own_at(j))),
            pl.BlockSpec((width, TILE), lambda j: (0, mate_at(j))),
            pl.BlockSpec((1, TILE), lambda j: (0, own_at(j))),
            pl.BlockSpec((1, TILE), lambda j: (0, mate_at(j))),
            pl.BlockSpec((TILE, width), lambda j: (own_at(j), 0)),
            pl.BlockSpec((TILE, width), lambda j: (mate_at(j), 0)),
            whole((BLOCK, width)),
            whole((BLOCK, width)),
            whole((rows, 1)),
        ],
        out_specs=[
            pl.BlockSpec((TILE, rows), lambda j: (j, 0)),
            pl.BlockSpec((rows, TILE), lambda j: (0, j)),
            whole((width, rows)),
            whole((rows, width)),
            whole((rows, width)),
            whole((rows, width)),
            whole((8, width)),
        ],
        out_shape=[
            jax.ShapeDtypeStruct((hidden, rows), BF16),
            pltpu.HBM((rows, hidden), BF16),
            jax.ShapeDtypeStruct((width, rows), BF16),
            jax.ShapeDtypeStruct((rows, width), BF16),
            jax.ShapeDtypeStruct((rows, width), F32),
            jax.ShapeDtypeStruct((rows, width), BF16),
            jax.ShapeDtypeStruct((8, width), F32),
        ],
        scratch_shapes=[pltpu.VMEM((rows, width), BF16), pltpu.VMEM((rows, width), F32)],
        compiler_params=vmem(40),
        cost_estimate=pl.CostEstimate(
            flops=4 * rows * width * hidden,
            bytes_accessed=rows * hidden * 4 + rows * width * 16 + width * hidden * 4,
            transcendentals=rows * hidden * 2,
        ),
        name="feed_forward",
    )(
        *hbm(mid_n), params, *hbm(own_in, mate_in), own_bias, mate_bias,
        *hbm(own_down, mate_down), *cot, weight,
    )


def product_kernel(a_ref, b_ref, c_ref):
    c_ref[...] = dot(a_ref[...], b_ref[...]).astype(BF16)


def product(a, first, rows, b, block):
    return pl.pallas_call(
        product_kernel,
        grid=(rows // block,),
        in_specs=[pl.BlockSpec((block, a.shape[1]), lambda j: (j + first // block, 0)), whole(b.shape)],
        out_specs=pl.BlockSpec((block, b.shape[1]), lambda j: (j, 0)),
        out_shape=jax.ShapeDtypeStruct((rows, b.shape[1]), BF16),
        compiler_params=vmem(12),
        cost_estimate=pl.CostEstimate(
            flops=2 * rows * a.shape[1] * b.shape[1],
            bytes_accessed=2 * (rows * (a.shape[1] + b.shape[1]) + b.shape[0] * b.shape[1]),
            transcendentals=0,
        ),
        name="weight_gradient",
    )(a, b)


def ffn_back_kernel(
    last, df_ref, slope_ref, wi_ref, wd_ref, h1_t_ref, start_ref, *refs
):
    if last:
        (mid_n_ref, rate_ref, ctx_t_ref, par_ref, gin_ref, db_ref, gown_ref, gmate_ref, ds1_ref,
         da_ref, vec_ref, du, acc) = refs
    else:
        gin_ref, db_ref, acc, du = refs
    step = pl.program_id(0)
    w_in = wi_ref[...]
    w_down = wd_ref[...]

    @pl.when(step == 0)
    def _():
        acc[...] = start_ref[...]

    size = 256
    total = 0.0
    cuts = [slice(at, at + size) for at in range(0, 2 * BLOCK, size)]
    ready = [dot(df_ref[cuts[0], :], w_down, NT)]
    for at, rows in enumerate(cuts):
        if at + 1 < len(cuts):
            ready.append(dot(df_ref[cuts[at + 1], :], w_down, NT))
        d_u = ready[at] * slope_ref[rows, :].astype(F32)
        total = total + jnp.sum(d_u, axis=0, keepdims=True)
        low = d_u.astype(BF16)
        du[rows, :] = low
        acc[rows, :] += dot(low, w_in, NT)
    db_ref[...] = total
    gin_ref[0] = dot(h1_t_ref[...], du[...]).astype(BF16)
    if not last:
        return

    @pl.when(step == pl.num_programs(0) - 1)
    def _():
        sums = [0.0, 0.0]
        gain = par_ref[0:1, :]
        for at in range(0, 2 * BLOCK, size):
            rows = slice(at, at + size)
            d_h1 = acc[rows, :]
            normed = mid_n_ref[rows, :]
            d_s1 = norm_back(d_h1, normed, rate_ref[rows, :], gain)
            ds1_ref[rows, :] = d_s1
            da_ref[rows, :] = d_s1.astype(BF16)
            for n, term in enumerate((d_h1, d_h1 * normed)):
                sums[n] = sums[n] + jnp.sum(term, axis=0, keepdims=True)
        vec_ref[...] = jnp.concatenate(sums + [jnp.zeros((6, gain.shape[1]), F32)], axis=0)
        cut = gown_ref.shape[0]
        gown_ref[...] = dot(ctx_t_ref[:cut, :], da_ref[...]).astype(BF16)
        gmate_ref[...] = dot(ctx_t_ref[cut:, :], da_ref[...]).astype(BF16)


def ffn_back(first, d_f, slope, w_in, w_down, h1_t, start, *rest):
    rows, width = d_f.shape
    hidden = w_in.shape[1]
    tiles = hidden // TILE
    last = len(rest) > 0
    grid_out = [
        pl.BlockSpec((1, width, TILE), lambda j: (j, 0, 0)),
        pl.BlockSpec((1, TILE), lambda j: (0, j)),
    ]
    shapes = [
        jax.ShapeDtypeStruct((tiles, width, TILE), BF16),
        jax.ShapeDtypeStruct((1, hidden), F32),
    ]
    scratch = [pltpu.VMEM((rows, TILE), BF16)]
    if last:
        whole_out = [((width // 2, width), BF16)] * 2 + [
            ((rows, width), F32), ((rows, width), BF16), ((8, width), F32)
        ]
        scratch.append(pltpu.VMEM((rows, width), F32))
    else:
        whole_out = [((rows, width), F32)]
    return pl.pallas_call(
        functools.partial(ffn_back_kernel, last),
        grid=(tiles,),
        in_specs=[
            whole((rows, width)),
            pl.BlockSpec((rows, TILE), lambda j: (0, j + first * tiles)),
            pl.BlockSpec((width, TILE), lambda j: (0, j)),
            pl.BlockSpec((TILE, width), lambda j: (j, 0)),
            whole((width, rows)),
            whole((rows, width)),
        ]
        + [whole(x.shape) for x in rest],
        out_specs=grid_out + [whole(shape) for shape, _ in whole_out],
        out_shape=shapes + [jax.ShapeDtypeStruct(shape, kind) for shape, kind in whole_out],
        scratch_shapes=scratch,
        compiler_params=vmem(32),
        cost_estimate=pl.CostEstimate(
            flops=6 * rows * width * hidden,
            bytes_accessed=rows * hidden * 2 + rows * width * 18 + width * hidden * 6,
            transcendentals=0,
        ),
        name="feed_forward_back",
    )(d_f, *hbm(slope, w_in, w_down), h1_t, start, *hbm(*rest[:-1]), *rest[-1:])


def attend_back_kernel(
    steps, swap_ref, qkv_ref, ctx_t_ref, lse_ref, wq_ref, wk_ref, wv_ref, wo_ref, da_ref, x_t_ref,
    start_ref, gw_ref, dx_ref, dqkv,
):
    step = pl.program_id(0)
    swap = swap_ref[...] > 0
    scale = LOG2E * HDIM**-0.5

    @pl.when(step == 0)
    def _():
        dx_ref[...] = start_ref[...]

    keys = [qkv_ref[rows, LANES : 2 * LANES] for rows in SLOTS]
    values = [qkv_ref[rows, 2 * LANES :] for rows in SLOTS]
    blocks, units = [], []
    for i, rows in enumerate(SLOTS):
        q = qkv_ref[rows, :LANES]
        k = jnp.where(swap, keys[1 - i], keys[i])
        v = jnp.where(swap, values[1 - i], values[i])
        dctx = dot(da_ref[rows, :], wo_ref[...], NT).astype(BF16)
        prod_t = dctx.T.astype(F32) * ctx_t_ref[:, rows].astype(F32)
        blocks.append((rows, q, k, v, k.T, dctx, prod_t))
    for i, (rows, q, k, v, k_t, dctx, prod_t) in enumerate(blocks):
        for n in (0, 1):
            own = head_lanes(n == 0)
            q_n = jnp.where(own, q, jnp.zeros_like(q))
            d_n = jnp.where(own, dctx, jnp.zeros_like(dctx))
            units.append((i, n, q_n, d_n))

    def products(unit):
        i, n, q_n, d_n = unit
        return dot(blocks[i][2], q_n, NT), dot(blocks[i][3], d_n, NT)

    ahead = 1
    ready = [products(unit) for unit in units[:ahead]]
    found = []
    for at, (i, n, q_n, d_n) in enumerate(units):
        if at + ahead < len(units):
            ready.append(products(units[at + ahead]))
        rows, q, k, v, k_t, dctx, prod_t = blocks[i]
        cut = slice(n * HDIM, (n + 1) * HDIM)
        s, d_p = ready[at]
        p = jnp.exp2(s * scale - lse_ref[0, n : n + 1, rows])
        inner = jnp.sum(prod_t[cut], axis=0, keepdims=True)
        ds = (p * (d_p - inner)).astype(BF16)
        dv_n = dot(p.astype(BF16), d_n)
        dk_n = dot(ds, q_n)
        if n == 0:
            dv, dk, dq_t = dv_n, dk_n, [dot(k_t[cut], ds)]
        else:
            dv, dk = dv + dv_n, dk + dk_n
            dq_t.append(dot(k_t[cut], ds))
            dq = jnp.concatenate(dq_t, axis=0).T
            dqkv[rows, :LANES] = (dq * HDIM**-0.5).astype(BF16)
            found.append(((dk * HDIM**-0.5).astype(BF16), dv.astype(BF16)))
    for i, rows in enumerate(SLOTS):
        for at in (0, 1):
            dqkv[rows, (at + 1) * LANES : (at + 2) * LANES] = jnp.where(
                swap, found[1 - i][at], found[i][at]
            )
    gw_ref[0] = dot(x_t_ref[...], dqkv[...]).astype(BF16)
    w = jnp.concatenate([wq_ref[...], wk_ref[...], wv_ref[...]], axis=1)
    for rows in SLOTS:
        dx_ref[rows, :] += dot(dqkv[rows, :], w, NT)


def attention_back(first, swap_lanes, qkv, ctx_t, lse, weights, w_out, d_a, x_t, start):
    rows, width = d_a.shape
    pairs = w_out.shape[0] // LANES
    w_spec = pl.BlockSpec((width, LANES), lambda p: (0, p))
    return pl.pallas_call(
        functools.partial(attend_back_kernel, pairs),
        grid=(pairs,),
        in_specs=[
            pl.BlockSpec((1, LANES), lambda p: (0, p + first)),
            pl.BlockSpec((rows, 3 * LANES), lambda p: (0, p + first)),
            pl.BlockSpec((LANES, rows), lambda p: (p + first, 0)),
            pl.BlockSpec((1, 2, rows), lambda p: (p + first, 0, 0)),
            w_spec,
            w_spec,
            w_spec,
            pl.BlockSpec((LANES, width), lambda p: (p, 0)),
            whole((rows, width)),
            whole((width, rows)),
            whole((rows, width)),
        ],
        out_specs=[
            pl.BlockSpec((1, width, 3 * LANES), lambda p: (p, 0, 0)),
            whole((rows, width)),
        ],
        out_shape=[
            jax.ShapeDtypeStruct((pairs, width, 3 * LANES), BF16),
            jax.ShapeDtypeStruct((rows, width), F32),
        ],
        scratch_shapes=[pltpu.VMEM((rows, 3 * LANES), BF16)],
        compiler_params=vmem(24),
        cost_estimate=pl.CostEstimate(
            flops=14 * rows * width * pairs * LANES + 4 * pairs * 10 * BLOCK * BLOCK * 256,
            bytes_accessed=rows * width * 14,
            transcendentals=4 * pairs * BLOCK * BLOCK,
        ),
        name="attention_backward",
    )(swap_lanes, *hbm(qkv, ctx_t), lse, *hbm(*weights, w_out), d_a, *hbm(x_t), start)


def halves(x, place):
    rows = x.shape[0] // 2
    return (
        lax.dynamic_slice_in_dim(x, place * rows, rows, 0),
        lax.dynamic_slice_in_dim(x, (1 - place) * rows, rows, 0),
    )


def joined(mine, other, place):
    return jnp.where(
        place == 0,
        jnp.concatenate([mine, other], axis=0),
        jnp.concatenate([other, mine], axis=0),
    )


def add_low(a, b):
    return (a.astype(F32) + b.astype(F32)).astype(BF16)


def after(x, *others):
    return lax.optimization_barrier((x, others))[0]


def spots(left, bit, value):
    low = sum(other < bit for other in left)
    count = 1 << (len(left) - 1)
    return [((n >> low) << (low + 1) | n & ((1 << low) - 1)) + (value << low) for n in range(count)]


class Streams:
    def __init__(self, refs, rows):
        self.refs, self.rows = refs, rows

    def at(self, stream, spot):
        if len(self.refs) == 2:
            return self.refs[stream].at[spot]
        first = sum(self.rows[:stream])
        return self.refs[0].at[spot, first : first + self.rows[stream]]


class TokSum:
    def __init__(self, streams, own, got, extra=None, finish=None, alone=False):
        self.size = lax.axis_size("tok")
        bits = self.size.bit_length() - 1
        self.there = [(0, 1), (1, 0)] + [(bit, bit) for bit in range(2, bits)]
        self.left = [list(reversed(range(bits)))] * 2
        self.job = 0
        self.alone = alone
        self.extra, self.finish = extra, finish
        units = [0] * len(own)
        for stream in streams:
            for n, first, rows in stream:
                units[n] = math.gcd(units[n], first, rows // self.size)
        self.items = [
            [(n, first // units[n], rows // self.size // units[n], units[n]) for n, first, rows in stream]
            for stream in streams
        ]
        self.rows = [sum(rows // self.size for _, _, rows in stream) for stream in streams]
        self.width = own[0].shape[-1]
        self.inputs = [
            x.reshape(-1, unit, self.width) for xs in (own, got) for x, unit in zip(xs, units)
        ]

    def shapes(self, count, together):
        rows = [sum(self.rows)] if together else self.rows
        return [jax.ShapeDtypeStruct((count, row, self.width), BF16) for row in rows]

    def work(self):
        steps = len(self.there)
        job, self.job = self.job, self.job + 1
        if job <= steps:
            return self.adding(job, steps)
        return self.joining(2 * steps - job)

    def adding(self, job, steps):
        inputs, rows, left = self.inputs, self.rows, self.left
        extra = self.extra if job == steps else None
        if job < steps:
            bits = self.there[job]
            together = bits[0] == bits[1]
            half = self.shapes(1 << (len(left[0]) - 1), together)
            shapes = half + half
            self.left = [[b for b in mine if b != bit] for mine, bit in zip(left, bits)]
        else:
            bits = None
            if extra is not None:
                self.rows = [row + x.shape[0] for row, x in zip(rows, extra)]
                inputs = inputs + list(extra)
            shapes = self.shapes(1, True)
        new_rows = self.rows
        self.sent = len(shapes) // 2 if job < steps else 0

        def body(place, ins, outs):
            if extra is not None:
                ins, extras = ins[:-2], ins[-2:]
            count = len(ins) // 2

            def sums(stream, spot):
                if job > 0:
                    found = [Streams(ins[:count], rows), Streams(ins[count:], rows)]
                    a, b = (part.at(stream, spot)[...] for part in found)
                    return [(0, rows[stream], add_low(a, b))]
                first, found = 0, []
                for n, base, count_each, unit in self.items[stream]:
                    for piece in range(count_each):
                        block = base + spot * count_each + piece
                        found.append((first, unit, add_low(ins[n][block], ins[count + n][block])))
                        first += unit
                return found

            for stream in (0, 1):
                if bits is None:
                    ref = Streams(outs, new_rows).at(stream, 0)
                    ((_, row, value),) = sums(stream, 0)
                    ref[:row, :] = value
                    if extra is not None:
                        ref[row:, :] = extras[stream][...]
                    continue
                mine = place >> bits[stream] & 1
                split = len(outs) // 2
                for which, value in ((0, mine), (1, 1 - mine)):
                    target = Streams(outs[which * split : (which + 1) * split], rows)
                    for n, spot in enumerate(spots(left[stream], bits[stream], value)):
                        ref = target.at(stream, n)
                        for first, row, total in sums(stream, spot):
                            ref[first : first + row, :] = total

        return inputs, shapes, body

    def joining(self, step):
        inputs, rows = self.inputs, self.rows
        bits = self.there[step]
        before = self.left
        self.left = left = [sorted(have + [bit], reverse=True) for have, bit in zip(before, bits)]
        self.sent = 0
        if step == 0:
            shapes, write = self.finish(rows)
        else:
            then = self.there[step - 1]
            shapes = self.shapes(1 << len(left[0]), then[0] == then[1])

        def body(place, ins, outs):
            count = len(ins) // 2
            found = [Streams(ins[:count], rows), Streams(ins[count:], rows)]
            for stream in (0, 1):
                bit = bits[stream]
                mine = place >> bit & 1
                if step == 0:
                    low = sum(other < bit for other in left[stream])
                    for spot in range(1 << len(left[stream])):
                        n = (spot >> (low + 1)) << low | spot & ((1 << low) - 1)
                        kept, new = (part.at(stream, n)[...] for part in found)
                        write(outs, stream, spot, jnp.where(mine == (spot >> low & 1), kept, new))
                    continue
                for part, value in zip(found, (mine, 1 - mine)):
                    for n, spot in enumerate(spots(left[stream], bit, value)):
                        Streams(outs, rows).at(stream, spot)[...] = part.at(stream, n)[...]

        return inputs, shapes, body

    def take(self, outs):
        steps = len(self.there)
        if self.job > 2 * steps:
            self.found = outs
            return []
        kept, sent = (outs[: self.sent], outs[self.sent :]) if self.sent else (outs, outs)
        if self.job == steps + 1 and self.alone:
            self.piece = [sent[0].reshape(sent[0].shape[1:])]
            return sent
        step = self.job - 1 if self.job <= steps else 2 * steps - self.job
        got = [swap_bit(x, "tok", bit) for x, bit in zip(sent, self.there[step])]
        self.inputs = list(kept) + got
        return sent


def gather_rest(one):
    spread = lax.all_gather(one.piece[0], "tok", axis=0)
    one.job = 2 * len(one.there) + 1
    rows = one.rows
    shapes, write = one.finish(rows)

    def kernel(x_ref, *outs):
        for spot in range(x_ref.shape[0]):
            write(outs, 0, spot, x_ref[spot, : rows[0]])
            write(outs, 1, spot, x_ref[spot, rows[0] :])

    one.found = pl.pallas_call(
        kernel,
        in_specs=[pl.BlockSpec(memory_space=pltpu.VMEM)],
        out_specs=[pl.BlockSpec(memory_space=pltpu.VMEM)] * len(shapes),
        out_shape=shapes,
        compiler_params=vmem(32),
        name="sum_spread",
    )(spread)


class PlainSum:
    def __init__(self, streams, own, got, extra=None, finish=None, alone=False):
        whole = [
            lax.psum(a.astype(F32) + b.astype(F32), "tok").reshape(-1, a.shape[-1])
            for a, b in zip(own, got)
        ]
        self.found = [
            [whole[n][first : first + rows] for n, first, rows in stream] for stream in streams
        ]


def advance(sums, *others):
    if not isinstance(sums[0], TokSum):
        return []
    place = after(lax.axis_index("tok").astype(jnp.int32).reshape(1), *others)
    works = [one.work() for one in sums]

    def kernel(place_ref, *refs):
        place = place_ref[0]
        ins = refs[: sum(len(work[0]) for work in works)]
        outs = refs[len(ins) :]
        for inputs, shapes, body in works:
            body(place, ins[: len(inputs)], outs[: len(shapes)])
            ins, outs = ins[len(inputs) :], outs[len(shapes) :]

    inputs = [x for work in works for x in work[0]]
    shapes = [x for work in works for x in work[1]]
    size = sum(x.size * x.dtype.itemsize for x in inputs + shapes)
    outs = pl.pallas_call(
        kernel,
        in_specs=[pl.BlockSpec(memory_space=pltpu.SMEM)]
        + [pl.BlockSpec(memory_space=pltpu.VMEM)] * len(inputs),
        out_specs=[pl.BlockSpec(memory_space=pltpu.VMEM)] * len(shapes),
        out_shape=shapes,
        compiler_params=vmem(32),
        cost_estimate=pl.CostEstimate(flops=size, bytes_accessed=size, transcendentals=0),
        name="sum_step",
    )(place, *inputs)
    sent = []
    for one, work in zip(sums, works):
        sent += one.take(outs[: len(work[1])])
        outs = outs[len(work[1]) :]
    return sent


def body(
    tokens,
    cotangent,
    block_source,
    mask_index,
    mask_count,
    w_query,
    w_key,
    w_value,
    w_output,
    mid_gain,
    mid_shift,
    w_inner,
    bias_inner,
    w_outer,
    bias_outer,
    end_gain,
    end_shift,
):
    tok_place = lax.axis_index("tok")
    head_place = lax.axis_index("head")
    half = tok_place % 2
    width = tokens.shape[1]

    def mate(x):
        return swap_bit(x, "head", 0)

    kept, given = halves(tokens, half)
    cot_kept, cot_given = halves(cotangent, half)
    x_got = swap_bit(given, "tok", 0)
    own_w = (w_query, w_key, w_value)
    mate_w = tuple(mate(w) for w in own_w)
    mate_out = mate(w_output)
    mate_in = mate(w_inner)
    mate_down = mate(w_outer)
    own_bias = bias_inner[None, :]
    mate_bias = mate(own_bias)

    sequence = tok_place // 2 * PAIR_SEQS + 2 * head_place + half
    source = lax.dynamic_slice_in_dim(block_source, sequence, 1, 0)[0, :, 0]
    per_half = GROUPS // 2
    flags = jnp.concatenate(
        [
            lax.dynamic_slice_in_dim(source, head_place * per_half, per_half, 0),
            lax.dynamic_slice_in_dim(source, (1 - head_place) * per_half, per_half, 0),
        ]
    )
    swap_lanes = jnp.repeat(flags, HEADS // GROUPS * HDIM)[None, :]
    positions = lax.dynamic_slice_in_dim(mask_index, sequence, 1, 0)[0]
    count = lax.dynamic_slice_in_dim(mask_count, sequence, 1, 0)[0]
    within = jnp.arange(BLOCK)
    places = jnp.concatenate([half * BLOCK + within, (1 - half) * BLOCK + within])
    live = jnp.arange(positions.shape[0]) < count
    hits = jnp.any((positions[None, :] == places[:, None]) & live[None, :], axis=1)
    weight = (1.0 + 3.0 * hits.astype(F32))[:, None]
    params = jnp.stack(
        [mid_gain, mid_shift, bias_outer, end_gain, end_shift] + [jnp.zeros_like(mid_gain)] * 3
    )

    qkv, lse, ctx_t, x_t, mid_n, mid_rate = attention(
        swap_lanes, (kept, after(x_got, swap_lanes, weight, params, cot_kept)), own_w, mate_w,
        w_output, mate_out,
    )
    cot_got = swap_bit(after(cot_given, x_got), "tok", 0)
    act_t, slope, h1_t, out, d_s2, d_f, end_vec = ffn(
        mid_n, params, w_inner, mate_in, own_bias, mate_bias, w_outer, mate_down,
        (cot_kept, cot_got), weight,
    )

    hidden = w_inner.shape[1]
    cut = w_output.shape[0]
    pairs = cut // LANES

    def side_by_side(g):
        return jnp.concatenate([g[:, n : n + COLS] for n in range(0, width, COLS)], axis=0)

    rest = width // 2

    def finish_down(rows):
        def write(outs, stream, spot, value):
            outs[0][stream, spot] = value.astype(F32)

        return [jax.ShapeDtypeStruct((2, lax.axis_size("tok"), rows[0], width), F32)], write

    def finish_inner(rows):
        size = lax.axis_size("tok")

        def write(outs, stream, spot, value):
            value = value.astype(F32)
            outs[0][spot, :, stream * width : (stream + 1) * width] = value[: rows[0]]
            if stream == 1:
                outs[1][spot] = value[rows[0] :]

        return [
            jax.ShapeDtypeStruct((size, rows[0], 2 * width), F32),
            jax.ShapeDtypeStruct((size, rows[1] - rows[0], width), F32),
        ], write

    size = lax.axis_size("tok")
    fits = size & (size - 1) == 0 and size >= 4 and rest % (8 * size) == 0
    Sum = TokSum if fits else PlainSum

    got = mate(product(act_t, hidden, hidden, d_f, BLOCK))
    mine = product(act_t, 0, hidden, d_f, BLOCK)
    cut = hidden // 2
    down = Sum([[(0, 0, cut)], [(0, cut, cut)]], [mine], [got], finish=finish_down, alone=False)
    part = BLOCK + BLOCK // 2
    out_first = swap_bit(out[BLOCK:part], "tok", 0)
    sent = advance([down], mine, out_first)
    gi_mate, gb_mate, d_h1 = ffn_back(
        1, after(d_f, sent), slope, mate_in, mate_down, h1_t, d_s2
    )
    sent = advance([down], gi_mate)
    out_rest = swap_bit(after(out[part:], sent), "tok", 0)
    got_in = mate(after(gi_mate, sent))
    gi_own, gb_own, go_own, go_mate, d_s1, d_a, mid_vec = ffn_back(
        0, after(d_f, sent), slope, w_inner, w_outer, h1_t, d_h1, mid_n, mid_rate, ctx_t, params
    )
    got_out = mate(after(go_mate, down.inputs[-2:]) if fits else go_mate)
    inner = Sum(
        [[(0, 0, width)], [(0, width, width), (1, 0, rest)]],
        [gi_own, go_own], [got_in, got_out], finish=finish_inner, alone=False,
    )
    sent = advance([inner, down], gi_own)
    gw_mate, d_x = attention_back(
        pairs, swap_lanes, qkv, ctx_t, lse, mate_w, mate_out, after(d_a, sent), x_t, d_s1
    )
    sent = advance([inner, down], gw_mate, out_rest)
    out = joined(out[:BLOCK], jnp.concatenate([out_first, out_rest], axis=0), half)
    gw_got = mate(after(gw_mate, sent))

    gb_own, gb_mate = gb_own.reshape(-1, width), gb_mate.reshape(-1, width)
    own_rows = gb_own.shape[0]
    small = jnp.concatenate([end_vec[:3], mid_vec[:2], gb_own, gb_mate], axis=0)
    theirs = mate(small)
    small = jnp.concatenate(
        [
            small[:5] + theirs[:5],
            small[5 : 5 + own_rows] + theirs[5 + own_rows :],
            jnp.zeros((1, width), F32),
        ],
        axis=0,
    )
    high = small.astype(BF16)
    low = (small - high.astype(F32)).astype(BF16)
    high, low = side_by_side(high), side_by_side(low)

    gw_own, d_x = attention_back(
        0, swap_lanes, qkv, ctx_t, lse, own_w, w_output, after(d_a, sent), x_t, d_x
    )
    cut = (pairs * width // size + 31) // 32 * 16 * size

    def finish_last(rows):
        def write(outs, stream, spot, value):
            value = value.astype(F32)
            extra = high.shape[0]
            count = rows[stream] - extra
            first = spot * count + (0 if stream == 0 else cut)
            done = 0
            while done < count:
                p, row = divmod(first + done, width)
                step = min(count - done, width - row)
                for at in range(3):
                    outs[at][row : row + step, p * LANES : (p + 1) * LANES] = value[
                        done : done + step, at * LANES : (at + 1) * LANES
                    ]
                done += step
            if stream == 0 and spot == 0:
                outs[3][...] = value[count:]
            else:
                outs[3][...] += value[count:]

        return [jax.ShapeDtypeStruct((width, pairs * LANES), F32)] * 3 + [
            jax.ShapeDtypeStruct(high.shape, F32)
        ], write

    last = Sum(
        [[(0, 0, cut)], [(0, cut, pairs * width - cut)]], [gw_own], [gw_got],
        extra=(high, low), finish=finish_last,
    )
    advance([last, inner, down], gw_own)
    dx_got = []
    if fits:
        while last.job <= 2 * len(last.there):
            for one in (inner, down):
                if one.alone and one.job == len(one.there) + 1:
                    gather_rest(one)
            sums = [one for one in (last, inner, down) if one.job <= 2 * len(one.there)]
            others = []
            if last.job in (2, 3):
                first = BLOCK + (last.job - 2) * (BLOCK // 2)
                rows_low = d_x[first : first + BLOCK // 2].astype(BF16)
                others = [swap_bit(after(rows_low, last.inputs[0]), "tok", 0)]
                dx_got += others
            advance(sums, *others)
        g_down, (g_in, g_out), (g_query, g_key, g_value, sums) = (
            down.found[0], inner.found, last.found
        )
        small = jnp.concatenate([sums[: small.shape[0]], sums[small.shape[0] :]], axis=1)
    else:
        dx_got = [swap_bit(d_x[BLOCK:].astype(BF16), "tok", 0)]
        g_down = jnp.concatenate([down.found[0][0], down.found[1][0]], axis=0)
        g_in = jnp.concatenate([inner.found[0][0], inner.found[1][0]], axis=1)
        g_out = inner.found[1][1]
        whole_w = jnp.concatenate([last.found[0][0], last.found[1][0]], axis=0)
        whole_w = whole_w.reshape(pairs, width, 3, LANES)
        g_query, g_key, g_value = (
            jnp.concatenate([whole_w[p, :, at] for p in range(pairs)], axis=1) for at in range(3)
        )
        small = lax.psum(small, "tok")
    dx_got = jnp.concatenate(dx_got, axis=0).astype(F32)
    grad_tokens = joined(d_x[:BLOCK], dx_got, half)
    g_down = g_down.reshape(hidden, width)
    g_in = g_in.reshape(width, hidden)
    g_out = g_out.reshape(rest, width)

    return (
        out,
        grad_tokens,
        g_query,
        g_key,
        g_value,
        g_out,
        small[4],
        small[3],
        g_in,
        small[5 : 5 + own_rows].reshape(-1),
        g_down,
        small[2],
        small[1],
        small[0],
    )


def solution(mesh):
    rows = P(("tok", "head"), None)
    return jax.shard_map(
        body,
        mesh=mesh,
        in_specs=(
            rows,
            rows,
            P(),
            P(),
            P(),
            P(None, "head"),
            P(None, "head"),
            P(None, "head"),
            P("head", None),
            P(),
            P(),
            P(None, "head"),
            P("head"),
            P("head", None),
            P(),
            P(),
            P(),
        ),
        out_specs=(
            rows,
            rows,
            P(None, "head"),
            P(None, "head"),
            P(None, "head"),
            P("head", None),
            P(),
            P(),
            P(None, "head"),
            P("head"),
            P("head", None),
            P(),
            P(),
            P(),
        ),
        check_vma=False,
    )
```

```python
import functools
import math

import jax
import jax.numpy as jnp
from jax import lax
from jax.experimental import pallas as pl
from jax.experimental.pallas import tpu as pltpu
from jax.sharding import PartitionSpec as P

HEADS = 12
HDIM = 64
GROUPS = 4
BLOCK = 512
PAIR_SEQS = 4
LANES = 128

NORM_EPS = 1e-05
LOG2E = 1.4426950408889634
BF16 = jnp.bfloat16
F32 = jnp.float32


def swap_bit(x, axis, bit):
    return lax.ppermute(x, axis, [(i, i ^ 1 << bit) for i in range(lax.axis_size(axis))])


def dot(a, b, dims=((1,), (0,))):
    return lax.dot_general(a, b, (dims, ((), ())), preferred_element_type=F32)


NT = ((1,), (1,))
TN = ((0,), (0,))


def head_lanes(first):
    lane = lax.broadcasted_iota(jnp.int32, (1, LANES), 1)
    return (lane < HDIM) if first else (lane >= HDIM)


def vmem(limit=56):
    return pltpu.CompilerParams(vmem_limit_bytes=limit * 1024 * 1024)


def whole(shape):
    return pl.BlockSpec(shape, lambda *_: (0,) * len(shape), pipeline_mode=pl.Buffered(1))


def hbm(*arrays):
    return [pltpu.with_memory_space_constraint(x, pltpu.HBM) for x in arrays]


def pick(own, w_own_ref, w_mate_ref):
    return jnp.where(own, w_own_ref[...], w_mate_ref[...])


def normalize(summed):
    center = summed - jnp.mean(summed, axis=-1, keepdims=True)
    rate = lax.rsqrt(jnp.mean(center * center, axis=-1, keepdims=True) + NORM_EPS)
    return center * rate, rate


def norm_back(grad, normed, rate, gain):
    scaled = grad * gain
    return rate * (
        scaled
        - jnp.mean(scaled, axis=-1, keepdims=True)
        - normed * jnp.mean(scaled * normed, axis=-1, keepdims=True)
    )


def gelu_parts(u):
    size = jnp.abs(u)
    bell = jnp.exp2(u * u * (-0.5 * LOG2E))
    t = 1.0 / (1.0 + (0.3275911 * 0.5**0.5) * size)
    poly = t * (
        0.5 * 0.254829592
        + t
        * (
            0.5 * -0.284496736
            + t * (0.5 * 1.421413741 + t * (0.5 * -1.453152027 + t * (0.5 * 1.061405429)))
        )
    )
    tail = poly * bell
    phi = jnp.where(u > 0, 1.0 - tail, tail)
    return u * phi, phi + u * (bell * 0.3989422804014327)


SLOTS = (slice(0, BLOCK), slice(BLOCK, 2 * BLOCK))


def attend_kernel(
    pairs, swap_ref, xa_ref, xb_ref, wq_ref, wk_ref, wv_ref, mq_ref, mk_ref, mv_ref, wo_ref, mo_ref,
    qkv_ref, lse_ref, ctx_t_ref, x_t_ref, mid_n_ref, rate_ref, ctx_all,
):
    step = pl.program_id(0)
    own = step < pairs // 2
    swap = swap_ref[...] > 0
    scale = LOG2E * HDIM**-0.5
    ones = jnp.ones((16, BLOCK), BF16)
    w = jnp.concatenate(
        [pick(own, wq_ref, mq_ref), pick(own, wk_ref, mk_ref), pick(own, wv_ref, mv_ref)], axis=1
    )
    for rows, x_ref in zip(SLOTS, (xa_ref, xb_ref)):
        qkv_ref[rows, :] = dot(x_ref[...], w).astype(BF16)
    keys = [qkv_ref[rows, LANES : 2 * LANES] for rows in SLOTS]
    values = [qkv_ref[rows, 2 * LANES :] for rows in SLOTS]
    units = []
    for i, rows in enumerate(SLOTS):
        q = qkv_ref[rows, :LANES]
        k = jnp.where(swap, keys[1 - i], keys[i])
        v_t = jnp.where(swap, values[1 - i], values[i]).T
        for n in (0, 1):
            q_n = jnp.where(head_lanes(n == 0), q, jnp.zeros_like(q))
            units.append((rows, n, v_t, dot(k, q_n, NT)))
    parts = []
    for rows, n, v_t, s in units:
        top = jnp.max(s, axis=0, keepdims=True)
        p = jnp.exp2((s - top) * scale).astype(BF16)
        v_n = jnp.concatenate([v_t[n * HDIM : (n + 1) * HDIM], ones], axis=0)
        acc = dot(v_n, p)
        total = acc[HDIM : HDIM + 1]
        parts.append(acc[:HDIM] / total)
        lse_ref[0, n : n + 1, rows] = top * scale + jnp.log2(total)
        if n == 1:
            ctx_t = jnp.concatenate(parts, axis=0)
            parts = []
            ctx_t_ref[:, rows] = ctx_t.astype(BF16)
            ctx_all[step, rows, :] = ctx_t.T.astype(BF16)

    cols = pl.ds(pl.multiple_of(step * LANES, LANES), LANES)
    for rows, x_ref in zip(SLOTS, (xa_ref, xb_ref)):
        x_t_ref[:, rows] = x_ref[:, cols].T

    @pl.when(step == pairs - 1)
    def _():
        for rows, x_ref in zip(SLOTS, (xa_ref, xb_ref)):
            total = x_ref[...].astype(F32)
            every = jnp.concatenate([ctx_all[p, rows, :] for p in range(pairs)], axis=1)
            cut = wo_ref.shape[0]
            total = total + dot(every[:, :cut], wo_ref[...]) + dot(every[:, cut:], mo_ref[...])
            normed, rate = normalize(total)
            mid_n_ref[rows, :] = normed
            rate_ref[rows, :] = rate


def attention(swap_lanes, blocks, own_w, mate_w, own_out, mate_out):
    width = blocks[0].shape[1]
    rows = 2 * BLOCK
    pairs = width // LANES
    per = own_w[0].shape[1] // LANES
    own_spec = pl.BlockSpec((width, LANES), lambda p: (0, jnp.minimum(p, per - 1)))
    mate_spec = pl.BlockSpec((width, LANES), lambda p: (0, jnp.maximum(p - per, 0)))
    return pl.pallas_call(
        functools.partial(attend_kernel, pairs),
        grid=(pairs,),
        in_specs=[pl.BlockSpec((1, LANES), lambda p: (0, p))]
        + [whole((BLOCK, width))] * 2
        + [own_spec] * 3
        + [mate_spec] * 3
        + [whole(own_out.shape)] * 2,
        out_specs=[
            pl.BlockSpec((rows, 3 * LANES), lambda p: (0, p)),
            pl.BlockSpec((1, 2, rows), lambda p: (p, 0, 0)),
            pl.BlockSpec((LANES, rows), lambda p: (p, 0)),
            pl.BlockSpec((LANES, rows), lambda p: (p, 0)),
            whole((rows, width)),
            whole((rows, 1)),
        ],
        out_shape=[
            pltpu.HBM((rows, 3 * width), BF16),
            jax.ShapeDtypeStruct((pairs, 2, rows), F32),
            pltpu.HBM((width, rows), BF16),
            pltpu.HBM((width, rows), BF16),
            pltpu.HBM((rows, width), F32),
            pltpu.HBM((rows, 1), F32),
        ],
        scratch_shapes=[pltpu.VMEM((pairs, rows, LANES), BF16)],
        compiler_params=vmem(28),
        cost_estimate=pl.CostEstimate(
            flops=2 * rows * width * width * 4 + 4 * pairs * 4 * BLOCK * BLOCK * 256,
            bytes_accessed=rows * width * 18 + width * width * 8,
            transcendentals=4 * pairs * BLOCK * BLOCK,
        ),
        name="attention_forward",
    )(swap_lanes, *blocks, *hbm(*own_w, *mate_w, own_out, mate_out))


def ffn_kernel(
    tiles, mid_n_ref, par_ref, wi_ref, mi_ref, bi_ref, mbi_ref, wd_ref, md_ref, ca_ref, cb_ref, wt_ref,
    act_t_ref, slope_ref, h1_t_ref, out_ref, ds2_ref, df_ref, vec_ref, gm_ref, h1_low, acc, act_m,
):
    step = pl.program_id(0)
    own = step < tiles // 2

    @pl.when(step == 0)
    def _():
        for rows in SLOTS:
            h1 = mid_n_ref[rows, :] * par_ref[0:1, :] + par_ref[1:2, :]
            low = h1.astype(BF16)
            h1_low[rows, :] = low
            h1_t_ref[:, rows] = low.T
            acc[rows, :] = h1 + par_ref[2:3, :]

    size = 256

    def tile(w_in, w_down, bias, act_ref):
        cuts = [slice(at, at + size) for at in range(0, 2 * BLOCK, size)]
        ready = [dot(h1_low[cuts[0], :], w_in)]
        for at, rows in enumerate(cuts):
            if at + 1 < len(cuts):
                ready.append(dot(h1_low[cuts[at + 1], :], w_in))
            value, slope = gelu_parts(ready[at] + bias)
            low = value.astype(BF16)
            slope_ref[rows, :] = slope.astype(BF16)
            act_ref[:, rows] = low.T
            acc[rows, :] += dot(low, w_down)

    @pl.when(own)
    def _():
        tile(wi_ref[...], wd_ref[...], bi_ref[...], act_t_ref)

    @pl.when(jnp.logical_and(step >= tiles // 2, step < tiles))
    def _():
        tile(mi_ref[...], md_ref[...], mbi_ref[...], act_m.at[step - tiles // 2])

    @pl.when(step >= tiles)
    def _():
        gm_ref[...] = dot(act_m[step - tiles], df_ref[...]).astype(BF16)

    @pl.when(step == tiles - 1)
    def _():
        gain = par_ref[3:4, :]
        sums = [0.0, 0.0, 0.0]
        for at in range(0, 2 * BLOCK, size):
            rows = slice(at, at + size)
            normed, rate = normalize(acc[rows, :])
            out_ref[rows, :] = (normed * gain + par_ref[4:5, :]).astype(BF16)
            cot_ref, first = (ca_ref, at) if at < BLOCK else (cb_ref, at - BLOCK)
            d_y = cot_ref[first : first + size, :].astype(F32) * wt_ref[rows, :]
            d_s2 = norm_back(d_y, normed, rate, gain)
            ds2_ref[rows, :] = d_s2
            df_ref[rows, :] = d_s2.astype(BF16)
            for n, term in enumerate((d_y, d_y * normed, d_s2)):
                sums[n] = sums[n] + jnp.sum(term, axis=0, keepdims=True)
        vec_ref[...] = jnp.concatenate(sums + [jnp.zeros((5, gain.shape[1]), F32)], axis=0)


TILE = 768
COLS = 384


def ffn(mid_n, params, own_in, mate_in, own_bias, mate_bias, own_down, mate_down, cot, weight):
    rows, width = mid_n.shape
    per = own_in.shape[1] // TILE
    tiles = 2 * per

    def own_at(j):
        return jnp.minimum(j, per - 1)

    def mate_at(j):
        return jnp.clip(j - per, 0, per - 1)

    hidden = 2 * own_in.shape[1]
    return pl.pallas_call(
        functools.partial(ffn_kernel, tiles),
        grid=(tiles + per,),
        in_specs=[
            whole((rows, width)),
            whole(params.shape),
            pl.BlockSpec((width, TILE), lambda j: (0, own_at(j))),
            pl.BlockSpec((width, TILE), lambda j: (0, mate_at(j))),
            pl.BlockSpec((1, TILE), lambda j: (0, own_at(j))),
            pl.BlockSpec((1, TILE), lambda j: (0, mate_at(j))),
            pl.BlockSpec((TILE, width), lambda j: (own_at(j), 0)),
            pl.BlockSpec((TILE, width), lambda j: (mate_at(j), 0)),
            whole((BLOCK, width)),
            whole((BLOCK, width)),
            whole((rows, 1)),
        ],
        out_specs=[
            pl.BlockSpec((TILE, rows), lambda j: (own_at(j), 0)),
            pl.BlockSpec((rows, TILE), lambda j: (0, jnp.minimum(j, tiles - 1))),
            whole((width, rows)),
            whole((rows, width)),
            whole((rows, width)),
            whole((rows, width)),
            whole((8, width)),
            pl.BlockSpec((TILE, width), lambda j: (jnp.maximum(j - tiles, 0), 0)),
        ],
        out_shape=[
            jax.ShapeDtypeStruct((hidden // 2, rows), BF16),
            pltpu.HBM((rows, hidden), BF16),
            jax.ShapeDtypeStruct((width, rows), BF16),
            jax.ShapeDtypeStruct((rows, width), BF16),
            jax.ShapeDtypeStruct((rows, width), F32),
            jax.ShapeDtypeStruct((rows, width), BF16),
            jax.ShapeDtypeStruct((8, width), F32),
            jax.ShapeDtypeStruct((hidden // 2, width), BF16),
        ],
        scratch_shapes=[
            pltpu.VMEM((rows, width), BF16),
            pltpu.VMEM((rows, width), F32),
            pltpu.VMEM((per, TILE, rows), BF16),
        ],
        compiler_params=vmem(40),
        cost_estimate=pl.CostEstimate(
            flops=4 * rows * width * hidden,
            bytes_accessed=rows * hidden * 4 + rows * width * 16 + width * hidden * 4,
            transcendentals=rows * hidden * 2,
        ),
        name="feed_forward",
    )(
        *hbm(mid_n), params, *hbm(own_in, mate_in), own_bias, mate_bias,
        *hbm(own_down, mate_down), *cot, weight,
    )


def product_kernel(a_ref, b_ref, c_ref):
    c_ref[...] = dot(a_ref[...], b_ref[...]).astype(BF16)


def product(a, first, rows, b, block):
    return pl.pallas_call(
        product_kernel,
        grid=(rows // block,),
        in_specs=[pl.BlockSpec((block, a.shape[1]), lambda j: (j + first // block, 0)), whole(b.shape)],
        out_specs=pl.BlockSpec((block, b.shape[1]), lambda j: (j, 0)),
        out_shape=jax.ShapeDtypeStruct((rows, b.shape[1]), BF16),
        compiler_params=vmem(12),
        cost_estimate=pl.CostEstimate(
            flops=2 * rows * a.shape[1] * b.shape[1],
            bytes_accessed=2 * (rows * (a.shape[1] + b.shape[1]) + b.shape[0] * b.shape[1]),
            transcendentals=0,
        ),
        name="weight_gradient",
    )(a, b)


def ffn_back_kernel(
    last, df_ref, slope_ref, wi_ref, wd_ref, h1_t_ref, start_ref, *refs
):
    if last:
        (mid_n_ref, rate_ref, ctx_t_ref, par_ref, gin_ref, db_ref, gown_ref, gmate_ref, ds1_ref,
         da_ref, vec_ref, du, acc) = refs
    else:
        gin_ref, db_ref, acc, du = refs
    step = pl.program_id(0)
    w_in = wi_ref[...]
    w_down = wd_ref[...]

    @pl.when(step == 0)
    def _():
        acc[...] = start_ref[...]

    size = 256
    total = 0.0
    cuts = [slice(at, at + size) for at in range(0, 2 * BLOCK, size)]
    ready = [dot(df_ref[cuts[0], :], w_down, NT)]
    for at, rows in enumerate(cuts):
        if at + 1 < len(cuts):
            ready.append(dot(df_ref[cuts[at + 1], :], w_down, NT))
        d_u = ready[at] * slope_ref[rows, :].astype(F32)
        total = total + jnp.sum(d_u, axis=0, keepdims=True)
        low = d_u.astype(BF16)
        du[rows, :] = low
        acc[rows, :] += dot(low, w_in, NT)
    db_ref[...] = total
    gin_ref[0] = dot(h1_t_ref[...], du[...]).astype(BF16)
    if not last:
        return

    @pl.when(step == pl.num_programs(0) - 1)
    def _():
        sums = [0.0, 0.0]
        gain = par_ref[0:1, :]
        for at in range(0, 2 * BLOCK, size):
            rows = slice(at, at + size)
            d_h1 = acc[rows, :]
            normed = mid_n_ref[rows, :]
            d_s1 = norm_back(d_h1, normed, rate_ref[rows, :], gain)
            ds1_ref[rows, :] = d_s1
            da_ref[rows, :] = d_s1.astype(BF16)
            for n, term in enumerate((d_h1, d_h1 * normed)):
                sums[n] = sums[n] + jnp.sum(term, axis=0, keepdims=True)
        vec_ref[...] = jnp.concatenate(sums + [jnp.zeros((6, gain.shape[1]), F32)], axis=0)
        cut = gown_ref.shape[0]
        gown_ref[...] = dot(ctx_t_ref[:cut, :], da_ref[...]).astype(BF16)
        gmate_ref[...] = dot(ctx_t_ref[cut:, :], da_ref[...]).astype(BF16)


def ffn_back(first, d_f, slope, w_in, w_down, h1_t, start, *rest):
    rows, width = d_f.shape
    hidden = w_in.shape[1]
    tiles = hidden // TILE
    last = len(rest) > 0
    grid_out = [
        pl.BlockSpec((1, width, TILE), lambda j: (j, 0, 0)),
        pl.BlockSpec((1, TILE), lambda j: (0, j)),
    ]
    shapes = [
        jax.ShapeDtypeStruct((tiles, width, TILE), BF16),
        jax.ShapeDtypeStruct((1, hidden), F32),
    ]
    scratch = [pltpu.VMEM((rows, TILE), BF16)]
    if last:
        whole_out = [((width // 2, width), BF16)] * 2 + [
            ((rows, width), F32), ((rows, width), BF16), ((8, width), F32)
        ]
        scratch.append(pltpu.VMEM((rows, width), F32))
    else:
        whole_out = [((rows, width), F32)]
    return pl.pallas_call(
        functools.partial(ffn_back_kernel, last),
        grid=(tiles,),
        in_specs=[
            whole((rows, width)),
            pl.BlockSpec((rows, TILE), lambda j: (0, j + first * tiles)),
            pl.BlockSpec((width, TILE), lambda j: (0, j)),
            pl.BlockSpec((TILE, width), lambda j: (j, 0)),
            whole((width, rows)),
            whole((rows, width)),
        ]
        + [whole(x.shape) for x in rest],
        out_specs=grid_out + [whole(shape) for shape, _ in whole_out],
        out_shape=shapes + [jax.ShapeDtypeStruct(shape, kind) for shape, kind in whole_out],
        scratch_shapes=scratch,
        compiler_params=vmem(32),
        cost_estimate=pl.CostEstimate(
            flops=6 * rows * width * hidden,
            bytes_accessed=rows * hidden * 2 + rows * width * 18 + width * hidden * 6,
            transcendentals=0,
        ),
        name="feed_forward_back",
    )(d_f, *hbm(slope, w_in, w_down), h1_t, start, *hbm(*rest[:-1]), *rest[-1:])


def attend_back_kernel(
    ends, swap_ref, qkv_ref, ctx_t_ref, lse_ref, da_ref, x_t_ref, *refs
):
    step = pl.program_id(0)
    outs = refs[-1 - len(ends) :]
    dqkv = outs[-1]
    w_out = pick(step >= ends[-2], *refs[:2]) if len(ends) > 1 else refs[0][...]
    swap = swap_ref[...] > 0
    scale = LOG2E * HDIM**-0.5

    keys = [qkv_ref[rows, LANES : 2 * LANES] for rows in SLOTS]
    values = [qkv_ref[rows, 2 * LANES :] for rows in SLOTS]
    blocks, units = [], []
    for i, rows in enumerate(SLOTS):
        q = qkv_ref[rows, :LANES]
        k = jnp.where(swap, keys[1 - i], keys[i])
        v = jnp.where(swap, values[1 - i], values[i])
        dctx = dot(da_ref[rows, :], w_out, NT).astype(BF16)
        prod_t = dctx.T.astype(F32) * ctx_t_ref[:, rows].astype(F32)
        blocks.append((rows, q, k, v, k.T, dctx, prod_t))
    for i, (rows, q, k, v, k_t, dctx, prod_t) in enumerate(blocks):
        for n in (0, 1):
            own = head_lanes(n == 0)
            q_n = jnp.where(own, q, jnp.zeros_like(q))
            d_n = jnp.where(own, dctx, jnp.zeros_like(dctx))
            units.append((i, n, q_n, d_n))

    def products(unit):
        i, n, q_n, d_n = unit
        return dot(blocks[i][2], q_n, NT), dot(blocks[i][3], d_n, NT)

    ahead = 1
    ready = [products(unit) for unit in units[:ahead]]
    found = []
    for at, (i, n, q_n, d_n) in enumerate(units):
        if at + ahead < len(units):
            ready.append(products(units[at + ahead]))
        rows, q, k, v, k_t, dctx, prod_t = blocks[i]
        cut = slice(n * HDIM, (n + 1) * HDIM)
        s, d_p = ready[at]
        p = jnp.exp2(s * scale - lse_ref[0, n : n + 1, rows])
        inner = jnp.sum(prod_t[cut], axis=0, keepdims=True)
        ds = (p * (d_p - inner)).astype(BF16)
        dv_n = dot(p.astype(BF16), d_n)
        dk_n = dot(ds, q_n)
        if n == 0:
            dv, dk, dq_t = dv_n, dk_n, [dot(k_t[cut], ds)]
        else:
            dv, dk = dv + dv_n, dk + dk_n
            dq_t.append(dot(k_t[cut], ds))
            dq = jnp.concatenate(dq_t, axis=0).T
            dqkv[rows, :LANES] = (dq * HDIM**-0.5).astype(BF16)
            found.append(((dk * HDIM**-0.5).astype(BF16), dv.astype(BF16)))
    for i, rows in enumerate(SLOTS):
        for at in (0, 1):
            dqkv[rows, (at + 1) * LANES : (at + 2) * LANES] = jnp.where(
                swap, found[1 - i][at], found[i][at]
            )
    grad = dot(x_t_ref[...], dqkv[...]).astype(BF16)
    if len(ends) == 1:
        outs[0][0] = grad
        return
    for first, end, gw_ref in zip((0,) + ends, ends, outs):

        @pl.when(jnp.logical_and(step >= first, step < end))
        def _():
            gw_ref[0] = grad


def attention_back(ends, at, swap_lanes, qkv, ctx_t, lse, w_outs, d_a, x_t):
    rows, width = d_a.shape
    pairs = ends[-1]
    if len(ends) > 1:
        w_at = [lambda p: jnp.maximum(p - ends[-2], 0), lambda p: jnp.minimum(p, ends[-2] - 1)]
    else:
        w_at = [at]

    def w_spec(place):
        return pl.BlockSpec((LANES, width), lambda p: (place(p), 0))

    def spec(first, end):
        return pl.BlockSpec(
            (1, width, 3 * LANES), lambda p: (jnp.clip(p - first, 0, end - first - 1), 0, 0)
        )

    parts = list(zip((0,) + ends, ends))
    return pl.pallas_call(
        functools.partial(attend_back_kernel, ends),
        grid=(pairs,),
        in_specs=[
            pl.BlockSpec((1, LANES), lambda p: (0, at(p))),
            pl.BlockSpec((rows, 3 * LANES), lambda p: (0, at(p))),
            pl.BlockSpec((LANES, rows), lambda p: (at(p), 0)),
            pl.BlockSpec((1, 2, rows), lambda p: (at(p), 0, 0)),
            whole((rows, width)),
            whole((width, rows)),
        ]
        + [w_spec(place) for place in w_at],
        out_specs=[spec(*part) for part in parts]
        + [pl.BlockSpec((rows, 3 * LANES), lambda p: (0, p))],
        out_shape=[
            jax.ShapeDtypeStruct((end - first, width, 3 * LANES), BF16) for first, end in parts
        ]
        + [pltpu.HBM((rows, pairs * 3 * LANES), BF16)],
        compiler_params=vmem(24),
        cost_estimate=pl.CostEstimate(
            flops=8 * rows * width * pairs * LANES + 4 * pairs * 10 * BLOCK * BLOCK * 256,
            bytes_accessed=rows * width * 14,
            transcendentals=4 * pairs * BLOCK * BLOCK,
        ),
        name="attention_backward",
    )(swap_lanes, *hbm(qkv, ctx_t), lse, d_a, *hbm(x_t, *w_outs))


def input_kernel(first_ref, later_ref, mate_ref, wq_ref, wk_ref, wv_ref, mq_ref, mk_ref, mv_ref, start_ref,
                 kept_ref, given_ref, acc):
    step = pl.program_id(0)
    w = jnp.concatenate([wq_ref[...], wk_ref[...], wv_ref[...]], axis=1)
    m = jnp.concatenate([mq_ref[...], mk_ref[...], mv_ref[...]], axis=1)

    @pl.when(step == 0)
    def _():
        acc[...] = start_ref[...]

    for rows in SLOTS:
        own = jnp.where(step == 0, first_ref[rows, :], later_ref[rows, :])
        acc[rows, :] += dot(own, w, NT) + dot(mate_ref[rows, :], m, NT)

    @pl.when(step == pl.num_programs(0) - 1)
    def _():
        kept_ref[...] = acc[:BLOCK, :]
        given_ref[...] = acc[BLOCK:, :].astype(BF16)


def input_gradient(early, late, own_w, mate_w, start):
    rows, width = start.shape
    pairs = early.shape[1] // (3 * LANES) - 1
    part = (rows, 3 * LANES)
    w_spec = pl.BlockSpec((width, LANES), lambda p: (0, p))
    return pl.pallas_call(
        input_kernel,
        grid=(pairs,),
        in_specs=[
            pl.BlockSpec(part, lambda p: (0, pairs)),
            pl.BlockSpec(part, lambda p: (0, jnp.maximum(p - 1, 0))),
            pl.BlockSpec(part, lambda p: (0, p)),
        ]
        + [w_spec] * 6 + [whole((rows, width))],
        out_specs=[whole((BLOCK, width))] * 2,
        out_shape=[
            jax.ShapeDtypeStruct((BLOCK, width), F32), jax.ShapeDtypeStruct((BLOCK, width), BF16)
        ],
        scratch_shapes=[pltpu.VMEM((rows, width), F32)],
        compiler_params=vmem(24),
        cost_estimate=pl.CostEstimate(
            flops=12 * rows * width * pairs * LANES,
            bytes_accessed=rows * width * 14,
            transcendentals=0,
        ),
        name="input_gradient",
    )(*hbm(early, late, early, *own_w, *mate_w), start)


def halves(x, place):
    rows = x.shape[0] // 2
    return (
        lax.dynamic_slice_in_dim(x, place * rows, rows, 0),
        lax.dynamic_slice_in_dim(x, (1 - place) * rows, rows, 0),
    )


def joined(mine, other, place):
    return jnp.where(
        place == 0,
        jnp.concatenate([mine, other], axis=0),
        jnp.concatenate([other, mine], axis=0),
    )


def add_low(a, b):
    return (a.astype(F32) + b.astype(F32)).astype(BF16)


def after(x, *others):
    return lax.optimization_barrier((x, others))[0]


def spots(left, bit, value):
    low = sum(other < bit for other in left)
    count = 1 << (len(left) - 1)
    return [((n >> low) << (low + 1) | n & ((1 << low) - 1)) + (value << low) for n in range(count)]


class Streams:
    def __init__(self, refs, rows):
        self.refs, self.rows = refs, rows

    def at(self, stream, spot):
        if len(self.refs) == 2:
            return self.refs[stream].at[spot]
        first = sum(self.rows[:stream])
        return self.refs[0].at[spot, first : first + self.rows[stream]]


class TokSum:
    def __init__(self, streams, own, got, extra=None, finish=None, alone=False):
        self.size = lax.axis_size("tok")
        bits = self.size.bit_length() - 1
        self.there = [(0, 1), (1, 0)] + [(bit, bit) for bit in range(2, bits)]
        self.left = [list(reversed(range(bits)))] * 2
        self.job = 0
        self.alone = alone
        self.extra, self.finish = extra, finish
        units = [0] * len(own)
        for stream in streams:
            for n, first, rows in stream:
                units[n] = math.gcd(units[n], first, rows // self.size)
        self.items = [
            [(n, first // units[n], rows // self.size // units[n], units[n]) for n, first, rows in stream]
            for stream in streams
        ]
        self.rows = [sum(rows // self.size for _, _, rows in stream) for stream in streams]
        self.width = own[0].shape[-1]
        self.inputs = [
            x.reshape(-1, unit, self.width) for xs in (own, got) for x, unit in zip(xs, units)
        ]

    def shapes(self, count, together):
        rows = [sum(self.rows)] if together else self.rows
        return [jax.ShapeDtypeStruct((count, row, self.width), BF16) for row in rows]

    def work(self):
        steps = len(self.there)
        job, self.job = self.job, self.job + 1
        if job <= steps:
            return self.adding(job, steps)
        return self.joining(2 * steps - job)

    def adding(self, job, steps):
        inputs, rows, left = self.inputs, self.rows, self.left
        extra = self.extra if job == steps else None
        if job < steps:
            bits = self.there[job]
            together = bits[0] == bits[1]
            half = self.shapes(1 << (len(left[0]) - 1), together)
            shapes = [pltpu.VMEM(x.shape, x.dtype) for x in half] + half
            self.left = [[b for b in mine if b != bit] for mine, bit in zip(left, bits)]
        else:
            bits = None
            if extra is not None:
                self.rows = [row + x.shape[0] for row, x in zip(rows, extra)]
                inputs = inputs + list(extra)
            shapes = self.shapes(1, True)
        new_rows = self.rows
        self.sent = len(shapes) // 2 if job < steps else 0

        def body(place, ins, outs):
            if extra is not None:
                ins, extras = ins[:-2], ins[-2:]
            count = len(ins) // 2

            def sums(stream, spot):
                if job > 0:
                    found = [Streams(ins[:count], rows), Streams(ins[count:], rows)]
                    a, b = (part.at(stream, spot)[...] for part in found)
                    return [(0, rows[stream], add_low(a, b))]
                first, found = 0, []
                for n, base, count_each, unit in self.items[stream]:
                    for piece in range(count_each):
                        block = base + spot * count_each + piece
                        found.append((first, unit, add_low(ins[n][block], ins[count + n][block])))
                        first += unit
                return found

            for stream in (0, 1):
                if bits is None:
                    ref = Streams(outs, new_rows).at(stream, 0)
                    ((_, row, value),) = sums(stream, 0)
                    ref[:row, :] = value
                    if extra is not None:
                        ref[row:, :] = extras[stream][...]
                    continue
                mine = place >> bits[stream] & 1
                split = len(outs) // 2
                for which, value in ((0, mine), (1, 1 - mine)):
                    target = Streams(outs[which * split : (which + 1) * split], rows)
                    for n, spot in enumerate(spots(left[stream], bits[stream], value)):
                        ref = target.at(stream, n)
                        for first, row, total in sums(stream, spot):
                            ref[first : first + row, :] = total

        return inputs, shapes, body

    def joining(self, step):
        inputs, rows = self.inputs, self.rows
        bits = self.there[step]
        before = self.left
        self.left = left = [sorted(have + [bit], reverse=True) for have, bit in zip(before, bits)]
        self.sent = 0
        if step == 0:
            shapes, write = self.finish(rows)
        else:
            then = self.there[step - 1]
            shapes = self.shapes(1 << len(left[0]), then[0] == then[1])

        def body(place, ins, outs):
            count = len(ins) // 2
            found = [Streams(ins[:count], rows), Streams(ins[count:], rows)]
            for stream in (0, 1):
                bit = bits[stream]
                mine = place >> bit & 1
                if step == 0:
                    low = sum(other < bit for other in left[stream])
                    for spot in range(1 << len(left[stream])):
                        n = (spot >> (low + 1)) << low | spot & ((1 << low) - 1)
                        kept, new = (part.at(stream, n)[...] for part in found)
                        write(outs, stream, spot, jnp.where(mine == (spot >> low & 1), kept, new))
                    continue
                for part, value in zip(found, (mine, 1 - mine)):
                    for n, spot in enumerate(spots(left[stream], bit, value)):
                        Streams(outs, rows).at(stream, spot)[...] = part.at(stream, n)[...]

        return inputs, shapes, body

    def take(self, outs):
        steps = len(self.there)
        if self.job > 2 * steps:
            self.found = outs
            return []
        kept, sent = (outs[: self.sent], outs[self.sent :]) if self.sent else (outs, outs)
        if self.job == steps + 1 and self.alone:
            self.piece = [sent[0].reshape(sent[0].shape[1:])]
            return sent
        step = self.job - 1 if self.job <= steps else 2 * steps - self.job
        got = [swap_bit(x, "tok", bit) for x, bit in zip(sent, self.there[step])]
        self.inputs = list(kept) + got
        return sent


def gather_rest(one):
    spread = lax.all_gather(one.piece[0], "tok", axis=0)
    one.job = 2 * len(one.there) + 1
    rows = one.rows
    shapes, write = one.finish(rows)

    def kernel(x_ref, *outs):
        for spot in range(x_ref.shape[0]):
            write(outs, 0, spot, x_ref[spot, : rows[0]])
            write(outs, 1, spot, x_ref[spot, rows[0] :])

    one.found = pl.pallas_call(
        kernel,
        in_specs=[pl.BlockSpec(memory_space=pltpu.VMEM)],
        out_specs=[pl.BlockSpec(memory_space=pltpu.VMEM)] * len(shapes),
        out_shape=shapes,
        compiler_params=vmem(32),
        name="sum_spread",
    )(spread)


class PlainSum:
    def __init__(self, streams, own, got, extra=None, finish=None, alone=False):
        whole = [
            lax.psum(a.astype(F32) + b.astype(F32), "tok").reshape(-1, a.shape[-1])
            for a, b in zip(own, got)
        ]
        self.found = [
            [whole[n][first : first + rows] for n, first, rows in stream] for stream in streams
        ]


def advance(sums, *others):
    if not isinstance(sums[0], TokSum):
        return []
    place = after(lax.axis_index("tok").astype(jnp.int32).reshape(1), *others)
    works = [one.work() for one in sums]

    def kernel(place_ref, *refs):
        place = place_ref[0]
        ins = refs[: sum(len(work[0]) for work in works)]
        outs = refs[len(ins) :]
        for inputs, shapes, body in works:
            body(place, ins[: len(inputs)], outs[: len(shapes)])
            ins, outs = ins[len(inputs) :], outs[len(shapes) :]

    inputs = [x for work in works for x in work[0]]
    shapes = [x for work in works for x in work[1]]
    size = 2 * sum(math.prod(x.shape) for x in inputs + shapes)
    outs = pl.pallas_call(
        kernel,
        in_specs=[pl.BlockSpec(memory_space=pltpu.SMEM)]
        + [pl.BlockSpec(memory_space=pltpu.VMEM)] * len(inputs),
        out_specs=[pl.BlockSpec(memory_space=pltpu.VMEM)] * len(shapes),
        out_shape=shapes,
        compiler_params=vmem(20),
        cost_estimate=pl.CostEstimate(flops=size, bytes_accessed=size, transcendentals=0),
        name="sum_step",
    )(place, *inputs)
    sent = []
    for one, work in zip(sums, works):
        sent += one.take(outs[: len(work[1])])
        outs = outs[len(work[1]) :]
    return sent


def body(
    tokens,
    cotangent,
    block_source,
    mask_index,
    mask_count,
    w_query,
    w_key,
    w_value,
    w_output,
    mid_gain,
    mid_shift,
    w_inner,
    bias_inner,
    w_outer,
    bias_outer,
    end_gain,
    end_shift,
):
    tok_place = lax.axis_index("tok")
    head_place = lax.axis_index("head")
    half = tok_place % 2
    width = tokens.shape[1]

    def mate(x):
        return swap_bit(x, "head", 0)

    kept, given = halves(tokens, half)
    cot_kept, cot_given = halves(cotangent, half)
    x_got = swap_bit(given, "tok", 0)
    own_w = (w_query, w_key, w_value)
    mate_w = tuple(mate(w) for w in own_w)
    mate_out = mate(w_output)
    mate_in = mate(w_inner)
    own_bias = bias_inner[None, :]
    mate_bias = mate(own_bias)

    sequence = tok_place // 2 * PAIR_SEQS + 2 * head_place + half
    source = lax.dynamic_slice_in_dim(block_source, sequence, 1, 0)[0, :, 0]
    per_half = GROUPS // 2
    flags = jnp.concatenate(
        [
            lax.dynamic_slice_in_dim(source, head_place * per_half, per_half, 0),
            lax.dynamic_slice_in_dim(source, (1 - head_place) * per_half, per_half, 0),
        ]
    )
    swap_lanes = jnp.repeat(flags, HEADS // GROUPS * HDIM)[None, :]
    positions = lax.dynamic_slice_in_dim(mask_index, sequence, 1, 0)[0]
    count = lax.dynamic_slice_in_dim(mask_count, sequence, 1, 0)[0]
    within = jnp.arange(BLOCK)
    places = jnp.concatenate([half * BLOCK + within, (1 - half) * BLOCK + within])
    live = jnp.arange(positions.shape[0]) < count
    hits = jnp.any((positions[None, :] == places[:, None]) & live[None, :], axis=1)
    weight = (1.0 + 3.0 * hits.astype(F32))[:, None]
    params = jnp.stack(
        [mid_gain, mid_shift, bias_outer, end_gain, end_shift] + [jnp.zeros_like(mid_gain)] * 3
    )
    mate_down = mate(after(w_outer, weight, swap_lanes, cot_given, params))

    qkv, lse, ctx_t, x_t, mid_n, mid_rate = attention(
        swap_lanes, (kept, after(x_got, swap_lanes, weight, params, cot_kept)), own_w, mate_w,
        w_output, mate_out,
    )
    cot_got = swap_bit(after(cot_given, x_got), "tok", 0)
    act_t, slope, h1_t, out, d_s2, d_f, end_vec, g_mate = ffn(
        mid_n, params, w_inner, mate_in, own_bias, mate_bias, w_outer, mate_down,
        (cot_kept, cot_got), weight,
    )

    hidden = w_inner.shape[1]
    cut = w_output.shape[0]
    pairs = cut // LANES

    def side_by_side(g):
        return jnp.concatenate([g[:, n : n + COLS] for n in range(0, width, COLS)], axis=0)

    rest = width // 2

    def finish_down(rows):
        def write(outs, stream, spot, value):
            outs[0][stream, spot] = value.astype(F32)

        return [jax.ShapeDtypeStruct((2, lax.axis_size("tok"), rows[0], width), F32)], write

    def finish_inner(rows):
        size = lax.axis_size("tok")

        def write(outs, stream, spot, value):
            value = value.astype(F32)
            outs[0][spot, :, stream * width : (stream + 1) * width] = value[: rows[0]]
            if stream == 1:
                outs[1][spot] = value[rows[0] :]

        return [
            jax.ShapeDtypeStruct((size, rows[0], 2 * width), F32),
            jax.ShapeDtypeStruct((size, rows[1] - rows[0], width), F32),
        ], write

    size = lax.axis_size("tok")
    fits = size & (size - 1) == 0 and size >= 4 and rest % (8 * size) == 0
    Sum = TokSum if fits else PlainSum

    got = mate(g_mate)
    mine = product(act_t, 0, hidden, d_f, BLOCK)
    cut = hidden // 2
    down = Sum([[(0, 0, cut)], [(0, cut, cut)]], [mine], [got], finish=finish_down, alone=False)
    sent = advance([down], mine)
    gi_mate, gb_mate, d_h1 = ffn_back(
        1, after(d_f, sent), slope, mate_in, mate_down, h1_t, d_s2
    )
    sent = advance([down], gi_mate)
    out_got = swap_bit(after(out[BLOCK:], sent), "tok", 0)
    got_in = mate(after(gi_mate, sent))
    gi_own, gb_own, go_own, go_mate, d_s1, d_a, mid_vec = ffn_back(
        0, after(d_f, sent), slope, w_inner, w_outer, h1_t, d_h1, mid_n, mid_rate, ctx_t, params
    )
    got_out = mate(after(go_mate, down.inputs[-2:], out_got) if fits else go_mate)
    inner = Sum(
        [[(0, 0, width)], [(0, width, width), (1, 0, rest)]],
        [gi_own, go_own], [got_in, got_out], finish=finish_inner, alone=False,
    )
    sent = advance([inner, down], gi_own)
    gw_mate, gw_mates, gw_own, dp_early = attention_back(
        (1, pairs, pairs + 1), lambda p: jnp.where(p < pairs, p + pairs, 0), swap_lanes, qkv, ctx_t,
        lse, (w_output, mate_out), after(d_a, sent), x_t,
    )
    sent = advance([inner, down], gw_own)
    gw_got, gw_gots = (mate(x) for x in after((gw_mate, gw_mates), sent))

    gb_own, gb_mate = gb_own.reshape(-1, width), gb_mate.reshape(-1, width)
    own_rows = gb_own.shape[0]
    small = jnp.concatenate([end_vec[:3], mid_vec[:2], gb_own, gb_mate], axis=0)
    theirs = mate(small)
    small = jnp.concatenate(
        [
            small[:5] + theirs[:5],
            small[5 : 5 + own_rows] + theirs[5 + own_rows :],
            jnp.zeros((1, width), F32),
        ],
        axis=0,
    )
    high = small.astype(BF16)
    low = (small - high.astype(F32)).astype(BF16)
    high, low = side_by_side(high), side_by_side(low)

    gw_owns, dp_late = attention_back(
        (pairs - 1,), lambda p: p + 1, swap_lanes, qkv, ctx_t, lse, (w_output,), after(d_a, sent), x_t
    )
    head = (pairs * width // size + 31) // 32 * 16 * size - width

    def finish_last(rows):
        def write(outs, stream, spot, value):
            value = value.astype(F32)
            extra = high.shape[0]
            count = rows[stream] - extra
            pieces = [(0, spot * count + width + head, count)]
            if stream == 0:
                one = width // size
                pieces = [(0, spot * one, one), (one, width + spot * (count - one), count - one)]
            for done, first, length in pieces:
                while length > 0:
                    p, row = divmod(first, width)
                    step = min(length, width - row)
                    for at in range(3):
                        outs[at][row : row + step, p * LANES : (p + 1) * LANES] = value[
                            done : done + step, at * LANES : (at + 1) * LANES
                        ]
                    done, first, length = done + step, first + step, length - step
            if stream == 0 and spot == 0:
                outs[3][...] = value[count:]
            else:
                outs[3][...] += value[count:]

        return [jax.ShapeDtypeStruct((width, pairs * LANES), F32)] * 3 + [
            jax.ShapeDtypeStruct(high.shape, F32)
        ], write

    rows = (pairs - 1) * width
    last = Sum(
        [[(0, 0, width), (1, 0, head)], [(1, head, rows - head)]],
        [x.reshape(-1, 3 * LANES) for x in (gw_own, gw_owns)],
        [x.reshape(-1, 3 * LANES) for x in (gw_got, gw_gots)],
        extra=(high, low), finish=finish_last,
    )
    sent = advance([last, inner, down], gw_owns)
    out = joined(out[:BLOCK], out_got, half)
    dx_kept, dx_given = input_gradient(dp_early, after(dp_late, sent), own_w, mate_w, d_s1)
    dx_got = []
    if fits:
        while last.job <= 2 * len(last.there):
            for one in (inner, down):
                if one.alone and one.job == len(one.there) + 1:
                    gather_rest(one)
            sums = [one for one in (last, inner, down) if one.job <= 2 * len(one.there)]
            others = [dx_given] if last.job == 1 else []
            if last.job in (2, 3):
                first = (last.job - 2) * (BLOCK // 2)
                part = dx_given[first : first + BLOCK // 2]
                others = [swap_bit(after(part, last.inputs[0]), "tok", 0)]
                dx_got += others
            advance(sums, *others)
        g_down, (g_in, g_out), (g_query, g_key, g_value, sums) = (
            down.found[0], inner.found, last.found
        )
        small = jnp.concatenate([sums[: small.shape[0]], sums[small.shape[0] :]], axis=1)
    else:
        dx_got = [swap_bit(dx_given, "tok", 0)]
        g_down = jnp.concatenate([down.found[0][0], down.found[1][0]], axis=0)
        g_in = jnp.concatenate([inner.found[0][0], inner.found[1][0]], axis=1)
        g_out = inner.found[1][1]
        whole_w = jnp.concatenate(last.found[0] + last.found[1], axis=0)
        whole_w = whole_w.reshape(pairs, width, 3, LANES)
        g_query, g_key, g_value = (
            jnp.concatenate([whole_w[p, :, at] for p in range(pairs)], axis=1) for at in range(3)
        )
        small = lax.psum(small, "tok")
    dx_got = jnp.concatenate(dx_got, axis=0).astype(F32)
    grad_tokens = joined(dx_kept, dx_got, half)
    g_down = g_down.reshape(hidden, width)
    g_in = g_in.reshape(width, hidden)
    g_out = g_out.reshape(rest, width)

    return (
        out,
        grad_tokens,
        g_query,
        g_key,
        g_value,
        g_out,
        small[4],
        small[3],
        g_in,
        small[5 : 5 + own_rows].reshape(-1),
        g_down,
        small[2],
        small[1],
        small[0],
    )


def solution(mesh):
    rows = P(("tok", "head"), None)
    return jax.shard_map(
        body,
        mesh=mesh,
        in_specs=(
            rows,
            rows,
            P(),
            P(),
            P(),
            P(None, "head"),
            P(None, "head"),
            P(None, "head"),
            P("head", None),
            P(),
            P(),
            P(None, "head"),
            P("head"),
            P("head", None),
            P(),
            P(),
            P(),
        ),
        out_specs=(
            rows,
            rows,
            P(None, "head"),
            P(None, "head"),
            P(None, "head"),
            P("head", None),
            P(),
            P(),
            P(None, "head"),
            P("head"),
            P("head", None),
            P(),
            P(),
            P(),
        ),
        check_vma=False,
    )
```

```python
import functools
import math

import jax
import jax.numpy as jnp
from jax import lax
from jax.experimental import pallas as pl
from jax.experimental.pallas import tpu as pltpu
from jax.sharding import PartitionSpec as P

HEADS = 12
HDIM = 64
GROUPS = 4
BLOCK = 512
PAIR_SEQS = 4
LANES = 128

NORM_EPS = 1e-05
LOG2E = 1.4426950408889634
BF16 = jnp.bfloat16
F32 = jnp.float32


def swap_bit(x, axis, bit):
    return lax.ppermute(x, axis, [(i, i ^ 1 << bit) for i in range(lax.axis_size(axis))])


def dot(a, b, dims=((1,), (0,))):
    return lax.dot_general(a, b, (dims, ((), ())), preferred_element_type=F32)


NT = ((1,), (1,))
TN = ((0,), (0,))


def head_lanes(first):
    lane = lax.broadcasted_iota(jnp.int32, (1, LANES), 1)
    return (lane < HDIM) if first else (lane >= HDIM)


def vmem(limit=56):
    return pltpu.CompilerParams(vmem_limit_bytes=limit * 1024 * 1024)


def whole(shape):
    return pl.BlockSpec(shape, lambda *_: (0,) * len(shape), pipeline_mode=pl.Buffered(1))


def hbm(*arrays):
    return [pltpu.with_memory_space_constraint(x, pltpu.HBM) for x in arrays]


def pick(own, w_own_ref, w_mate_ref):
    return jnp.where(own, w_own_ref[...], w_mate_ref[...])


def normalize(summed):
    center = summed - jnp.mean(summed, axis=-1, keepdims=True)
    rate = lax.rsqrt(jnp.mean(center * center, axis=-1, keepdims=True) + NORM_EPS)
    return center * rate, rate


def norm_back(grad, normed, rate, gain):
    scaled = grad * gain
    return rate * (
        scaled
        - jnp.mean(scaled, axis=-1, keepdims=True)
        - normed * jnp.mean(scaled * normed, axis=-1, keepdims=True)
    )


def gelu_parts(u):
    size = jnp.abs(u)
    bell = jnp.exp2(u * u * (-0.5 * LOG2E))
    t = 1.0 / (1.0 + (0.3275911 * 0.5**0.5) * size)
    poly = t * (
        0.5 * 0.254829592
        + t
        * (
            0.5 * -0.284496736
            + t * (0.5 * 1.421413741 + t * (0.5 * -1.453152027 + t * (0.5 * 1.061405429)))
        )
    )
    tail = poly * bell
    phi = jnp.where(u > 0, 1.0 - tail, tail)
    return u * phi, phi + u * (bell * 0.3989422804014327)


SLOTS = (slice(0, BLOCK), slice(BLOCK, 2 * BLOCK))


def attend_kernel(
    pairs, swap_ref, xa_ref, xb_ref, wq_ref, wk_ref, wv_ref, mq_ref, mk_ref, mv_ref, wo_ref, mo_ref,
    qkv_ref, lse_ref, ctx_t_ref, x_t_ref, mid_n_ref, rate_ref, ctx_all,
):
    step = pl.program_id(0)
    own = step < pairs // 2
    swap = swap_ref[...] > 0
    scale = LOG2E * HDIM**-0.5
    ones = jnp.ones((16, BLOCK), BF16)
    w = jnp.concatenate(
        [pick(own, wq_ref, mq_ref), pick(own, wk_ref, mk_ref), pick(own, wv_ref, mv_ref)], axis=1
    )
    for rows, x_ref in zip(SLOTS, (xa_ref, xb_ref)):
        qkv_ref[rows, :] = dot(x_ref[...], w).astype(BF16)
    keys = [qkv_ref[rows, LANES : 2 * LANES] for rows in SLOTS]
    values = [qkv_ref[rows, 2 * LANES :] for rows in SLOTS]
    units = []
    for i, rows in enumerate(SLOTS):
        q = qkv_ref[rows, :LANES]
        k = jnp.where(swap, keys[1 - i], keys[i])
        v_t = jnp.where(swap, values[1 - i], values[i]).T
        for n in (0, 1):
            q_n = jnp.where(head_lanes(n == 0), q, jnp.zeros_like(q))
            units.append((rows, n, v_t, dot(k, q_n, NT)))
    parts = []
    for rows, n, v_t, s in units:
        top = jnp.max(s, axis=0, keepdims=True)
        p = jnp.exp2((s - top) * scale).astype(BF16)
        v_n = jnp.concatenate([v_t[n * HDIM : (n + 1) * HDIM], ones], axis=0)
        acc = dot(v_n, p)
        total = acc[HDIM : HDIM + 1]
        parts.append(acc[:HDIM] / total)
        lse_ref[0, n : n + 1, rows] = top * scale + jnp.log2(total)
        if n == 1:
            ctx_t = jnp.concatenate(parts, axis=0)
            parts = []
            ctx_t_ref[:, rows] = ctx_t.astype(BF16)
            ctx_all[step, rows, :] = ctx_t.T.astype(BF16)

    cols = pl.ds(pl.multiple_of(step * LANES, LANES), LANES)
    for rows, x_ref in zip(SLOTS, (xa_ref, xb_ref)):
        x_t_ref[:, rows] = x_ref[:, cols].T

    @pl.when(step == pairs - 1)
    def _():
        for rows, x_ref in zip(SLOTS, (xa_ref, xb_ref)):
            total = x_ref[...].astype(F32)
            every = jnp.concatenate([ctx_all[p, rows, :] for p in range(pairs)], axis=1)
            cut = wo_ref.shape[0]
            total = total + dot(every[:, :cut], wo_ref[...]) + dot(every[:, cut:], mo_ref[...])
            normed, rate = normalize(total)
            mid_n_ref[rows, :] = normed
            rate_ref[rows, :] = rate


def attention(swap_lanes, blocks, own_w, mate_w, own_out, mate_out):
    width = blocks[0].shape[1]
    rows = 2 * BLOCK
    pairs = width // LANES
    per = own_w[0].shape[1] // LANES
    own_spec = pl.BlockSpec((width, LANES), lambda p: (0, jnp.minimum(p, per - 1)))
    mate_spec = pl.BlockSpec((width, LANES), lambda p: (0, jnp.maximum(p - per, 0)))
    return pl.pallas_call(
        functools.partial(attend_kernel, pairs),
        grid=(pairs,),
        in_specs=[pl.BlockSpec((1, LANES), lambda p: (0, p))]
        + [whole((BLOCK, width))] * 2
        + [own_spec] * 3
        + [mate_spec] * 3
        + [whole(own_out.shape)] * 2,
        out_specs=[
            pl.BlockSpec((rows, 3 * LANES), lambda p: (0, p)),
            pl.BlockSpec((1, 2, rows), lambda p: (p, 0, 0)),
            pl.BlockSpec((LANES, rows), lambda p: (p, 0)),
            pl.BlockSpec((LANES, rows), lambda p: (p, 0)),
            whole((rows, width)),
            whole((rows, 1)),
        ],
        out_shape=[
            pltpu.HBM((rows, 3 * width), BF16),
            jax.ShapeDtypeStruct((pairs, 2, rows), F32),
            pltpu.HBM((width, rows), BF16),
            pltpu.HBM((width, rows), BF16),
            pltpu.HBM((rows, width), F32),
            pltpu.HBM((rows, 1), F32),
        ],
        scratch_shapes=[pltpu.VMEM((pairs, rows, LANES), BF16)],
        compiler_params=vmem(28),
        cost_estimate=pl.CostEstimate(
            flops=2 * rows * width * width * 4 + 4 * pairs * 4 * BLOCK * BLOCK * 256,
            bytes_accessed=rows * width * 18 + width * width * 8,
            transcendentals=4 * pairs * BLOCK * BLOCK,
        ),
        name="attention_forward",
    )(swap_lanes, *blocks, *hbm(*own_w, *mate_w, own_out, mate_out))


def ffn_kernel(
    tiles, mid_n_ref, par_ref, wi_ref, mi_ref, bi_ref, mbi_ref, wd_ref, md_ref, ca_ref, cb_ref, wt_ref,
    act_t_ref, slope_ref, h1_t_ref, kept_ref, first_ref, rest_ref, ds2_ref, df_ref, vec_ref, gm_ref,
    h1_low, acc, act_m,
):
    step = pl.program_id(0)
    own = step < tiles // 2

    @pl.when(step == 0)
    def _():
        for rows in SLOTS:
            h1 = mid_n_ref[rows, :] * par_ref[0:1, :] + par_ref[1:2, :]
            low = h1.astype(BF16)
            h1_low[rows, :] = low
            h1_t_ref[:, rows] = low.T
            acc[rows, :] = h1 + par_ref[2:3, :]

    size = 256

    def tile(w_in, w_down, bias, act_ref):
        cuts = [slice(at, at + size) for at in range(0, 2 * BLOCK, size)]
        ready = [dot(h1_low[cuts[0], :], w_in)]
        for at, rows in enumerate(cuts):
            if at + 1 < len(cuts):
                ready.append(dot(h1_low[cuts[at + 1], :], w_in))
            value, slope = gelu_parts(ready[at] + bias)
            low = value.astype(BF16)
            slope_ref[rows, :] = slope.astype(BF16)
            act_ref[:, rows] = low.T
            acc[rows, :] += dot(low, w_down)

    @pl.when(own)
    def _():
        tile(wi_ref[...], wd_ref[...], bi_ref[...], act_t_ref)

    @pl.when(jnp.logical_and(step >= tiles // 2, step < tiles))
    def _():
        tile(mi_ref[...], md_ref[...], mbi_ref[...], act_m.at[step - tiles // 2])

    @pl.when(step >= tiles)
    def _():
        gm_ref[...] = dot(act_m[step - tiles], df_ref[...]).astype(BF16)

    @pl.when(step == tiles - 1)
    def _():
        gain = par_ref[3:4, :]
        sums = [0.0, 0.0, 0.0]
        for at in range(0, 2 * BLOCK, size):
            rows = slice(at, at + size)
            normed, rate = normalize(acc[rows, :])
            out = (normed * gain + par_ref[4:5, :]).astype(BF16)
            if at < BLOCK:
                kept_ref[rows, :] = out
            else:
                (first_ref if at == BLOCK else rest_ref)[...] = out
            cot_ref, first = (ca_ref, at) if at < BLOCK else (cb_ref, at - BLOCK)
            d_y = cot_ref[first : first + size, :].astype(F32) * wt_ref[rows, :]
            d_s2 = norm_back(d_y, normed, rate, gain)
            ds2_ref[rows, :] = d_s2
            df_ref[rows, :] = d_s2.astype(BF16)
            for n, term in enumerate((d_y, d_y * normed, d_s2)):
                sums[n] = sums[n] + jnp.sum(term, axis=0, keepdims=True)
        vec_ref[...] = jnp.concatenate(sums + [jnp.zeros((5, gain.shape[1]), F32)], axis=0)


TILE = 768
COLS = 384


def ffn(mid_n, params, own_in, mate_in, own_bias, mate_bias, own_down, mate_down, cot, weight):
    rows, width = mid_n.shape
    per = own_in.shape[1] // TILE
    tiles = 2 * per

    def own_at(j):
        return jnp.minimum(j, per - 1)

    def mate_at(j):
        return jnp.clip(j - per, 0, per - 1)

    hidden = 2 * own_in.shape[1]
    return pl.pallas_call(
        functools.partial(ffn_kernel, tiles),
        grid=(tiles + per,),
        in_specs=[
            whole((rows, width)),
            whole(params.shape),
            pl.BlockSpec((width, TILE), lambda j: (0, own_at(j))),
            pl.BlockSpec((width, TILE), lambda j: (0, mate_at(j))),
            pl.BlockSpec((1, TILE), lambda j: (0, own_at(j))),
            pl.BlockSpec((1, TILE), lambda j: (0, mate_at(j))),
            pl.BlockSpec((TILE, width), lambda j: (own_at(j), 0)),
            pl.BlockSpec((TILE, width), lambda j: (mate_at(j), 0)),
            whole((BLOCK, width)),
            whole((BLOCK, width)),
            whole((rows, 1)),
        ],
        out_specs=[
            pl.BlockSpec((TILE, rows), lambda j: (own_at(j), 0)),
            pl.BlockSpec((rows, TILE), lambda j: (0, jnp.minimum(j, tiles - 1))),
            whole((width, rows)),
            whole((BLOCK, width)),
            whole((BLOCK // 2, width)),
            whole((BLOCK // 2, width)),
            whole((rows, width)),
            whole((rows, width)),
            whole((8, width)),
            pl.BlockSpec((TILE, width), lambda j: (jnp.maximum(j - tiles, 0), 0)),
        ],
        out_shape=[
            jax.ShapeDtypeStruct((hidden // 2, rows), BF16),
            pltpu.HBM((rows, hidden), BF16),
            jax.ShapeDtypeStruct((width, rows), BF16),
            jax.ShapeDtypeStruct((BLOCK, width), BF16),
            jax.ShapeDtypeStruct((BLOCK // 2, width), BF16),
            jax.ShapeDtypeStruct((BLOCK // 2, width), BF16),
            jax.ShapeDtypeStruct((rows, width), F32),
            jax.ShapeDtypeStruct((rows, width), BF16),
            jax.ShapeDtypeStruct((8, width), F32),
            jax.ShapeDtypeStruct((hidden // 2, width), BF16),
        ],
        scratch_shapes=[
            pltpu.VMEM((rows, width), BF16),
            pltpu.VMEM((rows, width), F32),
            pltpu.VMEM((per, TILE, rows), BF16),
        ],
        compiler_params=vmem(40),
        cost_estimate=pl.CostEstimate(
            flops=4 * rows * width * hidden,
            bytes_accessed=rows * hidden * 4 + rows * width * 16 + width * hidden * 4,
            transcendentals=rows * hidden * 2,
        ),
        name="feed_forward",
    )(
        *hbm(mid_n), params, *hbm(own_in, mate_in), own_bias, mate_bias,
        *hbm(own_down, mate_down), *cot, weight,
    )


def product_kernel(a_ref, b_ref, c_ref):
    c_ref[...] = dot(a_ref[...], b_ref[...]).astype(BF16)


def product(a, first, rows, b, block):
    return pl.pallas_call(
        product_kernel,
        grid=(rows // block,),
        in_specs=[pl.BlockSpec((block, a.shape[1]), lambda j: (j + first // block, 0)), whole(b.shape)],
        out_specs=pl.BlockSpec((block, b.shape[1]), lambda j: (j, 0)),
        out_shape=jax.ShapeDtypeStruct((rows, b.shape[1]), BF16),
        compiler_params=vmem(12),
        cost_estimate=pl.CostEstimate(
            flops=2 * rows * a.shape[1] * b.shape[1],
            bytes_accessed=2 * (rows * (a.shape[1] + b.shape[1]) + b.shape[0] * b.shape[1]),
            transcendentals=0,
        ),
        name="weight_gradient",
    )(a, b)


def ffn_back_kernel(
    last, df_ref, slope_ref, wi_ref, wd_ref, h1_t_ref, start_ref, *refs
):
    if last:
        (mid_n_ref, rate_ref, ctx_t_ref, par_ref, gin_ref, db_ref, gown_ref, gmate_ref, ds1_ref,
         da_ref, vec_ref, du, acc) = refs
    else:
        gin_ref, db_ref, acc, du = refs
    step = pl.program_id(0)
    w_in = wi_ref[...]
    w_down = wd_ref[...]

    @pl.when(step == 0)
    def _():
        acc[...] = start_ref[...]

    size = 256
    total = 0.0
    cuts = [slice(at, at + size) for at in range(0, 2 * BLOCK, size)]
    ready = [dot(df_ref[cuts[0], :], w_down, NT)]
    for at, rows in enumerate(cuts):
        if at + 1 < len(cuts):
            ready.append(dot(df_ref[cuts[at + 1], :], w_down, NT))
        d_u = ready[at] * slope_ref[rows, :].astype(F32)
        total = total + jnp.sum(d_u, axis=0, keepdims=True)
        low = d_u.astype(BF16)
        du[rows, :] = low
        acc[rows, :] += dot(low, w_in, NT)
    db_ref[...] = total
    gin_ref[0] = dot(h1_t_ref[...], du[...]).astype(BF16)
    if not last:
        return

    @pl.when(step == pl.num_programs(0) - 1)
    def _():
        sums = [0.0, 0.0]
        gain = par_ref[0:1, :]
        for at in range(0, 2 * BLOCK, size):
            rows = slice(at, at + size)
            d_h1 = acc[rows, :]
            normed = mid_n_ref[rows, :]
            d_s1 = norm_back(d_h1, normed, rate_ref[rows, :], gain)
            ds1_ref[rows, :] = d_s1
            da_ref[rows, :] = d_s1.astype(BF16)
            for n, term in enumerate((d_h1, d_h1 * normed)):
                sums[n] = sums[n] + jnp.sum(term, axis=0, keepdims=True)
        vec_ref[...] = jnp.concatenate(sums + [jnp.zeros((6, gain.shape[1]), F32)], axis=0)
        cut = gown_ref.shape[0]
        gown_ref[...] = dot(ctx_t_ref[:cut, :], da_ref[...]).astype(BF16)
        gmate_ref[...] = dot(ctx_t_ref[cut:, :], da_ref[...]).astype(BF16)


def ffn_back(first, d_f, slope, w_in, w_down, h1_t, start, *rest):
    rows, width = d_f.shape
    hidden = w_in.shape[1]
    tiles = hidden // TILE
    last = len(rest) > 0
    grid_out = [
        pl.BlockSpec((1, width, TILE), lambda j: (j, 0, 0)),
        pl.BlockSpec((1, TILE), lambda j: (0, j)),
    ]
    shapes = [
        jax.ShapeDtypeStruct((tiles, width, TILE), BF16),
        jax.ShapeDtypeStruct((1, hidden), F32),
    ]
    scratch = [pltpu.VMEM((rows, TILE), BF16)]
    if last:
        whole_out = [((width // 2, width), BF16)] * 2 + [
            ((rows, width), F32), ((rows, width), BF16), ((8, width), F32)
        ]
        scratch.append(pltpu.VMEM((rows, width), F32))
    else:
        whole_out = [((rows, width), F32)]
    return pl.pallas_call(
        functools.partial(ffn_back_kernel, last),
        grid=(tiles,),
        in_specs=[
            whole((rows, width)),
            pl.BlockSpec((rows, TILE), lambda j: (0, j + first * tiles)),
            pl.BlockSpec((width, TILE), lambda j: (0, j)),
            pl.BlockSpec((TILE, width), lambda j: (j, 0)),
            whole((width, rows)),
            whole((rows, width)),
        ]
        + [whole(x.shape) for x in rest],
        out_specs=grid_out + [whole(shape) for shape, _ in whole_out],
        out_shape=shapes + [jax.ShapeDtypeStruct(shape, kind) for shape, kind in whole_out],
        scratch_shapes=scratch,
        compiler_params=vmem(32),
        cost_estimate=pl.CostEstimate(
            flops=6 * rows * width * hidden,
            bytes_accessed=rows * hidden * 2 + rows * width * 18 + width * hidden * 6,
            transcendentals=0,
        ),
        name="feed_forward_back",
    )(d_f, *hbm(slope, w_in, w_down), h1_t, start, *hbm(*rest[:-1]), *rest[-1:])


def attend_back_kernel(
    ends, swap_ref, qkv_ref, ctx_t_ref, lse_ref, da_ref, x_t_ref, *refs
):
    step = pl.program_id(0)
    outs = refs[-1 - len(ends) :]
    dqkv = outs[-1]
    w_out = pick(step >= ends[-2], *refs[:2]) if len(ends) > 1 else refs[0][...]
    swap = swap_ref[...] > 0
    scale = LOG2E * HDIM**-0.5

    keys = [qkv_ref[rows, LANES : 2 * LANES] for rows in SLOTS]
    values = [qkv_ref[rows, 2 * LANES :] for rows in SLOTS]
    blocks, units = [], []
    for i, rows in enumerate(SLOTS):
        q = qkv_ref[rows, :LANES]
        k = jnp.where(swap, keys[1 - i], keys[i])
        v = jnp.where(swap, values[1 - i], values[i])
        dctx = dot(da_ref[rows, :], w_out, NT).astype(BF16)
        prod_t = dctx.T.astype(F32) * ctx_t_ref[:, rows].astype(F32)
        blocks.append((rows, q, k, v, k.T, dctx, prod_t))
    for i, (rows, q, k, v, k_t, dctx, prod_t) in enumerate(blocks):
        for n in (0, 1):
            own = head_lanes(n == 0)
            q_n = jnp.where(own, q, jnp.zeros_like(q))
            d_n = jnp.where(own, dctx, jnp.zeros_like(dctx))
            units.append((i, n, q_n, d_n))

    def products(unit):
        i, n, q_n, d_n = unit
        return dot(blocks[i][2], q_n, NT), dot(blocks[i][3], d_n, NT)

    ahead = 1
    ready = [products(unit) for unit in units[:ahead]]
    found = []
    for at, (i, n, q_n, d_n) in enumerate(units):
        if at + ahead < len(units):
            ready.append(products(units[at + ahead]))
        rows, q, k, v, k_t, dctx, prod_t = blocks[i]
        cut = slice(n * HDIM, (n + 1) * HDIM)
        s, d_p = ready[at]
        p = jnp.exp2(s * scale - lse_ref[0, n : n + 1, rows])
        inner = jnp.sum(prod_t[cut], axis=0, keepdims=True)
        ds = (p * (d_p - inner)).astype(BF16)
        dv_n = dot(p.astype(BF16), d_n)
        dk_n = dot(ds, q_n)
        if n == 0:
            dv, dk, dq_t = dv_n, dk_n, [dot(k_t[cut], ds)]
        else:
            dv, dk = dv + dv_n, dk + dk_n
            dq_t.append(dot(k_t[cut], ds))
            dq = jnp.concatenate(dq_t, axis=0).T
            dqkv[rows, :LANES] = (dq * HDIM**-0.5).astype(BF16)
            found.append(((dk * HDIM**-0.5).astype(BF16), dv.astype(BF16)))
    for i, rows in enumerate(SLOTS):
        for at in (0, 1):
            dqkv[rows, (at + 1) * LANES : (at + 2) * LANES] = jnp.where(
                swap, found[1 - i][at], found[i][at]
            )
    grad = dot(x_t_ref[...], dqkv[...]).astype(BF16)
    if len(ends) == 1:
        outs[0][0] = grad
        return
    for first, end, gw_ref in zip((0,) + ends, ends, outs):

        @pl.when(jnp.logical_and(step >= first, step < end))
        def _():
            gw_ref[0] = grad


def attention_back(ends, at, swap_lanes, qkv, ctx_t, lse, w_outs, d_a, x_t):
    rows, width = d_a.shape
    pairs = ends[-1]
    if len(ends) > 1:
        w_at = [lambda p: jnp.maximum(p - ends[-2], 0), lambda p: jnp.minimum(p, ends[-2] - 1)]
    else:
        w_at = [at]

    def w_spec(place):
        return pl.BlockSpec((LANES, width), lambda p: (place(p), 0))

    def spec(first, end):
        return pl.BlockSpec(
            (1, width, 3 * LANES), lambda p: (jnp.clip(p - first, 0, end - first - 1), 0, 0)
        )

    parts = list(zip((0,) + ends, ends))
    return pl.pallas_call(
        functools.partial(attend_back_kernel, ends),
        grid=(pairs,),
        in_specs=[
            pl.BlockSpec((1, LANES), lambda p: (0, at(p))),
            pl.BlockSpec((rows, 3 * LANES), lambda p: (0, at(p))),
            pl.BlockSpec((LANES, rows), lambda p: (at(p), 0)),
            pl.BlockSpec((1, 2, rows), lambda p: (at(p), 0, 0)),
            whole((rows, width)),
            whole((width, rows)),
        ]
        + [w_spec(place) for place in w_at],
        out_specs=[spec(*part) for part in parts]
        + [pl.BlockSpec((rows, 3 * LANES), lambda p: (0, p))],
        out_shape=[
            jax.ShapeDtypeStruct((end - first, width, 3 * LANES), BF16) for first, end in parts
        ]
        + [pltpu.HBM((rows, pairs * 3 * LANES), BF16)],
        compiler_params=vmem(24),
        cost_estimate=pl.CostEstimate(
            flops=8 * rows * width * pairs * LANES + 4 * pairs * 10 * BLOCK * BLOCK * 256,
            bytes_accessed=rows * width * 14,
            transcendentals=4 * pairs * BLOCK * BLOCK,
        ),
        name="attention_backward",
    )(swap_lanes, *hbm(qkv, ctx_t), lse, d_a, *hbm(x_t, *w_outs))


def input_kernel(first_ref, later_ref, mate_ref, wq_ref, wk_ref, wv_ref, mq_ref, mk_ref, mv_ref, start_ref,
                 kept_ref, given_ref, acc):
    step = pl.program_id(0)
    w = jnp.concatenate([wq_ref[...], wk_ref[...], wv_ref[...]], axis=1)
    m = jnp.concatenate([mq_ref[...], mk_ref[...], mv_ref[...]], axis=1)

    @pl.when(step == 0)
    def _():
        acc[...] = start_ref[...]

    for rows in SLOTS:
        own = jnp.where(step == 0, first_ref[rows, :], later_ref[rows, :])
        acc[rows, :] += dot(own, w, NT) + dot(mate_ref[rows, :], m, NT)

    @pl.when(step == pl.num_programs(0) - 1)
    def _():
        kept_ref[...] = acc[:BLOCK, :]
        given_ref[...] = acc[BLOCK:, :].astype(BF16)


def input_gradient(early, late, own_w, mate_w, start):
    rows, width = start.shape
    pairs = early.shape[1] // (3 * LANES) - 1
    part = (rows, 3 * LANES)
    w_spec = pl.BlockSpec((width, LANES), lambda p: (0, p))
    return pl.pallas_call(
        input_kernel,
        grid=(pairs,),
        in_specs=[
            pl.BlockSpec(part, lambda p: (0, pairs)),
            pl.BlockSpec(part, lambda p: (0, jnp.maximum(p - 1, 0))),
            pl.BlockSpec(part, lambda p: (0, p)),
        ]
        + [w_spec] * 6 + [whole((rows, width))],
        out_specs=[whole((BLOCK, width))] * 2,
        out_shape=[
            jax.ShapeDtypeStruct((BLOCK, width), F32), jax.ShapeDtypeStruct((BLOCK, width), BF16)
        ],
        scratch_shapes=[pltpu.VMEM((rows, width), F32)],
        compiler_params=vmem(24),
        cost_estimate=pl.CostEstimate(
            flops=12 * rows * width * pairs * LANES,
            bytes_accessed=rows * width * 14,
            transcendentals=0,
        ),
        name="input_gradient",
    )(*hbm(early, late, early, *own_w, *mate_w), start)


def halves(x, place):
    rows = x.shape[0] // 2
    return (
        lax.dynamic_slice_in_dim(x, place * rows, rows, 0),
        lax.dynamic_slice_in_dim(x, (1 - place) * rows, rows, 0),
    )


def joined(mine, other, place):
    return jnp.where(
        place == 0,
        jnp.concatenate([mine, other], axis=0),
        jnp.concatenate([other, mine], axis=0),
    )


def add_low(a, b):
    return (a.astype(F32) + b.astype(F32)).astype(BF16)


def after(x, *others):
    return lax.optimization_barrier((x, others))[0]


def spots(left, bit, value):
    low = sum(other < bit for other in left)
    count = 1 << (len(left) - 1)
    return [((n >> low) << (low + 1) | n & ((1 << low) - 1)) + (value << low) for n in range(count)]


class Streams:
    def __init__(self, refs, rows):
        self.refs, self.rows = refs, rows

    def at(self, stream, spot):
        if len(self.refs) == 2:
            return self.refs[stream].at[spot]
        first = sum(self.rows[:stream])
        return self.refs[0].at[spot, first : first + self.rows[stream]]


class TokSum:
    def __init__(self, streams, own, got, extra=None, finish=None, alone=False):
        self.size = lax.axis_size("tok")
        bits = self.size.bit_length() - 1
        self.there = [(0, 1), (1, 0)] + [(bit, bit) for bit in range(2, bits)]
        self.left = [list(reversed(range(bits)))] * 2
        self.job = 0
        self.alone = alone
        self.keep = pltpu.VMEM
        self.extra, self.finish = extra, finish
        units = [0] * len(own)
        for stream in streams:
            for n, first, rows in stream:
                units[n] = math.gcd(units[n], first, rows // self.size)
        self.items = [
            [(n, first // units[n], rows // self.size // units[n], units[n]) for n, first, rows in stream]
            for stream in streams
        ]
        self.rows = [sum(rows // self.size for _, _, rows in stream) for stream in streams]
        self.width = own[0].shape[-1]
        self.inputs = [
            x.reshape(-1, unit, self.width) for xs in (own, got) for x, unit in zip(xs, units)
        ]

    def shapes(self, count, together):
        rows = [sum(self.rows)] if together else self.rows
        return [jax.ShapeDtypeStruct((count, row, self.width), BF16) for row in rows]

    def work(self):
        steps = len(self.there)
        job, self.job = self.job, self.job + 1
        if job <= steps:
            return self.adding(job, steps)
        return self.joining(2 * steps - job)

    def adding(self, job, steps):
        inputs, rows, left = self.inputs, self.rows, self.left
        extra = self.extra if job == steps else None
        if job < steps:
            bits = self.there[job]
            together = bits[0] == bits[1]
            half = self.shapes(1 << (len(left[0]) - 1), together)
            shapes = [self.keep(x.shape, x.dtype) for x in half] + half
            self.left = [[b for b in mine if b != bit] for mine, bit in zip(left, bits)]
        else:
            bits = None
            if extra is not None:
                self.rows = [row + x.shape[0] for row, x in zip(rows, extra)]
                inputs = inputs + list(extra)
            shapes = self.shapes(1, True)
        new_rows = self.rows
        self.sent = len(shapes) // 2 if job < steps else 0

        def body(place, ins, outs):
            if extra is not None:
                ins, extras = ins[:-2], ins[-2:]
            count = len(ins) // 2

            def sums(stream, spot):
                if job > 0:
                    found = [Streams(ins[:count], rows), Streams(ins[count:], rows)]
                    a, b = (part.at(stream, spot)[...] for part in found)
                    return [(0, rows[stream], add_low(a, b))]
                first, found = 0, []
                for n, base, count_each, unit in self.items[stream]:
                    for piece in range(count_each):
                        block = base + spot * count_each + piece
                        found.append((first, unit, add_low(ins[n][block], ins[count + n][block])))
                        first += unit
                return found

            for stream in (0, 1):
                if bits is None:
                    ref = Streams(outs, new_rows).at(stream, 0)
                    ((_, row, value),) = sums(stream, 0)
                    ref[:row, :] = value
                    if extra is not None:
                        ref[row:, :] = extras[stream][...]
                    continue
                mine = place >> bits[stream] & 1
                split = len(outs) // 2
                for which, value in ((0, mine), (1, 1 - mine)):
                    target = Streams(outs[which * split : (which + 1) * split], rows)
                    for n, spot in enumerate(spots(left[stream], bits[stream], value)):
                        ref = target.at(stream, n)
                        for first, row, total in sums(stream, spot):
                            ref[first : first + row, :] = total

        return inputs, shapes, body

    def joining(self, step):
        inputs, rows = self.inputs, self.rows
        bits = self.there[step]
        before = self.left
        self.left = left = [sorted(have + [bit], reverse=True) for have, bit in zip(before, bits)]
        self.sent = 0
        if step == 0:
            shapes, write = self.finish(rows)
        else:
            then = self.there[step - 1]
            shapes = self.shapes(1 << len(left[0]), then[0] == then[1])

        def body(place, ins, outs):
            count = len(ins) // 2
            found = [Streams(ins[:count], rows), Streams(ins[count:], rows)]
            for stream in (0, 1):
                bit = bits[stream]
                mine = place >> bit & 1
                if step == 0:
                    low = sum(other < bit for other in left[stream])
                    for spot in range(1 << len(left[stream])):
                        n = (spot >> (low + 1)) << low | spot & ((1 << low) - 1)
                        kept, new = (part.at(stream, n)[...] for part in found)
                        write(outs, stream, spot, jnp.where(mine == (spot >> low & 1), kept, new))
                    continue
                for part, value in zip(found, (mine, 1 - mine)):
                    for n, spot in enumerate(spots(left[stream], bit, value)):
                        Streams(outs, rows).at(stream, spot)[...] = part.at(stream, n)[...]

        return inputs, shapes, body

    def take(self, outs):
        steps = len(self.there)
        if self.job > 2 * steps:
            self.found = outs
            return []
        kept, sent = (outs[: self.sent], outs[self.sent :]) if self.sent else (outs, outs)
        if self.job == steps + 1 and self.alone:
            self.piece = [sent[0].reshape(sent[0].shape[1:])]
            return sent
        step = self.job - 1 if self.job <= steps else 2 * steps - self.job
        got = [swap_bit(x, "tok", bit) for x, bit in zip(sent, self.there[step])]
        self.inputs = list(kept) + got
        return sent


def gather_rest(one):
    spread = lax.all_gather(one.piece[0], "tok", axis=0)
    one.job = 2 * len(one.there) + 1
    rows = one.rows
    shapes, write = one.finish(rows)

    def kernel(x_ref, *outs):
        for spot in range(x_ref.shape[0]):
            write(outs, 0, spot, x_ref[spot, : rows[0]])
            write(outs, 1, spot, x_ref[spot, rows[0] :])

    one.found = pl.pallas_call(
        kernel,
        in_specs=[pl.BlockSpec(memory_space=pltpu.VMEM)],
        out_specs=[pl.BlockSpec(memory_space=pltpu.VMEM)] * len(shapes),
        out_shape=shapes,
        compiler_params=vmem(32),
        name="sum_spread",
    )(spread)


class PlainSum:
    def __init__(self, streams, own, got, extra=None, finish=None, alone=False):
        whole = [
            lax.psum(a.astype(F32) + b.astype(F32), "tok").reshape(-1, a.shape[-1])
            for a, b in zip(own, got)
        ]
        self.found = [
            [whole[n][first : first + rows] for n, first, rows in stream] for stream in streams
        ]


def advance(sums, *others):
    if not isinstance(sums[0], TokSum):
        return []
    place = after(lax.axis_index("tok").astype(jnp.int32).reshape(1), *others)
    works = [one.work() for one in sums]

    def kernel(place_ref, *refs):
        place = place_ref[0]
        ins = refs[: sum(len(work[0]) for work in works)]
        outs = refs[len(ins) :]
        for inputs, shapes, body in works:
            body(place, ins[: len(inputs)], outs[: len(shapes)])
            ins, outs = ins[len(inputs) :], outs[len(shapes) :]

    inputs = [x for work in works for x in work[0]]
    shapes = [x for work in works for x in work[1]]
    size = 2 * sum(math.prod(x.shape) for x in inputs + shapes)
    outs = pl.pallas_call(
        kernel,
        in_specs=[pl.BlockSpec(memory_space=pltpu.SMEM)]
        + [pl.BlockSpec(memory_space=pltpu.VMEM)] * len(inputs),
        out_specs=[pl.BlockSpec(memory_space=pltpu.VMEM)] * len(shapes),
        out_shape=shapes,
        compiler_params=vmem(20),
        cost_estimate=pl.CostEstimate(flops=size, bytes_accessed=size, transcendentals=0),
        name="sum_step",
    )(place, *inputs)
    sent = []
    for one, work in zip(sums, works):
        sent += one.take(outs[: len(work[1])])
        outs = outs[len(work[1]) :]
    return sent


def body(
    tokens,
    cotangent,
    block_source,
    mask_index,
    mask_count,
    w_query,
    w_key,
    w_value,
    w_output,
    mid_gain,
    mid_shift,
    w_inner,
    bias_inner,
    w_outer,
    bias_outer,
    end_gain,
    end_shift,
):
    tok_place = lax.axis_index("tok")
    head_place = lax.axis_index("head")
    half = tok_place % 2
    width = tokens.shape[1]

    def mate(x):
        return swap_bit(x, "head", 0)

    kept, given = halves(tokens, half)
    cot_kept, cot_given = halves(cotangent, half)
    x_got = swap_bit(given, "tok", 0)
    own_w = (w_query, w_key, w_value)
    mate_w = tuple(mate(w) for w in own_w)
    mate_out = mate(w_output)
    mate_in = mate(w_inner)
    own_bias = bias_inner[None, :]
    mate_bias = mate(own_bias)

    sequence = tok_place // 2 * PAIR_SEQS + 2 * head_place + half
    source = lax.dynamic_slice_in_dim(block_source, sequence, 1, 0)[0, :, 0]
    per_half = GROUPS // 2
    flags = jnp.concatenate(
        [
            lax.dynamic_slice_in_dim(source, head_place * per_half, per_half, 0),
            lax.dynamic_slice_in_dim(source, (1 - head_place) * per_half, per_half, 0),
        ]
    )
    swap_lanes = jnp.repeat(flags, HEADS // GROUPS * HDIM)[None, :]
    positions = lax.dynamic_slice_in_dim(mask_index, sequence, 1, 0)[0]
    count = lax.dynamic_slice_in_dim(mask_count, sequence, 1, 0)[0]
    within = jnp.arange(BLOCK)
    places = jnp.concatenate([half * BLOCK + within, (1 - half) * BLOCK + within])
    live = jnp.arange(positions.shape[0]) < count
    hits = jnp.any((positions[None, :] == places[:, None]) & live[None, :], axis=1)
    weight = (1.0 + 3.0 * hits.astype(F32))[:, None]
    params = jnp.stack(
        [mid_gain, mid_shift, bias_outer, end_gain, end_shift] + [jnp.zeros_like(mid_gain)] * 3
    )
    mate_down = mate(after(w_outer, weight, swap_lanes, cot_given, params))

    qkv, lse, ctx_t, x_t, mid_n, mid_rate = attention(
        swap_lanes, (kept, after(x_got, swap_lanes, weight, params, cot_kept)), own_w, mate_w,
        w_output, mate_out,
    )
    cot_got = swap_bit(after(cot_given, x_got), "tok", 0)
    act_t, slope, h1_t, out_kept, out_first, out_rest, d_s2, d_f, end_vec, g_mate = ffn(
        mid_n, params, w_inner, mate_in, own_bias, mate_bias, w_outer, mate_down,
        (cot_kept, cot_got), weight,
    )

    hidden = w_inner.shape[1]
    cut = w_output.shape[0]
    pairs = cut // LANES

    def side_by_side(g):
        return jnp.concatenate([g[:, n : n + COLS] for n in range(0, width, COLS)], axis=0)

    rest = width // 2

    def finish_down(rows):
        def write(outs, stream, spot, value):
            outs[0][stream, spot] = value.astype(F32)

        return [jax.ShapeDtypeStruct((2, lax.axis_size("tok"), rows[0], width), F32)], write

    def finish_inner(rows):
        size = lax.axis_size("tok")

        def write(outs, stream, spot, value):
            value = value.astype(F32)
            one = width // size
            outs[0][spot, :, stream * width : (stream + 1) * width] = value[:one]
            more = rows[stream] - one - 8
            first = spot * more + (third if stream else 0)
            outs[1][first : first + more, :] = value[one : one + more]
            if stream == 0 and spot == 0:
                outs[2][...] = value[one + more :]
            else:
                outs[2][...] += value[one + more :]

        return [
            jax.ShapeDtypeStruct((size, width // size, 2 * width), F32),
            jax.ShapeDtypeStruct((rest, width), F32),
            jax.ShapeDtypeStruct((8, width), F32),
        ], write

    size = lax.axis_size("tok")
    fits = size & (size - 1) == 0 and size >= 4 and rest % (8 * size) == 0
    Sum = TokSum if fits else PlainSum

    got = mate(g_mate)
    mine = product(act_t, 0, hidden, d_f, BLOCK)
    cut = hidden // 2
    down = Sum([[(0, 0, cut)], [(0, cut, cut)]], [mine], [got], finish=finish_down, alone=False)
    sent = advance([down], mine)
    gi_mate, gb_mate, d_h1 = ffn_back(
        1, after(d_f, sent), slope, mate_in, mate_down, h1_t, d_s2
    )
    sent = advance([down], gi_mate)
    first_got = swap_bit(after(out_first, sent), "tok", 0)
    got_in = mate(after(gi_mate, sent))
    gi_own, gb_own, go_own, go_mate, d_s1, d_a, mid_vec = ffn_back(
        0, after(d_f, sent), slope, w_inner, w_outer, h1_t, d_h1, mid_n, mid_rate, ctx_t, params
    )
    got_out = mate(after(go_mate, down.inputs[-2:], first_got) if fits else go_mate)
    third = 8 * size
    inner = Sum(
        [[(0, 0, width), (1, 0, third)], [(0, width, width), (1, third, rest - third)]],
        [gi_own, go_own], [got_in, got_out], finish=finish_inner, alone=False,
    )
    sent = advance([inner, down], gi_own)
    rest_got = swap_bit(after(out_rest, sent), "tok", 0)
    gw_mate, gw_mates, gw_own, dp_early = attention_back(
        (1, pairs, pairs + 1), lambda p: jnp.where(p < pairs, p + pairs, 0), swap_lanes, qkv, ctx_t,
        lse, (w_output, mate_out), after(d_a, sent), x_t,
    )
    sent = advance([inner, down], gw_own, rest_got)
    gw_got, gw_gots = (mate(x) for x in after((gw_mate, gw_mates), sent))

    gw_owns, dp_late = attention_back(
        (pairs - 1,), lambda p: p + 1, swap_lanes, qkv, ctx_t, lse, (w_output,), after(d_a, sent), x_t
    )
    head = (pairs * width // size + 31) // 32 * 16 * size - width

    def finish_last(rows):
        def write(outs, stream, spot, value):
            value = value.astype(F32)
            count = rows[stream]
            pieces = [(0, spot * count + width + head, count)]
            if stream == 0:
                one = width // size
                pieces = [(0, spot * one, one), (one, width + spot * (count - one), count - one)]
            for done, first, length in pieces:
                while length > 0:
                    p, row = divmod(first, width)
                    step = min(length, width - row)
                    for at in range(3):
                        outs[at][row : row + step, p * LANES : (p + 1) * LANES] = value[
                            done : done + step, at * LANES : (at + 1) * LANES
                        ]
                    done, first, length = done + step, first + step, length - step

        return [jax.ShapeDtypeStruct((width, pairs * LANES), F32)] * 3, write

    rows = (pairs - 1) * width
    last = Sum(
        [[(0, 0, width), (1, 0, head)], [(1, head, rows - head)]],
        [x.reshape(-1, 3 * LANES) for x in (gw_own, gw_owns)],
        [x.reshape(-1, 3 * LANES) for x in (gw_got, gw_gots)],
        finish=finish_last,
    )
    for one in (last, inner, down):
        one.keep = pltpu.VMEM
    sent = advance([last, inner, down], gw_owns)
    out = joined(out_kept, jnp.concatenate([first_got, rest_got], axis=0), half)
    own_rows = gb_own.size // width

    def small_vectors(sent):
        end, mid, own, other = after((end_vec, mid_vec, gb_own, gb_mate), sent)
        own, other = own.reshape(-1, width), other.reshape(-1, width)
        small = jnp.concatenate([end[:3], mid[:2], own, other], axis=0)
        theirs = mate(small)
        small = jnp.concatenate(
            [
                small[:5] + theirs[:5],
                small[5 : 5 + own_rows] + theirs[5 + own_rows :],
                jnp.zeros((1, width), F32),
            ],
            axis=0,
        )
        high = small.astype(BF16)
        low = (small - high.astype(F32)).astype(BF16)
        return small, (high, low)

    dx_kept, dx_given = input_gradient(dp_early, after(dp_late, sent), own_w, mate_w, d_s1)
    dx_got, finals = [], []
    if fits:
        while last.job <= 2 * len(last.there):
            for one in (inner, down):
                if one.alone and one.job == len(one.there) + 1:
                    gather_rest(one)
            sums = [one for one in (last, inner, down) if one.job <= 2 * len(one.there)]
            others = [dx_given] if last.job == 1 else []
            if last.job in (2, 3):
                first = (last.job - 2) * (BLOCK // 2)
                part = dx_given[first : first + BLOCK // 2]
                others = [swap_bit(after(part, last.inputs[0]), "tok", 0)]
                dx_got += others
            ending = [one for one in sums if one is not last and one.job == 2 * len(one.there)]
            sent = advance([one for one in sums if one not in ending], *others, *finals)
            if last.job == 2:
                small, inner.extra = small_vectors(sent)
            finals = []
            for one in ending:
                advance([one], sent)
                finals += one.found
        g_down, (g_in, g_out, small), (g_query, g_key, g_value) = (
            down.found[0], inner.found, last.found
        )
    else:
        dx_got = [swap_bit(dx_given, "tok", 0)]
        g_down = jnp.concatenate([down.found[0][0], down.found[1][0]], axis=0)
        g_in = jnp.concatenate([inner.found[0][0], inner.found[1][0]], axis=1)
        g_out = jnp.concatenate([inner.found[0][1], inner.found[1][1]], axis=0)
        whole_w = jnp.concatenate(last.found[0] + last.found[1], axis=0)
        whole_w = whole_w.reshape(pairs, width, 3, LANES)
        g_query, g_key, g_value = (
            jnp.concatenate([whole_w[p, :, at] for p in range(pairs)], axis=1) for at in range(3)
        )
        small = lax.psum(small_vectors(())[0], "tok")
    dx_got = jnp.concatenate(dx_got, axis=0).astype(F32)
    grad_tokens = joined(dx_kept, dx_got, half)
    g_down = g_down.reshape(hidden, width)
    g_in = g_in.reshape(width, hidden)
    g_out = g_out.reshape(rest, width)

    return (
        out,
        grad_tokens,
        g_query,
        g_key,
        g_value,
        g_out,
        small[4],
        small[3],
        g_in,
        small[5 : 5 + own_rows].reshape(-1),
        g_down,
        small[2],
        small[1],
        small[0],
    )


def solution(mesh):
    rows = P(("tok", "head"), None)
    return jax.shard_map(
        body,
        mesh=mesh,
        in_specs=(
            rows,
            rows,
            P(),
            P(),
            P(),
            P(None, "head"),
            P(None, "head"),
            P(None, "head"),
            P("head", None),
            P(),
            P(),
            P(None, "head"),
            P("head"),
            P("head", None),
            P(),
            P(),
            P(),
        ),
        out_specs=(
            rows,
            rows,
            P(None, "head"),
            P(None, "head"),
            P(None, "head"),
            P("head", None),
            P(),
            P(),
            P(None, "head"),
            P("head"),
            P("head", None),
            P(),
            P(),
            P(),
        ),
        check_vma=False,
    )
```

```python
import functools
import math

import jax
import jax.numpy as jnp
from jax import lax
from jax.experimental import pallas as pl
from jax.experimental.pallas import tpu as pltpu
from jax.sharding import PartitionSpec as P

HEADS = 12
HDIM = 64
GROUPS = 4
BLOCK = 512
PAIR_SEQS = 4
LANES = 128

NORM_EPS = 1e-05
LOG2E = 1.4426950408889634
BF16 = jnp.bfloat16
F32 = jnp.float32


def swap_bit(x, axis, bit):
    return lax.ppermute(x, axis, [(i, i ^ 1 << bit) for i in range(lax.axis_size(axis))])


def dot(a, b, dims=((1,), (0,))):
    return lax.dot_general(a, b, (dims, ((), ())), preferred_element_type=F32)


NT = ((1,), (1,))
TN = ((0,), (0,))


def head_lanes(first):
    lane = lax.broadcasted_iota(jnp.int32, (1, LANES), 1)
    return (lane < HDIM) if first else (lane >= HDIM)


def vmem(limit=56):
    return pltpu.CompilerParams(vmem_limit_bytes=limit * 1024 * 1024)


def whole(shape):
    return pl.BlockSpec(shape, lambda *_: (0,) * len(shape), pipeline_mode=pl.Buffered(1))


def hbm(*arrays):
    return [pltpu.with_memory_space_constraint(x, pltpu.HBM) for x in arrays]


def pick(own, w_own_ref, w_mate_ref):
    return jnp.where(own, w_own_ref[...], w_mate_ref[...])


def normalize(summed):
    center = summed - jnp.mean(summed, axis=-1, keepdims=True)
    rate = lax.rsqrt(jnp.mean(center * center, axis=-1, keepdims=True) + NORM_EPS)
    return center * rate, rate


def norm_back(grad, normed, rate, gain):
    scaled = grad * gain
    return rate * (
        scaled
        - jnp.mean(scaled, axis=-1, keepdims=True)
        - normed * jnp.mean(scaled * normed, axis=-1, keepdims=True)
    )


def gelu_parts(u):
    size = jnp.abs(u)
    bell = jnp.exp2(u * u * (-0.5 * LOG2E))
    t = 1.0 / (1.0 + (0.3275911 * 0.5**0.5) * size)
    poly = t * (
        0.5 * 0.254829592
        + t
        * (
            0.5 * -0.284496736
            + t * (0.5 * 1.421413741 + t * (0.5 * -1.453152027 + t * (0.5 * 1.061405429)))
        )
    )
    tail = poly * bell
    phi = jnp.where(u > 0, 1.0 - tail, tail)
    return u * phi, phi + u * (bell * 0.3989422804014327)


SLOTS = (slice(0, BLOCK), slice(BLOCK, 2 * BLOCK))


def attend_kernel(
    pairs, swap_ref, xa_ref, xb_ref, wq_ref, wk_ref, wv_ref, mq_ref, mk_ref, mv_ref, wo_ref, mo_ref,
    qkv_ref, lse_ref, ctx_t_ref, x_t_ref, mid_n_ref, rate_ref, ctx_all,
):
    step = pl.program_id(0)
    own = step < pairs // 2
    swap = swap_ref[...] > 0
    scale = LOG2E * HDIM**-0.5
    ones = jnp.ones((16, BLOCK), BF16)
    w = jnp.concatenate(
        [pick(own, wq_ref, mq_ref), pick(own, wk_ref, mk_ref), pick(own, wv_ref, mv_ref)], axis=1
    )
    for rows, x_ref in zip(SLOTS, (xa_ref, xb_ref)):
        qkv_ref[rows, :] = dot(x_ref[...], w).astype(BF16)
    keys = [qkv_ref[rows, LANES : 2 * LANES] for rows in SLOTS]
    values = [qkv_ref[rows, 2 * LANES :] for rows in SLOTS]
    units = []
    for i, rows in enumerate(SLOTS):
        q = qkv_ref[rows, :LANES]
        k = jnp.where(swap, keys[1 - i], keys[i])
        v_t = jnp.where(swap, values[1 - i], values[i]).T
        for n in (0, 1):
            q_n = jnp.where(head_lanes(n == 0), q, jnp.zeros_like(q))
            units.append((rows, n, v_t, dot(k, q_n, NT)))
    parts = []
    for rows, n, v_t, s in units:
        top = jnp.max(s, axis=0, keepdims=True)
        p = jnp.exp2((s - top) * scale).astype(BF16)
        v_n = jnp.concatenate([v_t[n * HDIM : (n + 1) * HDIM], ones], axis=0)
        acc = dot(v_n, p)
        total = acc[HDIM : HDIM + 1]
        parts.append(acc[:HDIM] / total)
        lse_ref[0, n : n + 1, rows] = top * scale + jnp.log2(total)
        if n == 1:
            ctx_t = jnp.concatenate(parts, axis=0)
            parts = []
            ctx_t_ref[:, rows] = ctx_t.astype(BF16)
            ctx_all[step, rows, :] = ctx_t.T.astype(BF16)

    cols = pl.ds(pl.multiple_of(step * LANES, LANES), LANES)
    for rows, x_ref in zip(SLOTS, (xa_ref, xb_ref)):
        x_t_ref[:, rows] = x_ref[:, cols].T

    @pl.when(step == pairs - 1)
    def _():
        for rows, x_ref in zip(SLOTS, (xa_ref, xb_ref)):
            total = x_ref[...].astype(F32)
            every = jnp.concatenate([ctx_all[p, rows, :] for p in range(pairs)], axis=1)
            cut = wo_ref.shape[0]
            total = total + dot(every[:, :cut], wo_ref[...]) + dot(every[:, cut:], mo_ref[...])
            normed, rate = normalize(total)
            mid_n_ref[rows, :] = normed
            rate_ref[rows, :] = rate


def attention(swap_lanes, blocks, own_w, mate_w, own_out, mate_out):
    width = blocks[0].shape[1]
    rows = 2 * BLOCK
    pairs = width // LANES
    per = own_w[0].shape[1] // LANES
    own_spec = pl.BlockSpec((width, LANES), lambda p: (0, jnp.minimum(p, per - 1)))
    mate_spec = pl.BlockSpec((width, LANES), lambda p: (0, jnp.maximum(p - per, 0)))
    return pl.pallas_call(
        functools.partial(attend_kernel, pairs),
        grid=(pairs,),
        in_specs=[pl.BlockSpec((1, LANES), lambda p: (0, p))]
        + [whole((BLOCK, width))] * 2
        + [own_spec] * 3
        + [mate_spec] * 3
        + [whole(own_out.shape)] * 2,
        out_specs=[
            pl.BlockSpec((rows, 3 * LANES), lambda p: (0, p)),
            pl.BlockSpec((1, 2, rows), lambda p: (p, 0, 0)),
            pl.BlockSpec((LANES, rows), lambda p: (p, 0)),
            pl.BlockSpec((LANES, rows), lambda p: (p, 0)),
            whole((rows, width)),
            whole((rows, 1)),
        ],
        out_shape=[
            pltpu.HBM((rows, 3 * width), BF16),
            jax.ShapeDtypeStruct((pairs, 2, rows), F32),
            pltpu.HBM((width, rows), BF16),
            pltpu.HBM((width, rows), BF16),
            pltpu.HBM((rows, width), F32),
            pltpu.HBM((rows, 1), F32),
        ],
        scratch_shapes=[pltpu.VMEM((pairs, rows, LANES), BF16)],
        compiler_params=vmem(28),
        cost_estimate=pl.CostEstimate(
            flops=2 * rows * width * width * 4 + 4 * pairs * 4 * BLOCK * BLOCK * 256,
            bytes_accessed=rows * width * 18 + width * width * 8,
            transcendentals=4 * pairs * BLOCK * BLOCK,
        ),
        name="attention_forward",
    )(swap_lanes, *blocks, *hbm(*own_w, *mate_w, own_out, mate_out))


def ffn_kernel(
    tiles, mid_n_ref, par_ref, wi_ref, mi_ref, bi_ref, mbi_ref, wd_ref, md_ref, ca_ref, cb_ref, wt_ref,
    act_t_ref, slope_ref, h1_t_ref, kept_ref, first_ref, rest_ref, ds2_ref, df_ref, vec_ref, gm_ref,
    h1_low, acc, act_m,
):
    step = pl.program_id(0)
    own = step < tiles // 2

    @pl.when(step == 0)
    def _():
        for rows in SLOTS:
            h1 = mid_n_ref[rows, :] * par_ref[0:1, :] + par_ref[1:2, :]
            low = h1.astype(BF16)
            h1_low[rows, :] = low
            h1_t_ref[:, rows] = low.T
            acc[rows, :] = h1 + par_ref[2:3, :]

    size = 256

    def tile(w_in, w_down, bias, act_ref):
        cuts = [slice(at, at + size) for at in range(0, 2 * BLOCK, size)]
        ready = [dot(h1_low[cuts[0], :], w_in)]
        for at, rows in enumerate(cuts):
            if at + 1 < len(cuts):
                ready.append(dot(h1_low[cuts[at + 1], :], w_in))
            value, slope = gelu_parts(ready[at] + bias)
            low = value.astype(BF16)
            slope_ref[rows, :] = slope.astype(BF16)
            act_ref[:, rows] = low.T
            acc[rows, :] += dot(low, w_down)

    @pl.when(own)
    def _():
        tile(wi_ref[...], wd_ref[...], bi_ref[...], act_t_ref)

    @pl.when(jnp.logical_and(step >= tiles // 2, step < tiles))
    def _():
        tile(mi_ref[...], md_ref[...], mbi_ref[...], act_m.at[step - tiles // 2])

    @pl.when(step >= tiles)
    def _():
        gm_ref[...] = dot(act_m[step - tiles], df_ref[...]).astype(BF16)

    @pl.when(step == tiles - 1)
    def _():
        gain = par_ref[3:4, :]
        sums = [0.0, 0.0, 0.0]
        for at in range(0, 2 * BLOCK, size):
            rows = slice(at, at + size)
            normed, rate = normalize(acc[rows, :])
            out = (normed * gain + par_ref[4:5, :]).astype(BF16)
            if at < BLOCK:
                kept_ref[rows, :] = out
            else:
                (first_ref if at == BLOCK else rest_ref)[...] = out
            cot_ref, first = (ca_ref, at) if at < BLOCK else (cb_ref, at - BLOCK)
            d_y = cot_ref[first : first + size, :].astype(F32) * wt_ref[rows, :]
            d_s2 = norm_back(d_y, normed, rate, gain)
            ds2_ref[rows, :] = d_s2
            df_ref[rows, :] = d_s2.astype(BF16)
            for n, term in enumerate((d_y, d_y * normed, d_s2)):
                sums[n] = sums[n] + jnp.sum(term, axis=0, keepdims=True)
        vec_ref[...] = jnp.concatenate(sums + [jnp.zeros((5, gain.shape[1]), F32)], axis=0)


TILE = 768
COLS = 384


def ffn(mid_n, params, own_in, mate_in, own_bias, mate_bias, own_down, mate_down, cot, weight):
    rows, width = mid_n.shape
    per = own_in.shape[1] // TILE
    tiles = 2 * per

    def own_at(j):
        return jnp.minimum(j, per - 1)

    def mate_at(j):
        return jnp.clip(j - per, 0, per - 1)

    hidden = 2 * own_in.shape[1]
    return pl.pallas_call(
        functools.partial(ffn_kernel, tiles),
        grid=(tiles + per,),
        in_specs=[
            whole((rows, width)),
            whole(params.shape),
            pl.BlockSpec((width, TILE), lambda j: (0, own_at(j))),
            pl.BlockSpec((width, TILE), lambda j: (0, mate_at(j))),
            pl.BlockSpec((1, TILE), lambda j: (0, own_at(j))),
            pl.BlockSpec((1, TILE), lambda j: (0, mate_at(j))),
            pl.BlockSpec((TILE, width), lambda j: (own_at(j), 0)),
            pl.BlockSpec((TILE, width), lambda j: (mate_at(j), 0)),
            whole((BLOCK, width)),
            whole((BLOCK, width)),
            whole((rows, 1)),
        ],
        out_specs=[
            pl.BlockSpec((TILE, rows), lambda j: (own_at(j), 0)),
            pl.BlockSpec((rows, TILE), lambda j: (0, jnp.minimum(j, tiles - 1))),
            whole((width, rows)),
            whole((BLOCK, width)),
            whole((BLOCK // 2, width)),
            whole((BLOCK // 2, width)),
            whole((rows, width)),
            whole((rows, width)),
            whole((8, width)),
            pl.BlockSpec((TILE, width), lambda j: (jnp.maximum(j - tiles, 0), 0)),
        ],
        out_shape=[
            jax.ShapeDtypeStruct((hidden // 2, rows), BF16),
            pltpu.HBM((rows, hidden), BF16),
            jax.ShapeDtypeStruct((width, rows), BF16),
            jax.ShapeDtypeStruct((BLOCK, width), BF16),
            jax.ShapeDtypeStruct((BLOCK // 2, width), BF16),
            jax.ShapeDtypeStruct((BLOCK // 2, width), BF16),
            jax.ShapeDtypeStruct((rows, width), F32),
            jax.ShapeDtypeStruct((rows, width), BF16),
            jax.ShapeDtypeStruct((8, width), F32),
            jax.ShapeDtypeStruct((hidden // 2, width), BF16),
        ],
        scratch_shapes=[
            pltpu.VMEM((rows, width), BF16),
            pltpu.VMEM((rows, width), F32),
            pltpu.VMEM((per, TILE, rows), BF16),
        ],
        compiler_params=vmem(40),
        cost_estimate=pl.CostEstimate(
            flops=4 * rows * width * hidden,
            bytes_accessed=rows * hidden * 4 + rows * width * 16 + width * hidden * 4,
            transcendentals=rows * hidden * 2,
        ),
        name="feed_forward",
    )(
        *hbm(mid_n), params, *hbm(own_in, mate_in), own_bias, mate_bias,
        *hbm(own_down, mate_down), *cot, weight,
    )


def product_kernel(a_ref, b_ref, c_ref):
    c_ref[...] = dot(a_ref[...], b_ref[...]).astype(BF16)


def product(a, first, rows, b, block):
    return pl.pallas_call(
        product_kernel,
        grid=(rows // block,),
        in_specs=[pl.BlockSpec((block, a.shape[1]), lambda j: (j + first // block, 0)), whole(b.shape)],
        out_specs=pl.BlockSpec((block, b.shape[1]), lambda j: (j, 0)),
        out_shape=jax.ShapeDtypeStruct((rows, b.shape[1]), BF16),
        compiler_params=vmem(12),
        cost_estimate=pl.CostEstimate(
            flops=2 * rows * a.shape[1] * b.shape[1],
            bytes_accessed=2 * (rows * (a.shape[1] + b.shape[1]) + b.shape[0] * b.shape[1]),
            transcendentals=0,
        ),
        name="weight_gradient",
    )(a, b)


def ffn_back_kernel(
    last, df_ref, slope_ref, wi_ref, wd_ref, h1_t_ref, start_ref, *refs
):
    if last:
        (mid_n_ref, rate_ref, ctx_t_ref, par_ref, gin_ref, db_ref, gown_ref, gmate_ref, ds1_ref,
         da_ref, vec_ref, du, acc) = refs
    else:
        gin_ref, db_ref, acc, du = refs
    step = pl.program_id(0)
    w_in = wi_ref[...]
    w_down = wd_ref[...]

    @pl.when(step == 0)
    def _():
        acc[...] = start_ref[...]

    size = 256
    total = 0.0
    cuts = [slice(at, at + size) for at in range(0, 2 * BLOCK, size)]
    ready = [dot(df_ref[cuts[0], :], w_down, NT)]
    for at, rows in enumerate(cuts):
        if at + 1 < len(cuts):
            ready.append(dot(df_ref[cuts[at + 1], :], w_down, NT))
        d_u = ready[at] * slope_ref[rows, :].astype(F32)
        total = total + jnp.sum(d_u, axis=0, keepdims=True)
        low = d_u.astype(BF16)
        du[rows, :] = low
        acc[rows, :] += dot(low, w_in, NT)
    db_ref[...] = total
    gin_ref[0] = dot(h1_t_ref[...], du[...]).astype(BF16)
    if not last:
        return

    @pl.when(step == pl.num_programs(0) - 1)
    def _():
        sums = [0.0, 0.0]
        gain = par_ref[0:1, :]
        for at in range(0, 2 * BLOCK, size):
            rows = slice(at, at + size)
            d_h1 = acc[rows, :]
            normed = mid_n_ref[rows, :]
            d_s1 = norm_back(d_h1, normed, rate_ref[rows, :], gain)
            ds1_ref[rows, :] = d_s1
            da_ref[rows, :] = d_s1.astype(BF16)
            for n, term in enumerate((d_h1, d_h1 * normed)):
                sums[n] = sums[n] + jnp.sum(term, axis=0, keepdims=True)
        vec_ref[...] = jnp.concatenate(sums + [jnp.zeros((6, gain.shape[1]), F32)], axis=0)
        cut = gown_ref.shape[0]
        gown_ref[...] = dot(ctx_t_ref[:cut, :], da_ref[...]).astype(BF16)
        gmate_ref[...] = dot(ctx_t_ref[cut:, :], da_ref[...]).astype(BF16)


def ffn_back(first, d_f, slope, w_in, w_down, h1_t, start, *rest):
    rows, width = d_f.shape
    hidden = w_in.shape[1]
    tiles = hidden // TILE
    last = len(rest) > 0
    grid_out = [
        pl.BlockSpec((1, width, TILE), lambda j: (j, 0, 0)),
        pl.BlockSpec((1, TILE), lambda j: (0, j)),
    ]
    shapes = [
        jax.ShapeDtypeStruct((tiles, width, TILE), BF16),
        jax.ShapeDtypeStruct((1, hidden), F32),
    ]
    scratch = [pltpu.VMEM((rows, TILE), BF16)]
    if last:
        whole_out = [((width // 2, width), BF16)] * 2 + [
            ((rows, width), F32), ((rows, width), BF16), ((8, width), F32)
        ]
        scratch.append(pltpu.VMEM((rows, width), F32))
    else:
        whole_out = [((rows, width), F32)]
    return pl.pallas_call(
        functools.partial(ffn_back_kernel, last),
        grid=(tiles,),
        in_specs=[
            whole((rows, width)),
            pl.BlockSpec((rows, TILE), lambda j: (0, j + first * tiles)),
            pl.BlockSpec((width, TILE), lambda j: (0, j)),
            pl.BlockSpec((TILE, width), lambda j: (j, 0)),
            whole((width, rows)),
            whole((rows, width)),
        ]
        + [whole(x.shape) for x in rest],
        out_specs=grid_out + [whole(shape) for shape, _ in whole_out],
        out_shape=shapes + [jax.ShapeDtypeStruct(shape, kind) for shape, kind in whole_out],
        scratch_shapes=scratch,
        compiler_params=vmem(32),
        cost_estimate=pl.CostEstimate(
            flops=6 * rows * width * hidden,
            bytes_accessed=rows * hidden * 2 + rows * width * 18 + width * hidden * 6,
            transcendentals=0,
        ),
        name="feed_forward_back",
    )(d_f, *hbm(slope, w_in, w_down), h1_t, start, *hbm(*rest[:-1]), *rest[-1:])


def attend_back_kernel(
    ends, swap_ref, qkv_ref, ctx_t_ref, lse_ref, da_ref, x_t_ref, *refs
):
    step = pl.program_id(0)
    outs = refs[-1 - len(ends) :]
    dqkv = outs[-1]
    w_out = pick(step >= ends[-2], *refs[:2]) if len(ends) > 1 else refs[0][...]
    swap = swap_ref[...] > 0
    scale = LOG2E * HDIM**-0.5

    keys = [qkv_ref[rows, LANES : 2 * LANES] for rows in SLOTS]
    values = [qkv_ref[rows, 2 * LANES :] for rows in SLOTS]
    blocks, units = [], []
    for i, rows in enumerate(SLOTS):
        q = qkv_ref[rows, :LANES]
        k = jnp.where(swap, keys[1 - i], keys[i])
        v = jnp.where(swap, values[1 - i], values[i])
        dctx = dot(da_ref[rows, :], w_out, NT).astype(BF16)
        prod_t = dctx.T.astype(F32) * ctx_t_ref[:, rows].astype(F32)
        blocks.append((rows, q, k, v, k.T, dctx, prod_t))
    for i, (rows, q, k, v, k_t, dctx, prod_t) in enumerate(blocks):
        for n in (0, 1):
            own = head_lanes(n == 0)
            q_n = jnp.where(own, q, jnp.zeros_like(q))
            d_n = jnp.where(own, dctx, jnp.zeros_like(dctx))
            units.append((i, n, q_n, d_n))

    def products(unit):
        i, n, q_n, d_n = unit
        return dot(blocks[i][2], q_n, NT), dot(blocks[i][3], d_n, NT)

    ahead = 2
    ready = [products(unit) for unit in units[:ahead]]
    found = []
    for at, (i, n, q_n, d_n) in enumerate(units):
        if at + ahead < len(units):
            ready.append(products(units[at + ahead]))
        rows, q, k, v, k_t, dctx, prod_t = blocks[i]
        cut = slice(n * HDIM, (n + 1) * HDIM)
        s, d_p = ready[at]
        p = jnp.exp2(s * scale - lse_ref[0, n : n + 1, rows])
        inner = jnp.sum(prod_t[cut], axis=0, keepdims=True)
        ds = (p * (d_p - inner)).astype(BF16)
        dv_n = dot(p.astype(BF16), d_n)
        dk_n = dot(ds, q_n)
        if n == 0:
            dv, dk, dq_t = dv_n, dk_n, [dot(k_t[cut], ds)]
        else:
            dv, dk = dv + dv_n, dk + dk_n
            dq_t.append(dot(k_t[cut], ds))
            dq = jnp.concatenate(dq_t, axis=0).T
            dqkv[rows, :LANES] = (dq * HDIM**-0.5).astype(BF16)
            found.append(((dk * HDIM**-0.5).astype(BF16), dv.astype(BF16)))
    for i, rows in enumerate(SLOTS):
        for at in (0, 1):
            dqkv[rows, (at + 1) * LANES : (at + 2) * LANES] = jnp.where(
                swap, found[1 - i][at], found[i][at]
            )
    grad = dot(x_t_ref[...], dqkv[...]).astype(BF16)
    if len(ends) == 1:
        outs[0][0] = grad
        return
    for first, end, gw_ref in zip((0,) + ends, ends, outs):

        @pl.when(jnp.logical_and(step >= first, step < end))
        def _():
            gw_ref[0] = grad


def attention_back(ends, at, swap_lanes, qkv, ctx_t, lse, w_outs, d_a, x_t):
    rows, width = d_a.shape
    pairs = ends[-1]
    if len(ends) > 1:
        w_at = [lambda p: jnp.maximum(p - ends[-2], 0), lambda p: jnp.minimum(p, ends[-2] - 1)]
    else:
        w_at = [at]

    def w_spec(place):
        return pl.BlockSpec((LANES, width), lambda p: (place(p), 0))

    def spec(first, end):
        return pl.BlockSpec(
            (1, width, 3 * LANES), lambda p: (jnp.clip(p - first, 0, end - first - 1), 0, 0)
        )

    parts = list(zip((0,) + ends, ends))
    return pl.pallas_call(
        functools.partial(attend_back_kernel, ends),
        grid=(pairs,),
        in_specs=[
            pl.BlockSpec((1, LANES), lambda p: (0, at(p))),
            pl.BlockSpec((rows, 3 * LANES), lambda p: (0, at(p))),
            pl.BlockSpec((LANES, rows), lambda p: (at(p), 0)),
            pl.BlockSpec((1, 2, rows), lambda p: (at(p), 0, 0)),
            whole((rows, width)),
            whole((width, rows)),
        ]
        + [w_spec(place) for place in w_at],
        out_specs=[spec(*part) for part in parts]
        + [pl.BlockSpec((rows, 3 * LANES), lambda p: (0, p))],
        out_shape=[
            jax.ShapeDtypeStruct((end - first, width, 3 * LANES), BF16) for first, end in parts
        ]
        + [pltpu.HBM((rows, pairs * 3 * LANES), BF16)],
        compiler_params=vmem(24),
        cost_estimate=pl.CostEstimate(
            flops=8 * rows * width * pairs * LANES + 4 * pairs * 10 * BLOCK * BLOCK * 256,
            bytes_accessed=rows * width * 14,
            transcendentals=4 * pairs * BLOCK * BLOCK,
        ),
        name="attention_backward",
    )(swap_lanes, *hbm(qkv, ctx_t), lse, d_a, *hbm(x_t, *w_outs))


def input_kernel(first_ref, later_ref, mate_ref, wq_ref, wk_ref, wv_ref, mq_ref, mk_ref, mv_ref, start_ref,
                 kept_ref, given_ref, acc):
    step = pl.program_id(0)
    w = jnp.concatenate([wq_ref[...], wk_ref[...], wv_ref[...]], axis=1)
    m = jnp.concatenate([mq_ref[...], mk_ref[...], mv_ref[...]], axis=1)

    @pl.when(step == 0)
    def _():
        acc[...] = start_ref[...]

    for rows in SLOTS:
        own = jnp.where(step == 0, first_ref[rows, :], later_ref[rows, :])
        acc[rows, :] += dot(own, w, NT) + dot(mate_ref[rows, :], m, NT)

    @pl.when(step == pl.num_programs(0) - 1)
    def _():
        kept_ref[...] = acc[:BLOCK, :]
        given_ref[...] = acc[BLOCK:, :].astype(BF16)


def input_gradient(early, late, own_w, mate_w, start):
    rows, width = start.shape
    pairs = early.shape[1] // (3 * LANES) - 1
    part = (rows, 3 * LANES)
    w_spec = pl.BlockSpec((width, LANES), lambda p: (0, p))
    return pl.pallas_call(
        input_kernel,
        grid=(pairs,),
        in_specs=[
            pl.BlockSpec(part, lambda p: (0, pairs)),
            pl.BlockSpec(part, lambda p: (0, jnp.maximum(p - 1, 0))),
            pl.BlockSpec(part, lambda p: (0, p)),
        ]
        + [w_spec] * 6 + [whole((rows, width))],
        out_specs=[whole((BLOCK, width))] * 2,
        out_shape=[
            jax.ShapeDtypeStruct((BLOCK, width), F32), jax.ShapeDtypeStruct((BLOCK, width), BF16)
        ],
        scratch_shapes=[pltpu.VMEM((rows, width), F32)],
        compiler_params=vmem(24),
        cost_estimate=pl.CostEstimate(
            flops=12 * rows * width * pairs * LANES,
            bytes_accessed=rows * width * 14,
            transcendentals=0,
        ),
        name="input_gradient",
    )(*hbm(early, late, early, *own_w, *mate_w), start)


def halves(x, place):
    rows = x.shape[0] // 2
    return (
        lax.dynamic_slice_in_dim(x, place * rows, rows, 0),
        lax.dynamic_slice_in_dim(x, (1 - place) * rows, rows, 0),
    )


def joined(mine, other, place):
    return jnp.where(
        place == 0,
        jnp.concatenate([mine, other], axis=0),
        jnp.concatenate([other, mine], axis=0),
    )


def add_low(a, b):
    return (a.astype(F32) + b.astype(F32)).astype(BF16)


def after(x, *others):
    return lax.optimization_barrier((x, others))[0]


def spots(left, bit, value):
    low = sum(other < bit for other in left)
    count = 1 << (len(left) - 1)
    return [((n >> low) << (low + 1) | n & ((1 << low) - 1)) + (value << low) for n in range(count)]


class Streams:
    def __init__(self, refs, rows):
        self.refs, self.rows = refs, rows

    def at(self, stream, spot):
        if len(self.refs) == 2:
            return self.refs[stream].at[spot]
        first = sum(self.rows[:stream])
        return self.refs[0].at[spot, first : first + self.rows[stream]]


class TokSum:
    def __init__(self, streams, own, got, extra=None, finish=None, alone=False):
        self.size = lax.axis_size("tok")
        bits = self.size.bit_length() - 1
        self.there = [(0, 1), (1, 0)] + [(bit, bit) for bit in range(2, bits)]
        self.left = [list(reversed(range(bits)))] * 2
        self.job = 0
        self.alone = alone
        self.keep = pltpu.VMEM
        self.extra, self.finish = extra, finish
        units = [0] * len(own)
        for stream in streams:
            for n, first, rows in stream:
                units[n] = math.gcd(units[n], first, rows // self.size)
        self.items = [
            [(n, first // units[n], rows // self.size // units[n], units[n]) for n, first, rows in stream]
            for stream in streams
        ]
        self.rows = [sum(rows // self.size for _, _, rows in stream) for stream in streams]
        self.width = own[0].shape[-1]
        self.inputs = [
            x.reshape(-1, unit, self.width) for xs in (own, got) for x, unit in zip(xs, units)
        ]

    def shapes(self, count, together):
        rows = [sum(self.rows)] if together else self.rows
        return [jax.ShapeDtypeStruct((count, row, self.width), BF16) for row in rows]

    def work(self):
        steps = len(self.there)
        job, self.job = self.job, self.job + 1
        if job <= steps:
            return self.adding(job, steps)
        return self.joining(2 * steps - job)

    def adding(self, job, steps):
        inputs, rows, left = self.inputs, self.rows, self.left
        extra = self.extra if job == steps else None
        if job < steps:
            bits = self.there[job]
            together = bits[0] == bits[1]
            half = self.shapes(1 << (len(left[0]) - 1), together)
            shapes = [self.keep(x.shape, x.dtype) for x in half] + half
            self.left = [[b for b in mine if b != bit] for mine, bit in zip(left, bits)]
        else:
            bits = None
            if extra is not None:
                self.rows = [row + x.shape[0] for row, x in zip(rows, extra)]
                inputs = inputs + list(extra)
            shapes = self.shapes(1, True)
        new_rows = self.rows
        self.sent = len(shapes) // 2 if job < steps else 0

        def body(place, ins, outs):
            if extra is not None:
                ins, extras = ins[:-2], ins[-2:]
            count = len(ins) // 2

            def sums(stream, spot):
                if job > 0:
                    found = [Streams(ins[:count], rows), Streams(ins[count:], rows)]
                    a, b = (part.at(stream, spot)[...] for part in found)
                    return [(0, rows[stream], add_low(a, b))]
                first, found = 0, []
                for n, base, count_each, unit in self.items[stream]:
                    for piece in range(count_each):
                        block = base + spot * count_each + piece
                        found.append((first, unit, add_low(ins[n][block], ins[count + n][block])))
                        first += unit
                return found

            for stream in (0, 1):
                if bits is None:
                    ref = Streams(outs, new_rows).at(stream, 0)
                    ((_, row, value),) = sums(stream, 0)
                    ref[:row, :] = value
                    if extra is not None:
                        ref[row:, :] = extras[stream][...]
                    continue
                mine = place >> bits[stream] & 1
                split = len(outs) // 2
                for which, value in ((0, mine), (1, 1 - mine)):
                    target = Streams(outs[which * split : (which + 1) * split], rows)
                    for n, spot in enumerate(spots(left[stream], bits[stream], value)):
                        ref = target.at(stream, n)
                        for first, row, total in sums(stream, spot):
                            ref[first : first + row, :] = total

        return inputs, shapes, body

    def joining(self, step):
        inputs, rows = self.inputs, self.rows
        bits = self.there[step]
        before = self.left
        self.left = left = [sorted(have + [bit], reverse=True) for have, bit in zip(before, bits)]
        self.sent = 0
        if step == 0:
            shapes, write = self.finish(rows)
        else:
            then = self.there[step - 1]
            shapes = self.shapes(1 << len(left[0]), then[0] == then[1])

        def body(place, ins, outs):
            count = len(ins) // 2
            found = [Streams(ins[:count], rows), Streams(ins[count:], rows)]
            for stream in (0, 1):
                bit = bits[stream]
                mine = place >> bit & 1
                if step == 0:
                    low = sum(other < bit for other in left[stream])
                    for spot in range(1 << len(left[stream])):
                        n = (spot >> (low + 1)) << low | spot & ((1 << low) - 1)
                        kept, new = (part.at(stream, n)[...] for part in found)
                        write(outs, stream, spot, jnp.where(mine == (spot >> low & 1), kept, new))
                    continue
                for part, value in zip(found, (mine, 1 - mine)):
                    for n, spot in enumerate(spots(left[stream], bit, value)):
                        Streams(outs, rows).at(stream, spot)[...] = part.at(stream, n)[...]

        return inputs, shapes, body

    def take(self, outs):
        steps = len(self.there)
        if self.job > 2 * steps:
            self.found = outs
            return []
        kept, sent = (outs[: self.sent], outs[self.sent :]) if self.sent else (outs, outs)
        if self.job == steps + 1 and self.alone:
            self.piece = [sent[0].reshape(sent[0].shape[1:])]
            return sent
        step = self.job - 1 if self.job <= steps else 2 * steps - self.job
        got = [swap_bit(x, "tok", bit) for x, bit in zip(sent, self.there[step])]
        self.inputs = list(kept) + got
        return sent


def gather_rest(one):
    spread = lax.all_gather(one.piece[0], "tok", axis=0)
    one.job = 2 * len(one.there) + 1
    rows = one.rows
    shapes, write = one.finish(rows)

    def kernel(x_ref, *outs):
        for spot in range(x_ref.shape[0]):
            write(outs, 0, spot, x_ref[spot, : rows[0]])
            write(outs, 1, spot, x_ref[spot, rows[0] :])

    one.found = pl.pallas_call(
        kernel,
        in_specs=[pl.BlockSpec(memory_space=pltpu.VMEM)],
        out_specs=[pl.BlockSpec(memory_space=pltpu.VMEM)] * len(shapes),
        out_shape=shapes,
        compiler_params=vmem(32),
        name="sum_spread",
    )(spread)


class PlainSum:
    def __init__(self, streams, own, got, extra=None, finish=None, alone=False):
        whole = [
            lax.psum(a.astype(F32) + b.astype(F32), "tok").reshape(-1, a.shape[-1])
            for a, b in zip(own, got)
        ]
        self.found = [
            [whole[n][first : first + rows] for n, first, rows in stream] for stream in streams
        ]


def advance(sums, *others):
    if not isinstance(sums[0], TokSum):
        return []
    place = after(lax.axis_index("tok").astype(jnp.int32).reshape(1), *others)
    works = [one.work() for one in sums]

    def kernel(place_ref, *refs):
        place = place_ref[0]
        ins = refs[: sum(len(work[0]) for work in works)]
        outs = refs[len(ins) :]
        for inputs, shapes, body in works:
            body(place, ins[: len(inputs)], outs[: len(shapes)])
            ins, outs = ins[len(inputs) :], outs[len(shapes) :]

    inputs = [x for work in works for x in work[0]]
    shapes = [x for work in works for x in work[1]]
    size = 2 * sum(math.prod(x.shape) for x in inputs + shapes)
    outs = pl.pallas_call(
        kernel,
        in_specs=[pl.BlockSpec(memory_space=pltpu.SMEM)]
        + [pl.BlockSpec(memory_space=pltpu.VMEM)] * len(inputs),
        out_specs=[pl.BlockSpec(memory_space=pltpu.VMEM)] * len(shapes),
        out_shape=shapes,
        compiler_params=vmem(20),
        cost_estimate=pl.CostEstimate(flops=size, bytes_accessed=size, transcendentals=0),
        name="sum_step",
    )(place, *inputs)
    sent = []
    for one, work in zip(sums, works):
        sent += one.take(outs[: len(work[1])])
        outs = outs[len(work[1]) :]
    return sent


def body(
    tokens,
    cotangent,
    block_source,
    mask_index,
    mask_count,
    w_query,
    w_key,
    w_value,
    w_output,
    mid_gain,
    mid_shift,
    w_inner,
    bias_inner,
    w_outer,
    bias_outer,
    end_gain,
    end_shift,
):
    tok_place = lax.axis_index("tok")
    head_place = lax.axis_index("head")
    half = tok_place % 2
    width = tokens.shape[1]

    def mate(x):
        return swap_bit(x, "head", 0)

    kept, given = halves(tokens, half)
    cot_kept, cot_given = halves(cotangent, half)
    x_got = swap_bit(given, "tok", 0)
    own_w = (w_query, w_key, w_value)
    mate_w = tuple(mate(w) for w in own_w)
    mate_out = mate(w_output)
    mate_in = mate(w_inner)
    own_bias = bias_inner[None, :]
    mate_bias = mate(own_bias)

    sequence = tok_place // 2 * PAIR_SEQS + 2 * head_place + half
    source = lax.dynamic_slice_in_dim(block_source, sequence, 1, 0)[0, :, 0]
    per_half = GROUPS // 2
    flags = jnp.concatenate(
        [
            lax.dynamic_slice_in_dim(source, head_place * per_half, per_half, 0),
            lax.dynamic_slice_in_dim(source, (1 - head_place) * per_half, per_half, 0),
        ]
    )
    swap_lanes = jnp.repeat(flags, HEADS // GROUPS * HDIM)[None, :]
    positions = lax.dynamic_slice_in_dim(mask_index, sequence, 1, 0)[0]
    count = lax.dynamic_slice_in_dim(mask_count, sequence, 1, 0)[0]
    within = jnp.arange(BLOCK)
    places = jnp.concatenate([half * BLOCK + within, (1 - half) * BLOCK + within])
    live = jnp.arange(positions.shape[0]) < count
    hits = jnp.any((positions[None, :] == places[:, None]) & live[None, :], axis=1)
    weight = (1.0 + 3.0 * hits.astype(F32))[:, None]
    params = jnp.stack(
        [mid_gain, mid_shift, bias_outer, end_gain, end_shift] + [jnp.zeros_like(mid_gain)] * 3
    )
    mate_down = mate(after(w_outer, weight, swap_lanes, cot_given, params))

    qkv, lse, ctx_t, x_t, mid_n, mid_rate = attention(
        swap_lanes, (kept, after(x_got, swap_lanes, weight, params, cot_kept)), own_w, mate_w,
        w_output, mate_out,
    )
    cot_got = swap_bit(after(cot_given, x_got), "tok", 0)
    act_t, slope, h1_t, out_kept, out_first, out_rest, d_s2, d_f, end_vec, g_mate = ffn(
        mid_n, params, w_inner, mate_in, own_bias, mate_bias, w_outer, mate_down,
        (cot_kept, cot_got), weight,
    )

    hidden = w_inner.shape[1]
    cut = w_output.shape[0]
    pairs = cut // LANES

    def side_by_side(g):
        return jnp.concatenate([g[:, n : n + COLS] for n in range(0, width, COLS)], axis=0)

    rest = width // 2

    def finish_down(rows):
        def write(outs, stream, spot, value):
            outs[0][stream, spot] = value.astype(F32)

        return [jax.ShapeDtypeStruct((2, lax.axis_size("tok"), rows[0], width), F32)], write

    def finish_inner(rows):
        size = lax.axis_size("tok")

        def write(outs, stream, spot, value):
            value = value.astype(F32)
            one = width // size
            outs[0][spot, :, stream * width : (stream + 1) * width] = value[:one]
            more = rows[stream] - one - 8
            first = spot * more + (third if stream else 0)
            outs[1][first : first + more, :] = value[one : one + more]
            if stream == 0 and spot == 0:
                outs[2][...] = value[one + more :]
            else:
                outs[2][...] += value[one + more :]

        return [
            jax.ShapeDtypeStruct((size, width // size, 2 * width), F32),
            jax.ShapeDtypeStruct((rest, width), F32),
            jax.ShapeDtypeStruct((8, width), F32),
        ], write

    size = lax.axis_size("tok")
    fits = size & (size - 1) == 0 and size >= 4 and rest % (8 * size) == 0
    Sum = TokSum if fits else PlainSum

    got = mate(g_mate)
    mine = product(act_t, 0, hidden, d_f, BLOCK)
    cut = hidden // 2
    down = Sum([[(0, 0, cut)], [(0, cut, cut)]], [mine], [got], finish=finish_down, alone=False)
    sent = advance([down], mine)
    gi_mate, gb_mate, d_h1 = ffn_back(
        1, after(d_f, sent), slope, mate_in, mate_down, h1_t, d_s2
    )
    sent = advance([down], gi_mate)
    first_got = swap_bit(after(out_first, sent), "tok", 0)
    got_in = mate(after(gi_mate, sent))
    gi_own, gb_own, go_own, go_mate, d_s1, d_a, mid_vec = ffn_back(
        0, after(d_f, sent), slope, w_inner, w_outer, h1_t, d_h1, mid_n, mid_rate, ctx_t, params
    )
    got_out = mate(after(go_mate, down.inputs[-2:], first_got) if fits else go_mate)
    third = 8 * size
    inner = Sum(
        [[(0, 0, width), (1, 0, third)], [(0, width, width), (1, third, rest - third)]],
        [gi_own, go_own], [got_in, got_out], finish=finish_inner, alone=False,
    )
    sent = advance([inner, down], gi_own)
    rest_got = swap_bit(after(out_rest, sent), "tok", 0)
    gw_mate, gw_mates, gw_own, dp_early = attention_back(
        (1, pairs, pairs + 1), lambda p: jnp.where(p < pairs, p + pairs, 0), swap_lanes, qkv, ctx_t,
        lse, (w_output, mate_out), after(d_a, sent), x_t,
    )
    sent = advance([inner, down], gw_own, rest_got)
    gw_got, gw_gots = (mate(x) for x in after((gw_mate, gw_mates), sent))

    gw_owns, dp_late = attention_back(
        (pairs - 1,), lambda p: p + 1, swap_lanes, qkv, ctx_t, lse, (w_output,), after(d_a, sent), x_t
    )
    head = (pairs * width // size + 31) // 32 * 16 * size - width

    def finish_last(rows):
        def write(outs, stream, spot, value):
            value = value.astype(F32)
            count = rows[stream]
            pieces = [(0, spot * count + width + head, count)]
            if stream == 0:
                one = width // size
                pieces = [(0, spot * one, one), (one, width + spot * (count - one), count - one)]
            for done, first, length in pieces:
                while length > 0:
                    p, row = divmod(first, width)
                    step = min(length, width - row)
                    for at in range(3):
                        outs[at][row : row + step, p * LANES : (p + 1) * LANES] = value[
                            done : done + step, at * LANES : (at + 1) * LANES
                        ]
                    done, first, length = done + step, first + step, length - step

        return [jax.ShapeDtypeStruct((width, pairs * LANES), F32)] * 3, write

    rows = (pairs - 1) * width
    last = Sum(
        [[(0, 0, width), (1, 0, head)], [(1, head, rows - head)]],
        [x.reshape(-1, 3 * LANES) for x in (gw_own, gw_owns)],
        [x.reshape(-1, 3 * LANES) for x in (gw_got, gw_gots)],
        finish=finish_last,
    )
    for one in (last, inner, down):
        one.keep = pltpu.VMEM
    sent = advance([last, inner, down], gw_owns)
    out = joined(out_kept, jnp.concatenate([first_got, rest_got], axis=0), half)
    own_rows = gb_own.size // width

    def small_vectors(sent):
        end, mid, own, other = after((end_vec, mid_vec, gb_own, gb_mate), sent)
        own, other = own.reshape(-1, width), other.reshape(-1, width)
        small = jnp.concatenate([end[:3], mid[:2], own, other], axis=0)
        theirs = mate(small)
        small = jnp.concatenate(
            [
                small[:5] + theirs[:5],
                small[5 : 5 + own_rows] + theirs[5 + own_rows :],
                jnp.zeros((1, width), F32),
            ],
            axis=0,
        )
        high = small.astype(BF16)
        low = (small - high.astype(F32)).astype(BF16)
        return small, (high, low)

    dx_kept, dx_given = input_gradient(dp_early, after(dp_late, sent), own_w, mate_w, d_s1)
    dx_got, finals = [], []
    if fits:
        while last.job <= 2 * len(last.there):
            for one in (inner, down):
                if one.alone and one.job == len(one.there) + 1:
                    gather_rest(one)
            sums = [one for one in (last, inner, down) if one.job <= 2 * len(one.there)]
            others = [dx_given] if last.job == 1 else []
            if last.job in (2, 3):
                first = (last.job - 2) * (BLOCK // 2)
                part = dx_given[first : first + BLOCK // 2]
                others = [swap_bit(after(part, last.inputs[0]), "tok", 0)]
                dx_got += others
            ending = [one for one in sums if one is not last and one.job == 2 * len(one.there)]
            sent = advance([one for one in sums if one not in ending], *others, *finals)
            if last.job == 2:
                small, inner.extra = small_vectors(sent)
            finals = []
            for one in ending:
                advance([one], sent)
                finals += one.found
        g_down, (g_in, g_out, small), (g_query, g_key, g_value) = (
            down.found[0], inner.found, last.found
        )
    else:
        dx_got = [swap_bit(dx_given, "tok", 0)]
        g_down = jnp.concatenate([down.found[0][0], down.found[1][0]], axis=0)
        g_in = jnp.concatenate([inner.found[0][0], inner.found[1][0]], axis=1)
        g_out = jnp.concatenate([inner.found[0][1], inner.found[1][1]], axis=0)
        whole_w = jnp.concatenate(last.found[0] + last.found[1], axis=0)
        whole_w = whole_w.reshape(pairs, width, 3, LANES)
        g_query, g_key, g_value = (
            jnp.concatenate([whole_w[p, :, at] for p in range(pairs)], axis=1) for at in range(3)
        )
        small = lax.psum(small_vectors(())[0], "tok")
    dx_got = jnp.concatenate(dx_got, axis=0).astype(F32)
    grad_tokens = joined(dx_kept, dx_got, half)
    g_down = g_down.reshape(hidden, width)
    g_in = g_in.reshape(width, hidden)
    g_out = g_out.reshape(rest, width)

    return (
        out,
        grad_tokens,
        g_query,
        g_key,
        g_value,
        g_out,
        small[4],
        small[3],
        g_in,
        small[5 : 5 + own_rows].reshape(-1),
        g_down,
        small[2],
        small[1],
        small[0],
    )


def solution(mesh):
    rows = P(("tok", "head"), None)
    return jax.shard_map(
        body,
        mesh=mesh,
        in_specs=(
            rows,
            rows,
            P(),
            P(),
            P(),
            P(None, "head"),
            P(None, "head"),
            P(None, "head"),
            P("head", None),
            P(),
            P(),
            P(None, "head"),
            P("head"),
            P("head", None),
            P(),
            P(),
            P(),
        ),
        out_specs=(
            rows,
            rows,
            P(None, "head"),
            P(None, "head"),
            P(None, "head"),
            P("head", None),
            P(),
            P(),
            P(None, "head"),
            P("head"),
            P("head", None),
            P(),
            P(),
            P(),
        ),
        check_vma=False,
    )
```
